256 devices in a mesh: ctx: 4 (over x_lo, core), fsdp: 64 (over x_hi, y, z).
Axes of the slice: x: 4 (x_hi: 2, x_lo: 2; x = x_hi * 2 + x_lo), y: 4, z: 8, core: 2. Of those that a mesh axis runs over, the one named last changes fastest.
Arguments:
- tokens: bfloat16 [8192, 6144], P('fsdp'), may hold values from -6 to 6
- expert_ids: int32 [8192, 1], P('fsdp'), may hold values from 0 to 7; in each aligned block of 128 rows (0 to 127, 128 to 255, ...) at most 17 rows name the same one
- router_gate: float32 [8192], P('fsdp'), may hold values from 0.25 to 1
- w_gate: bfloat16 [43008, 6144], P(('fsdp', 'ctx')), may hold values from -0.078125 to 0.078125
- w_up: bfloat16 [43008, 6144], P(('fsdp', 'ctx')), may hold values from -0.078125 to 0.078125
- w_down: bfloat16 [43008, 6144], P(('fsdp', 'ctx')), may hold values from -0.078125 to 0.078125
Outputs:
- expert_out: bfloat16 [8192, 6144], P('fsdp', 'ctx')
The draws below stay inside these ranges and needn't reach their ends.
Inputs may be any that keep to these rules, and one draw needn't show every extreme that they name: `expert_ids`: among the 128 tokens of one fsdp index no expert is chosen more than 17 times, a bound that some block reaches.
All inputs are finite; a program needn't handle non-finite values.
Results may differ from the reference program's by a relative error of at most 0.014.
Values may be sent and summed in bfloat16 or wider, within the bound.
A program may use at most 128 MiB of HBM per device.

```python
import math
import jax
import jax.numpy as jnp
import numpy as np
from jax import lax

D = 6144
FF = 5376
EXPERTS = 8
TOK_DEV = 128
SLOTS = 17
TOKENS = 8192
N_CTX = 4
N_FSDP = 64


def block_scale(rng, shape, pieces, least, top_value):
    gain, own = 1.0, jax.random.fold_in(rng, 6)
    for dim, parts in pieces:
        heights = jnp.exp(jax.random.uniform(jax.random.fold_in(own, dim), (parts,), jnp.float32, least / len(pieces), top_value / len(pieces)))
        gain = gain * jnp.repeat(heights, shape[dim] // parts).reshape([-1 if axis == dim else 1 for axis in range(len(shape))])
    return gain


def deal_out(key, own, number, rows, count, top, most, slope):
    order = jax.random.permutation(key, count)
    packed, usual = portions_of(count, rows * top, most, slope, True), portions_of(count, rows * top, most, slope, False)
    places = jnp.arange(count)

    def named(tallies, turn):
        used = int((tallies > 0).sum())
        fixed = max(1, used // 4)
        moved = fixed + (places - fixed + turn * (used - fixed)) % max(1, count - fixed)
        return jnp.zeros((count,), jnp.int32).at[order[jnp.where(places < fixed, places, moved)]].set(jnp.asarray(tallies, jnp.int32))

    tallies = jnp.where(number % 4 == 0, named(packed, number // 4), named(usual, number - number // 4 - 1))
    mixed = jax.random.permutation(jax.random.fold_in(own, 3), count)
    source_of, receiver = mixed[0:count // 2 * 2:2], mixed[1:count // 2 * 2:2]
    margin = jnp.minimum(tallies[source_of] - 1, most - tallies[receiver]) // 2
    margin = jnp.where((source_of == order[0]) | (receiver == order[0]) | (tallies[receiver] == 0), 0, jnp.maximum(margin, 0))
    moved = jax.random.randint(jax.random.fold_in(own, 4), (count // 2,), 0, 1 << 20) % (margin + 1)
    tallies = tallies.at[source_of].add(-moved).at[receiver].add(moved)
    members = jnp.searchsorted(jnp.cumsum(tallies), jnp.arange(rows * top), side="right").astype(jnp.int32)
    grid = members.reshape(top, rows).T
    grid = grid[jax.random.permutation(jax.random.fold_in(own, 1), rows)]
    turn = jax.random.randint(jax.random.fold_in(own, 2), (rows, 1), 0, top)
    return jnp.take_along_axis(grid, (jnp.arange(top)[None, :] + turn) % top, axis=1)


def portions_of(count, total, bound, lean, full):
    loads = [(1 << 20) // math.isqrt(grade ** lean) + 1 for grade in range(1, count + 1)]
    largest = bound if full else min(bound, max(-(-total // count), total * loads[0] // sum(loads)))
    least = 1 if total - largest >= count - 1 else 0
    given, surplus = [largest] + [least] * (count - 1), total - largest - least * (count - 1)
    while surplus > 0:
        movable = [i for i in range(1, count) if given[i] < largest] or [i for i in range(1, count) if given[i] < bound]
        whole, budget = sum([loads[i] for i in movable]), surplus
        for i in movable:
            more = min(bound - given[i], max(1, budget * loads[i] // whole), surplus)
            given[i] = given[i] + more
            surplus = surplus - more
    return np.array(given)


def noise(rng, shape, spread, most, split=(), held_as=jnp.bfloat16):
    loudness = block_scale(rng, shape, split, -0.22, 0.18) if split else 1.0
    result = jax.random.normal(rng, shape, jnp.float32) * spread * loudness
    return jnp.minimum(jnp.maximum(result, -most), most).astype(held_as)


def setup_inputs(seed: int = 0) -> dict:
    streams_of = jax.random.split(jax.random.key(seed), 7)
    tokens = noise(streams_of[0], (TOKENS, D), 1.0, 6.0, ((0, 64),))
    expert_ids_keys = jax.random.split(jax.random.fold_in(streams_of[1], 1), TOKENS // TOK_DEV)
    expert_ids_turns = jax.random.permutation(jax.random.fold_in(streams_of[1], 3), TOKENS // TOK_DEV)
    expert_ids = jax.vmap(lambda own, number: deal_out(jax.random.fold_in(streams_of[1], 2), own, number, TOK_DEV, EXPERTS, 1, SLOTS, 2))(expert_ids_keys, expert_ids_turns).reshape((TOKENS, 1))
    router_gate = jnp.clip(0.25 + 0.75 * jax.random.uniform(streams_of[2], (TOKENS,), jnp.float32) ** block_scale(streams_of[2], (TOKENS,), ((0, 64),), -0.2, 0.2), 0.25, 1.0)
    w_gate = noise(streams_of[3], (EXPERTS * FF, D), D ** -0.5, 0.078125, ((0, 256),))
    w_up = noise(streams_of[4], (EXPERTS * FF, D), D ** -0.5, 0.078125, ((0, 256),))
    w_down = noise(streams_of[5], (EXPERTS * FF, D), FF ** -0.5, 0.078125, ((0, 256),))
    return dict(tokens=tokens, expert_ids=expert_ids, router_gate=router_gate, w_gate=w_gate, w_up=w_up, w_down=w_down)


def project_rows(rows, weight_rows):
    return lax.dot_general(rows, weight_rows, (((1,), (1,)), ((), ())), preferred_element_type=jnp.float32)


def reference(tokens, expert_ids, router_gate, w_gate, w_up, w_down):
    slice_count = N_CTX * N_FSDP // EXPERTS
    slice_width = FF // slice_count
    most_rows = N_FSDP * SLOTS
    expert_of = expert_ids[:, 0].astype(jnp.int32)
    sorted_rows = jnp.argsort(expert_of, stable=True).astype(jnp.int32)
    counts = jnp.sum((expert_of[:, None] == jnp.arange(EXPERTS, dtype=jnp.int32)[None, :]).astype(jnp.int32), axis=0)
    starts = (jnp.cumsum(counts) - counts).astype(jnp.int32)

    def one_expert(expert, output):
        expert = jnp.asarray(expert).astype(jnp.int32)
        position = starts[expert] + jnp.arange(most_rows, dtype=jnp.int32)
        is_live = position < starts[expert] + counts[expert]
        row_index = sorted_rows[jnp.minimum(position, TOKENS - 1)].astype(jnp.int32)
        picked = jnp.where(is_live[:, None], tokens[row_index], jnp.zeros((), tokens.dtype))
        column = (expert * FF).astype(jnp.int32)
        gate_rows = lax.dynamic_slice_in_dim(w_gate, column, FF, 0)
        up_rows = lax.dynamic_slice_in_dim(w_up, column, FF, 0)
        down_rows = lax.dynamic_slice_in_dim(w_down, column, FF, 0)
        gate_part = project_rows(picked, gate_rows)
        up_part = project_rows(picked, up_rows)
        hidden = (jax.nn.silu(gate_part) * up_part).astype(jnp.bfloat16)
        total = jnp.zeros((most_rows, D), jnp.float32)
        for piece in range(slice_count):
            lower = piece * slice_width
            term = jnp.dot(hidden[:, lower:lower + slice_width], down_rows[lower:lower + slice_width], preferred_element_type=jnp.float32).astype(jnp.bfloat16)
            total = total + lax.optimization_barrier(term).astype(jnp.float32)
        total = jnp.where(is_live[:, None], total, jnp.zeros((), total.dtype))
        return output.at[row_index].add(total)

    summed = lax.fori_loop(0, EXPERTS, one_expert, jnp.zeros((TOKENS, D), jnp.float32))
    return (router_gate[:, None] * summed).astype(jnp.bfloat16)
```

```python
import functools

import jax
import jax.numpy as jnp
from jax import lax
from jax.experimental import pallas as pl
from jax.experimental.pallas import tpu as pltpu
from jax.sharding import PartitionSpec as P

MESH = pl.DeviceIdType.MESH
EXPERTS = 8
MAIN = 16
PAIR = 32
ROWS = EXPERTS * MAIN + MAIN
RING = 8
HALF = ((0, 80), (80, 64))
BF16, F32 = jnp.bfloat16, jnp.float32


def nt_dot(a, b):
    return lax.dot_general(a, b, (((1,), (1,)), ((), ())), preferred_element_type=F32)


def kernel(
    tok_ref, ids_ref, gate_ref, wg_ref, wu_ref, wd_ref,
    out_ref,
    sel, send, staged, x, wgu, wdn, gu_own, gu_out, gu_in, hid, y, yx, back, final, fx, parcel, result,
    w_sem, ws_sem, wr_sem, as_sem, ar_sem, zs_sem, zr_sem, xs_sem, xr_sem,
    gs_sem, gr_sem, hs_sem, hr_sem, ys_sem, yr_sem, bs_sem, br_sem, fs_sem, fr_sem, ds_sem, dr_sem,
):
    c, f = lax.axis_index("ctx"), lax.axis_index("fsdp")
    xl, co = c // 2, c % 2
    col, z = f // RING, f % RING
    units = wg_ref.shape[0]
    width = x.shape[3]

    def on_z(d):
        return (c, col * RING + (z + d + RING) % RING)

    def in_column(e):
        return (c, e * RING + z)

    sibling = (c + 1 - 2 * co, f)
    across = ((c + 2) % 4, f)

    def remote(src, dst, ssem, rsem, dev):
        return pltpu.make_async_remote_copy(
            src_ref=src, dst_ref=dst, send_sem=ssem, recv_sem=rsem, device_id=dev, device_id_type=MESH
        )

    barrier = pltpu.get_barrier_semaphore()
    partners = [on_z(1), on_z(-1), sibling, across] + [in_column((col + i) % EXPERTS) for i in range(1, EXPERTS)]
    for dev in partners:
        pl.semaphore_signal(barrier, inc=1, device_id=dev, device_id_type=MESH)

    def column_of(core, blk):
        return pl.multiple_of(((blk % 2) * 2 + core) * 2 * width + (blk // 2) * width, 128)

    def weight_slot(m, unit_core, blk):
        return wdn.at[unit_core, blk] if m == 2 else wgu.at[m, unit_core, blk]

    w_refs = (wg_ref, wu_ref, wd_ref)
    own_w = [
        pltpu.make_async_copy(
            w_refs[m].at[:, pl.ds(column_of(co, blk), width)], weight_slot(m, co, blk), w_sem.at[m, blk]
        )
        for m in range(3) for blk in range(4)
    ]
    other_w = [
        remote(
            w_refs[m].at[:, pl.ds(column_of(1 - co, blk), width)], weight_slot(m, co, blk),
            ws_sem.at[m, blk], wr_sem.at[m, blk], sibling,
        )
        for m in range(3) for blk in range(4)
    ]
    for cp in own_w:
        cp.start()

    n_tok = tok_ref.shape[0]
    rows_i = lax.broadcasted_iota(jnp.int32, (n_tok, n_tok), 0)
    cols_i = lax.broadcasted_iota(jnp.int32, (n_tok, n_tok), 1)
    ids_row = ids_ref[...]
    ids_col = jnp.sum(jnp.where(rows_i == cols_i, ids_row, 0), axis=1, keepdims=True)
    gate_col = jnp.sum(jnp.where(rows_i == cols_i, gate_ref[...], 0.0), axis=1, keepdims=True)
    same = (ids_row == ids_col) & (cols_i < rows_i)
    rank = jnp.sum(same.astype(jnp.int32), axis=1, keepdims=True)
    place = ids_col * PAIR + jnp.where(rank < MAIN, rank, MAIN + col)
    slots = lax.broadcasted_iota(jnp.int32, (n_tok, EXPERTS * PAIR), 1)
    select = (slots == place).astype(F32)
    sel[...] = select.astype(BF16)
    pack = jnp.transpose(select).astype(BF16)
    share_cols = (column_of(co, 0), column_of(co, 1), column_of(co, 2 + xl))
    for p in range(3):
        packed = jnp.dot(pack, tok_ref[:, pl.ds(share_cols[p], width)], preferred_element_type=F32)
        send[:, :, p * width:(p + 1) * width] = packed.astype(BF16).reshape(EXPERTS, PAIR, width)

    pl.semaphore_wait(barrier, len(partners))

    def phase_a(i):
        return remote(
            send.at[(col + i) % EXPERTS], staged.at[col], as_sem.at[i - 1], ar_sem.at[i - 1],
            in_column((col + i) % EXPERTS),
        )

    to_experts = [phase_a(i) for i in range(1, EXPERTS)]
    for cp in to_experts:
        cp.start()
    for cp in other_w:
        cp.start()
    staged[col] = send[col]
    for cp in to_experts:
        cp.wait()

    def piece_of(p):
        return 2 + xl if p == 2 else p

    for p in range(3):
        cs = slice(p * width, (p + 1) * width)
        extra = staged[0, MAIN:, cs]
        for s in range(EXPERTS):
            x[z, piece_of(p), s * MAIN:(s + 1) * MAIN, :] = staged[s, :MAIN, cs]
            if s:
                extra = extra + staged[s, MAIN:, cs]
        x[z, piece_of(p), EXPERTS * MAIN:, :] = extra

    def plane(d):
        return (z + d + RING) % RING

    def z_send(side, k, p):
        d = 1 - 2 * side
        blk = x.at[plane(-d * (k - 1)), piece_of(p)]
        if k == 4:
            blk = blk.at[pl.ds(*HALF[side])]
        return remote(blk, blk, zs_sem.at[side, k - 1, p], zr_sem.at[side, k - 1, p], on_z(d))

    def x_send(i):
        side, k = (i + 1) % 2, (i + 1) // 2
        if i == 0:
            blk = x.at[z, 2 + xl]
        elif i < 7:
            blk = x.at[plane(-(1 - 2 * side) * k), 2 + xl]
        else:
            side = i - 7
            blk = x.at[plane(4), 2 + xl].at[pl.ds(*HALF[side])]
        return remote(blk, blk, xs_sem.at[i], xr_sem.at[i], across)

    order = [0, -1, 1, -2, 2, -3, 3, 4]

    def gu_send(i):
        return remote(gu_out.at[i], gu_in.at[i], gs_sem.at[i], gr_sem.at[i], sibling)

    def hid_send(i):
        return remote(hid.at[i, co], hid.at[i, co], hs_sem.at[i], hr_sem.at[i], sibling)

    def gate_up(i):
        pi = plane(order[i])
        x_send(i).wait_recv()
        if i == 7:
            x_send(8).wait_recv()
        for m in range(2):
            gu_own[i, m] = jnp.zeros(gu_own.shape[2:], F32)
            gu_out[i, m] = jnp.zeros(gu_own.shape[2:], F32)

        def body(blk, carry):
            xb = x[pi, blk]
            for m in range(2):
                gu_own[i, m] += nt_dot(xb, wgu[m, co, blk])
                gu_out[i, m] += nt_dot(xb, wgu[m, 1 - co, blk])
            return carry

        lax.fori_loop(0, 4, body, 0)
        gu_send(i).start()

    def hidden(i):
        gu_send(i).wait_recv()
        g = gu_own[i, 0] + gu_in[i, 0]
        u = gu_own[i, 1] + gu_in[i, 1]
        hid[i, co] = (g / (1.0 + jnp.exp(-g)) * u).astype(BF16)
        hid_send(i).start()

    def y_send(i):
        return remote(y.at[plane(order[i]), 2 + 1 - xl], yx.at[i], ys_sem.at[i], yr_sem.at[i], across)

    def down(i):
        pi = plane(order[i])
        hid_send(i).wait_recv()

        def body(blk, carry):
            part = jnp.dot(hid[i, 0], wdn[0, blk], preferred_element_type=F32)
            part += jnp.dot(hid[i, 1], wdn[1, blk], preferred_element_type=F32)
            y[pi, blk] = part.astype(BF16)
            return carry

        lax.fori_loop(0, 4, body, 0)
        y_send(i).start()

    def add_across(i):
        y_send(i).wait()
        pi = plane(order[i])
        y[pi, 2 + xl] = (y[pi, 2 + xl].astype(F32) + yx[i].astype(F32)).astype(BF16)

    def compute(i):
        if i < 8:
            gate_up(i)
        if 0 < i < 9:
            hidden(i - 1)
        if 1 < i:
            down(i - 2)

    pieces = (2, 0, 1)
    x_send(0).start()
    for p in pieces:
        for side in range(2):
            z_send(side, 1, p).start()
    for cp in own_w:
        cp.wait()
    for cp in other_w:
        cp.wait()
    compute(0)
    for k in range(2, 5):
        for p in pieces:
            for side in range(2):
                z_send(side, k - 1, p).wait_recv()
                z_send(side, k, p).start()
                if p == 2:
                    x_send(2 * (k - 1) - 1 + side).start()
        compute(2 * (k - 1) - 1)
        compute(2 * (k - 1))
    for p in pieces:
        for side in range(2):
            z_send(side, 4, p).wait_recv()
            if p == 2:
                x_send(7 + side).start()
    for i in range(7, 10):
        compute(i)

    def back_send(side, j, p):
        d = 1 - 2 * side
        src = y.at[plane(d * (5 - j)), piece_of(p)]
        dst = back.at[side, j - 1, p]
        if j == 1:
            src, dst = src.at[pl.ds(*HALF[side])], dst.at[pl.ds(*HALF[side])]
        return remote(src, dst, bs_sem.at[side, j - 1, p], br_sem.at[side, j - 1, p], on_z(d))

    def index_of(d):
        return order.index(d)

    for j in range(1, 5):
        for p in (0, 1, 2):
            for side in range(2):
                d = 1 - 2 * side
                if p == 2 and (j > 1 or side == 0):
                    add_across(7 if j == 1 else index_of(d * (5 - j)))
                if j > 1:
                    back_send(side, j - 1, p).wait_recv()
                    pi = plane(d * (5 - j))
                    rows = pl.ds(*HALF[side]) if j == 2 else slice(None)
                    y[pi, piece_of(p), rows, :] = (
                        y[pi, piece_of(p), rows, :].astype(F32) + back[side, j - 2, p, rows, :].astype(F32)
                    ).astype(BF16)
                back_send(side, j, p).start()
    add_across(0)
    f_send = remote(final.at[1 - xl], fx, fs_sem, fr_sem, across)
    for p in range(3):
        for side in range(2):
            back_send(side, 4, p).wait_recv()
        total = y[z, piece_of(p)].astype(F32) + back[0, 3, p].astype(F32) + back[1, 3, p].astype(F32)
        final[p] = total.astype(BF16)
        if p == 1:
            f_send.start()
    f_send.wait()
    mine = (final[xl].astype(F32) + fx[...].astype(F32)).astype(BF16)
    rest = final[2]
    for s in range(EXPERTS):
        parcel[s, :MAIN, :width] = mine[s * MAIN:(s + 1) * MAIN]
        parcel[s, :MAIN, width:] = rest[s * MAIN:(s + 1) * MAIN]
        parcel[s, MAIN:, :width] = mine[EXPERTS * MAIN:]
        parcel[s, MAIN:, width:] = rest[EXPERTS * MAIN:]

    def deliver(i):
        return remote(
            parcel.at[(col + i) % EXPERTS], result.at[col], ds_sem.at[i - 1], dr_sem.at[i - 1],
            in_column((col + i) % EXPERTS),
        )

    to_owners = [deliver(i) for i in range(1, EXPERTS)]
    for cp in to_owners:
        cp.start()
    result[col] = parcel[col]

    x_sends = [x_send(i) for i in range(9)]
    for cp in x_sends:
        cp.wait_send()
    for i in range(8):
        gu_send(i).wait_send()
        hid_send(i).wait_send()
    for side in range(2):
        for k in range(1, 5):
            for p in range(3):
                z_send(side, k, p).wait_send()
                back_send(side, k, p).wait_send()
    for cp in to_owners:
        cp.wait()
    rows = jnp.dot(sel[...], result[...].reshape(EXPERTS * PAIR, 2 * width), preferred_element_type=F32)
    out_ref[...] = (gate_col * rows).astype(BF16)


def local(tokens, expert_ids, router_gate, w_gate, w_up, w_down):
    n_tok, dmodel = tokens.shape
    units = w_gate.shape[0]
    width = dmodel // 8
    vmem, dma = pltpu.VMEM, pltpu.SemaphoreType.DMA
    return pl.pallas_call(
        kernel,
        out_shape=jax.ShapeDtypeStruct((n_tok, 2 * width), BF16),
        in_specs=[pl.BlockSpec(memory_space=pltpu.VMEM)] * 3 + [pl.BlockSpec(memory_space=pl.ANY)] * 3,
        out_specs=pl.BlockSpec(memory_space=pltpu.VMEM),
        scratch_shapes=[
            vmem((n_tok, EXPERTS * PAIR), BF16),
            vmem((EXPERTS, PAIR, 3 * width), BF16),
            vmem((EXPERTS, PAIR, 3 * width), BF16),
            vmem((RING, 4, ROWS, width), BF16),
            vmem((2, 2, 4, units, width), BF16),
            vmem((2, 4, units, width), BF16),
            vmem((RING, 2, ROWS, units), F32),
            vmem((RING, 2, ROWS, units), F32),
            vmem((RING, 2, ROWS, units), F32),
            vmem((RING, 2, ROWS, units), BF16),
            vmem((RING, 4, ROWS, width), BF16),
            vmem((RING, ROWS, width), BF16),
            vmem((2, 4, 3, ROWS, width), BF16),
            vmem((3, ROWS, width), BF16),
            vmem((ROWS, width), BF16),
            vmem((EXPERTS, PAIR, 2 * width), BF16),
            vmem((EXPERTS, PAIR, 2 * width), BF16),
            dma((3, 4)), dma((3, 4)), dma((3, 4)),
            dma((7,)), dma((7,)),
            dma((2, 4, 3)), dma((2, 4, 3)),
            dma((9,)), dma((9,)),
            dma((8,)), dma((8,)),
            dma((8,)), dma((8,)),
            dma((8,)), dma((8,)),
            dma((2, 4, 3)), dma((2, 4, 3)),
            dma, dma,
            dma((7,)), dma((7,)),
        ],
        compiler_params=pltpu.CompilerParams(
            collective_id=0, has_side_effects=True, vmem_limit_bytes=60 * 2**20
        ),
        cost_estimate=pl.CostEstimate(flops=7 * 10**9, bytes_accessed=10**7, transcendentals=200000),
        name="routed_experts",
    )(tokens, expert_ids.reshape(1, n_tok), router_gate.reshape(1, n_tok), w_gate, w_up, w_down)


def solution(mesh):
    placed = (
        P("fsdp", None),
        P("fsdp", None),
        P("fsdp"),
        P(("fsdp", "ctx"), None),
        P(("fsdp", "ctx"), None),
        P(("fsdp", "ctx"), None),
    )
    return jax.shard_map(
        local, mesh=mesh, in_specs=placed, out_specs=P("fsdp", "ctx"), check_vma=False
    )
```

```python
import functools

import jax
import jax.numpy as jnp
from jax import lax
from jax.experimental import pallas as pl
from jax.experimental.pallas import tpu as pltpu
from jax.sharding import PartitionSpec as P

MESH = pl.DeviceIdType.MESH
EXPERTS = 8
MAIN = 16
RING = 8
BF16, F32 = jnp.bfloat16, jnp.float32
SOURCES = ((0, 0), (0, 2), (1, 0), (1, 2), (0, 1), (0, 3), (1, 1), (1, 3))
ROWS = (4 * MAIN, 5 * MAIN)
HALF = (((0, 32), (32, 32)), ((0, 48), (48, 32)))
ORDER = (0, -1, 1, -2, 2, -3, 3, 4)
GROUPS = ((0, 3), (3, 5), (5, 7), (7, 8))


def nt_dot(a, b):
    return lax.dot_general(a, b, (((1,), (1,)), ((), ())), preferred_element_type=F32)


def dot(a, b):
    return jnp.dot(a, b, preferred_element_type=F32)


def transposition(shape):
    r = lax.broadcasted_iota(jnp.int32, shape, 0)
    q = lax.broadcasted_iota(jnp.int32, shape, 1)
    return (((r >> 4) == (q & 15)) & ((r & 15) == (q >> 4))).astype(F32).astype(BF16)


def fold(rows):
    tiles = []
    for lo in range(0, rows.shape[1], 2048):
        part = rows[:, lo:lo + 2048]
        n = part.shape[1] // 128
        stack = jnp.concatenate([part[:, j * 128:(j + 1) * 128] for j in range(n)], axis=0)
        tiles.append(dot(transposition((128, n * 16)), stack).astype(BF16))
    return tiles


def unfold(tiles, n_blocks):
    blocks = []
    for t, tile in enumerate(tiles):
        n = min(16, n_blocks - 16 * t)
        stack = dot(transposition((n * 16, 128)), tile).astype(BF16)
        blocks += [stack[j * 16:(j + 1) * 16] for j in range(n)]
    return jnp.concatenate(blocks, axis=1)


def kernel(
    tok_ref, ids_ref, gate_ref, wg_ref, wu_ref, wd_ref,
    out_ref,
    sel, send, staged, wgu, wdn, parcel, parcel_x, result, result_x, *rest,
):
    per_wave, sems = rest[:20], rest[20:]
    x, gu_own, gu_out, gu_in, hid, y, yx, back, final, fx = [per_wave[2 * i:2 * i + 2] for i in range(10)]
    (
        w_sem, ws_sem, wr_sem, as_sem, ar_sem, zs_sem, zr_sem, xs_sem, xr_sem,
        gs_sem, gr_sem, hs_sem, hr_sem, ys_sem, yr_sem, bs_sem, br_sem, fs_sem, fr_sem,
        ds_sem, dr_sem, es_sem, er_sem,
    ) = sems
    c, f = lax.axis_index("ctx"), lax.axis_index("fsdp")
    xl, co = c // 2, c % 2
    col, z = f // RING, f % RING
    width = x[0].shape[3]
    share = 3 * width

    def on_z(d):
        return (c, col * RING + (z + d + RING) % RING)

    def column(r, sign):
        dx, dy = SOURCES[r]
        return (col // 4 + dx) % 2 * 4 + (col % 4 + sign * dy + 4) % 4

    def in_column(e):
        return (c, e * RING + z)

    sibling = (c + 1 - 2 * co, f)
    across = ((c + 2) % 4, f)

    def remote(src, dst, ssem, rsem, dev):
        return pltpu.make_async_remote_copy(
            src_ref=src, dst_ref=dst, send_sem=ssem, recv_sem=rsem, device_id=dev, device_id_type=MESH
        )

    barrier = pltpu.get_barrier_semaphore()
    partners = [on_z(1), on_z(-1), sibling, across] + [in_column((col + i) % EXPERTS) for i in range(1, EXPERTS)]
    for dev in partners:
        pl.semaphore_signal(barrier, inc=1, device_id=dev, device_id_type=MESH)

    def column_of(core, blk):
        return pl.multiple_of(((blk % 2) * 2 + core) * 2 * width + (blk // 2) * width, 128)

    def weight_slot(m, unit_core, blk):
        return wdn.at[unit_core, blk] if m == 2 else wgu.at[m, unit_core, blk]

    w_refs = (wg_ref, wu_ref, wd_ref)
    own_w = [
        pltpu.make_async_copy(
            w_refs[m].at[:, pl.ds(column_of(co, blk), width)], weight_slot(m, co, blk), w_sem.at[m, blk]
        )
        for m in range(3) for blk in range(4)
    ]
    other_w = [
        remote(
            w_refs[m].at[:, pl.ds(column_of(1 - co, blk), width)], weight_slot(m, co, blk),
            ws_sem.at[m, blk], wr_sem.at[m, blk], sibling,
        )
        for m in range(3) for blk in range(4)
    ]
    for cp in own_w:
        cp.start()

    n_tok = tok_ref.shape[0]
    rows_i = lax.broadcasted_iota(jnp.int32, (n_tok, n_tok), 0)
    cols_i = lax.broadcasted_iota(jnp.int32, (n_tok, n_tok), 1)
    ids_row = ids_ref[...]
    ids_col = jnp.sum(jnp.where(rows_i == cols_i, ids_row, 0), axis=1, keepdims=True)
    gate_col = jnp.sum(jnp.where(rows_i == cols_i, gate_ref[...], 0.0), axis=1, keepdims=True)
    same = (ids_row == ids_col) & (cols_i < rows_i)
    rank = jnp.sum(same.astype(jnp.int32), axis=1, keepdims=True)
    main = ((cols_i == ids_col * MAIN + rank) & (rank < MAIN)).astype(F32)
    last = ((cols_i == ids_col) & (rank == MAIN)).astype(F32)
    sel[0] = main.astype(BF16)
    sel[1] = last.astype(BF16)
    pack = jnp.transpose(main).astype(BF16)
    pack_last = jnp.transpose(last)[:16].astype(BF16)
    share_cols = (column_of(co, 0), column_of(co, 1), column_of(co, 2 + xl))
    lasts = []
    for p in range(3):
        part = tok_ref[:, pl.ds(share_cols[p], width)]
        send[:, :, p * width:(p + 1) * width] = dot(pack, part).astype(BF16).reshape(EXPERTS, MAIN, width)
        lasts.append(dot(pack_last, part).astype(BF16))
    for t, tile in enumerate(fold(jnp.concatenate(lasts, axis=1))):
        send[:, :, share + t * 128:share + (t + 1) * 128] = tile.reshape(EXPERTS, MAIN, 128)

    pl.semaphore_wait(barrier, len(partners))

    def phase_a(r):
        e = column(r, -1)
        return remote(send.at[e], staged.at[r], as_sem.at[r], ar_sem.at[r], in_column(e))

    def piece_of(p):
        return 2 + xl if p == 2 else p

    def land(w):
        for q in range(4):
            r = 4 * w + q
            if r == 0:
                staged[0] = send[col]
            else:
                phase_a(r).wait_recv()
            for p in range(3):
                x[w][z, piece_of(p), q * MAIN:(q + 1) * MAIN, :] = staged[r, :, p * width:(p + 1) * width]
        if w == 1:
            tiles = [
                staged[:, :, lo:lo + 128].reshape(EXPERTS * MAIN, 128)
                for lo in range(share, staged.shape[2], 128)
            ]
            extra = unfold(tiles, share // 128)
            for p in range(3):
                x[1][z, piece_of(p), 4 * MAIN:, :] = extra[:, p * width:(p + 1) * width]

    def plane(d):
        return (z + d + RING) % RING

    def z_send(w, side, k, p):
        d = 1 - 2 * side
        blk = x[w].at[plane(-d * (k - 1)), piece_of(p)]
        if k == 4:
            blk = blk.at[pl.ds(*HALF[w][side])]
        return remote(blk, blk, zs_sem.at[w, side, k - 1, p], zr_sem.at[w, side, k - 1, p], on_z(d))

    def x_send(w, i):
        if i < 7:
            blk = x[w].at[plane(ORDER[i]), 2 + xl]
        else:
            blk = x[w].at[plane(4), 2 + xl].at[pl.ds(*HALF[w][i - 7])]
        return remote(blk, blk, xs_sem.at[w, i], xr_sem.at[w, i], across)

    def z_step(w, k):
        for p in (2, 0, 1):
            for side in range(2):
                if k > 1:
                    z_send(w, side, k - 1, p).wait_recv()
                if k < 5:
                    z_send(w, side, k, p).start()
                if p == 2 and k > 1:
                    x_send(w, 2 * (k - 1) - 1 + side).start()
                elif p == 2 and side == 0:
                    x_send(w, 0).start()

    def group_rows(w, g):
        return GROUPS[g][0] * ROWS[w], (GROUPS[g][1] - GROUPS[g][0]) * ROWS[w]

    def gu_send(w, g):
        rows = pl.ds(*group_rows(w, g))
        return remote(gu_out[w].at[:, rows], gu_in[w].at[:, rows], gs_sem.at[w, g], gr_sem.at[w, g], sibling)

    def hid_send(w, g):
        mine = hid[w].at[co, pl.ds(*group_rows(w, g))]
        return remote(mine, mine, hs_sem.at[w, g], hr_sem.at[w, g], sibling)

    def gate_up(w, g):
        lo, n = group_rows(w, g)
        ids = range(*GROUPS[g])
        for i in ids:
            x_send(w, i).wait_recv()
            if i == 7:
                x_send(w, 8).wait_recv()
        for m in range(2):
            gu_own[w][m, lo:lo + n] = jnp.zeros((n, gu_own[w].shape[2]), F32)
            gu_out[w][m, lo:lo + n] = jnp.zeros((n, gu_own[w].shape[2]), F32)

        def body(blk, carry):
            xb = jnp.concatenate([x[w][plane(ORDER[i]), blk] for i in ids], axis=0)
            for m in range(2):
                gu_own[w][m, lo:lo + n] += nt_dot(xb, wgu[m, co, blk])
                gu_out[w][m, lo:lo + n] += nt_dot(xb, wgu[m, 1 - co, blk])
            return carry

        lax.fori_loop(0, 4, body, 0)
        gu_send(w, g).start()

    def hidden(w, g):
        lo, n = group_rows(w, g)
        gu_send(w, g).wait_recv()
        gate = gu_own[w][0, lo:lo + n] + gu_in[w][0, lo:lo + n]
        up = gu_own[w][1, lo:lo + n] + gu_in[w][1, lo:lo + n]
        hid[w][co, lo:lo + n] = (gate / (1.0 + jnp.exp(-gate)) * up).astype(BF16)
        hid_send(w, g).start()

    def down(w, g):
        lo, n = group_rows(w, g)
        hid_send(w, g).wait_recv()

        def body(blk, carry):
            part = dot(hid[w][0, lo:lo + n], wdn[0, blk]) + dot(hid[w][1, lo:lo + n], wdn[1, blk])
            part = part.astype(BF16)
            for at, i in enumerate(range(*GROUPS[g])):
                y[w][plane(ORDER[i]), blk] = part[at * ROWS[w]:(at + 1) * ROWS[w]]
            return carry

        lax.fori_loop(0, 4, body, 0)

    def y_send(w, i):
        return remote(
            y[w].at[plane(ORDER[i]), 2 + 1 - xl], yx[w].at[i], ys_sem.at[w, i], yr_sem.at[w, i], across
        )

    def add_across(w, i):
        y_send(w, i).wait()
        pi = plane(ORDER[i])
        y[w][pi, 2 + xl] = (y[w][pi, 2 + xl].astype(F32) + yx[w][i].astype(F32)).astype(BF16)

    def back_send(w, side, j, p):
        d = 1 - 2 * side
        src = y[w].at[plane(d * (5 - j)), piece_of(p)]
        dst = back[w].at[side, j - 1, p]
        if j == 1:
            src, dst = src.at[pl.ds(*HALF[w][side])], dst.at[pl.ds(*HALF[w][side])]
        return remote(src, dst, bs_sem.at[w, side, j - 1, p], br_sem.at[w, side, j - 1, p], on_z(d))

    def ret(w, j, *ps):
        for p in ps:
            for side in range(2):
                d = 1 - 2 * side
                far = plane(d * (5 - j))
                if p == 2 and (j > 1 or side == 0):
                    add_across(w, ORDER.index(d * (5 - j)))
                if j > 1:
                    back_send(w, side, j - 1, p).wait_recv()
                    lo, n = HALF[w][side] if j == 2 else (0, ROWS[w])
                    y[w][far, piece_of(p), lo:lo + n, :] = (
                        y[w][far, piece_of(p), lo:lo + n, :].astype(F32)
                        + back[w][side, j - 2, p, lo:lo + n, :].astype(F32)
                    ).astype(BF16)
                back_send(w, side, j, p).start()

    def f_send(w):
        return remote(final[w].at[1 - xl], fx[w], fs_sem.at[w], fr_sem.at[w], across)

    def finish(w, *ps):
        for p in ps:
            if p == 2:
                add_across(w, 0)
            for side in range(2):
                back_send(w, side, 4, p).wait_recv()
            total = y[w][z, piece_of(p)].astype(F32) + back[w][0, 3, p].astype(F32) + back[w][1, 3, p].astype(F32)
            final[w][p] = total.astype(BF16)
            if p == 1:
                f_send(w).start()

    def deliver(r):
        s = column(r, 1)
        return remote(parcel.at[r], result.at[col], ds_sem.at[r], dr_sem.at[r], in_column(s))

    def deliver_last(r):
        s = column(r, 1)
        return remote(parcel_x.at[r], result_x.at[col], es_sem.at[r], er_sem.at[r], in_column(s))

    def hand_out(w):
        f_send(w).wait()
        mine = (final[w][xl].astype(F32) + fx[w][...].astype(F32)).astype(BF16)
        rest_of = final[w][2]
        for q in range(4):
            r = 4 * w + q
            parcel[r, :, :width] = mine[q * MAIN:(q + 1) * MAIN]
            parcel[r, :, width:] = rest_of[q * MAIN:(q + 1) * MAIN]
            if r:
                deliver(r).start()
            else:
                result[col] = parcel[0]
        if w == 1:
            tile = fold(jnp.concatenate([mine[4 * MAIN:], rest_of[4 * MAIN:]], axis=1))[0]
            parcel_x[...] = tile.reshape(EXPERTS, MAIN, 128)
            result_x[col] = parcel_x[0]
            for r in range(1, EXPERTS):
                deliver_last(r).start()

    for r in range(1, EXPERTS):
        phase_a(r).start()
    for cp in other_w:
        cp.start()

    def cross(w, *idx):
        for i in idx:
            y_send(w, i).start()

    land(0)
    z_step(0, 1)
    land(1)
    for cp in own_w + other_w:
        cp.wait()
    z_step(0, 2)
    gate_up(0, 0)
    z_step(0, 3)
    gate_up(0, 1)
    hidden(0, 0)
    z_step(0, 4)
    z_step(1, 1)
    gate_up(0, 2)
    hidden(0, 1)
    down(0, 0)
    z_step(0, 5)
    z_step(1, 2)
    hidden(0, 2)
    gate_up(0, 3)
    down(0, 1)
    down(0, 2)
    cross(0, 5, 6)
    hidden(0, 3)
    down(0, 3)
    cross(0, 7)
    ret(0, 1, 0, 1)
    z_step(1, 3)
    cross(0, 3, 4)
    gate_up(1, 0)
    ret(0, 2, 0, 1)
    ret(0, 1, 2)
    z_step(1, 4)
    cross(0, 1, 2)
    gate_up(1, 1)
    hidden(1, 0)
    ret(0, 3, 0, 1)
    ret(0, 2, 2)
    z_step(1, 5)
    cross(0, 0)
    gate_up(1, 2)
    hidden(1, 1)
    down(1, 0)
    ret(0, 4, 0, 1)
    ret(0, 3, 2)
    gate_up(1, 3)
    hidden(1, 2)
    down(1, 1)
    hidden(1, 3)
    down(1, 2)
    cross(1, 5, 6)
    down(1, 3)
    cross(1, 7)
    ret(1, 1, 0, 1)
    ret(0, 4, 2)
    cross(1, 3, 4)
    finish(0, 0, 1)
    ret(1, 2, 0, 1)
    ret(1, 1, 2)
    cross(1, 1, 2)
    finish(0, 2)
    ret(1, 3, 0, 1)
    ret(1, 2, 2)
    hand_out(0)
    cross(1, 0)
    ret(1, 4, 0, 1)
    ret(1, 3, 2)
    finish(1, 0, 1)
    ret(1, 4, 2)
    finish(1, 2)
    hand_out(1)

    for r in range(1, EXPERTS):
        phase_a(r).wait_send()
        deliver(r).wait()
        deliver_last(r).wait()
    for w in range(2):
        for i in range(9):
            x_send(w, i).wait_send()
        for g in range(4):
            gu_send(w, g).wait_send()
            hid_send(w, g).wait_send()
        for side in range(2):
            for k in range(1, 5):
                for p in range(3):
                    z_send(w, side, k, p).wait_send()
                    back_send(w, side, k, p).wait_send()
    tile = result_x[...].reshape(EXPERTS * MAIN, 128)
    rows = dot(sel[0], result[...].reshape(EXPERTS * MAIN, 2 * width))
    rows += dot(sel[1][:, :16], unfold([tile], 2 * width // 128))
    out_ref[...] = (gate_col * rows).astype(BF16)


def local(tokens, expert_ids, router_gate, w_gate, w_up, w_down):
    n_tok, dmodel = tokens.shape
    units = w_gate.shape[0]
    width = dmodel // 8
    folded = -(-3 * width // 2048) * 128
    vmem, dma = pltpu.VMEM, pltpu.SemaphoreType.DMA

    def waves(shape_of, dtype):
        return [vmem(shape_of(n), dtype) for n in ROWS]

    return pl.pallas_call(
        kernel,
        out_shape=jax.ShapeDtypeStruct((n_tok, 2 * width), BF16),
        in_specs=[pl.BlockSpec(memory_space=pltpu.VMEM)] * 3 + [pl.BlockSpec(memory_space=pl.ANY)] * 3,
        out_specs=pl.BlockSpec(memory_space=pltpu.VMEM),
        scratch_shapes=[
            vmem((2, n_tok, EXPERTS * MAIN), BF16),
            vmem((EXPERTS, MAIN, 3 * width + folded), BF16),
            vmem((EXPERTS, MAIN, 3 * width + folded), BF16),
            vmem((2, 2, 4, units, width), BF16),
            vmem((2, 4, units, width), BF16),
            vmem((EXPERTS, MAIN, 2 * width), BF16),
            vmem((EXPERTS, MAIN, 128), BF16),
            vmem((EXPERTS, MAIN, 2 * width), BF16),
            vmem((EXPERTS, MAIN, 128), BF16),
            *waves(lambda n: (RING, 4, n, width), BF16),
            *waves(lambda n: (2, RING * n, units), F32),
            *waves(lambda n: (2, RING * n, units), F32),
            *waves(lambda n: (2, RING * n, units), F32),
            *waves(lambda n: (2, RING * n, units), BF16),
            *waves(lambda n: (RING, 4, n, width), BF16),
            *waves(lambda n: (RING, n, width), BF16),
            *waves(lambda n: (2, 4, 3, n, width), BF16),
            *waves(lambda n: (3, n, width), BF16),
            *waves(lambda n: (n, width), BF16),
            dma((3, 4)), dma((3, 4)), dma((3, 4)),
            dma((8,)), dma((8,)),
            dma((2, 2, 4, 3)), dma((2, 2, 4, 3)),
            dma((2, 9)), dma((2, 9)),
            dma((2, 4)), dma((2, 4)),
            dma((2, 4)), dma((2, 4)),
            dma((2, 8)), dma((2, 8)),
            dma((2, 2, 4, 3)), dma((2, 2, 4, 3)),
            dma((2,)), dma((2,)),
            dma((8,)), dma((8,)),
            dma((8,)), dma((8,)),
        ],
        compiler_params=pltpu.CompilerParams(
            collective_id=0, has_side_effects=True, vmem_limit_bytes=60 * 2**20
        ),
        cost_estimate=pl.CostEstimate(flops=7 * 10**9, bytes_accessed=10**7, transcendentals=200000),
        name="routed_experts",
    )(tokens, expert_ids.reshape(1, n_tok), router_gate.reshape(1, n_tok), w_gate, w_up, w_down)


def solution(mesh):
    placed = (
        P("fsdp", None),
        P("fsdp", None),
        P("fsdp"),
        P(("fsdp", "ctx"), None),
        P(("fsdp", "ctx"), None),
        P(("fsdp", "ctx"), None),
    )
    return jax.shard_map(
        local, mesh=mesh, in_specs=placed, out_specs=P("fsdp", "ctx"), check_vma=False
    )
```

```python
import functools

import jax
import jax.numpy as jnp
from jax import lax
from jax.experimental import pallas as pl
from jax.experimental.pallas import tpu as pltpu
from jax.sharding import PartitionSpec as P

MESH = pl.DeviceIdType.MESH
EXPERTS = 8
MAIN = 16
RING = 8
N = 4 * MAIN
BF16, F32 = jnp.bfloat16, jnp.float32
SOURCES = ((0, 0), (0, 2), (1, 0), (1, 2), (0, 1), (0, 3), (1, 1), (1, 3))
HALF = ((0, 32), (32, 32))
ORDER = (0, -1, 1, -2, 2, -3, 3, 4)
GROUPS = (((0, 5), (5, 8)), ((0, 5), (5, 7), (7, 8)))
B_BLOCKS = 6


def nt_dot(a, b):
    return lax.dot_general(a, b, (((1,), (1,)), ((), ())), preferred_element_type=F32)


def dot(a, b):
    return jnp.dot(a, b, preferred_element_type=F32)


def transposition(shape):
    r = lax.broadcasted_iota(jnp.int32, shape, 0)
    q = lax.broadcasted_iota(jnp.int32, shape, 1)
    return (((r >> 4) == (q & 15)) & ((r & 15) == (q >> 4))).astype(F32).astype(BF16)


def fold(rows):
    tiles = []
    for lo in range(0, rows.shape[1], 2048):
        part = rows[:, lo:lo + 2048]
        n = part.shape[1] // 128
        stack = jnp.concatenate([part[:, j * 128:(j + 1) * 128] for j in range(n)], axis=0)
        tiles.append(dot(transposition((128, n * 16)), stack).astype(BF16))
    return tiles


def unfold(tiles, n_blocks):
    blocks = []
    for t, tile in enumerate(tiles):
        n = min(16, n_blocks - 16 * t)
        stack = dot(transposition((n * 16, 128)), tile).astype(BF16)
        blocks += [stack[j * 16:(j + 1) * 16] for j in range(n)]
    return jnp.concatenate(blocks, axis=1)


def widths_of(dmodel):
    wb = B_BLOCKS * 128
    wa = dmodel // 4 - wb
    return wa, wb, -(-B_BLOCKS // 2) * 128


def group_rows(w, g):
    at = 0
    for h, (lo, hi) in enumerate(GROUPS[w]):
        main, extra = (hi - lo) * N, w * (-(-(hi - lo) // 2) * 16)
        if h == g:
            return at, main + extra, extra
        at += main + extra
    return at, 0, 0


def pair_up(left, right):
    if right.shape[1] < left.shape[1]:
        pad = jnp.zeros((8, left.shape[1] - right.shape[1]), F32)
        right = jnp.concatenate([right, pad], axis=1)
    return jnp.concatenate([left, right], axis=0)


def kernel(
    tok_ref, ids_ref, gate_ref, wg_ref, wu_ref, wd_ref,
    out_ref,
    tok, sel, send, send_x, staged, staged_x, wgu_a, wgu_b, wdn_a, wdn_b,
    parcel_a, parcel_b, parcel_x, result_a, result_b, result_x, xo, yo, yxo, back_o, final_o, fxo, *rest,
):
    per_wave, sems = rest[:28], rest[28:]
    (
        x_a, x_b, gu_own, gu_out, gu_in, hid, y_a, y_b, yx, back_a, back_b, final_a, final_b, fx,
    ) = [per_wave[2 * i:2 * i + 2] for i in range(14)]
    (
        t_sem, w_sem, ws_sem, wr_sem, as_sem, ar_sem, zs_sem, zr_sem, xs_sem, xr_sem,
        gs_sem, gr_sem, hs_sem, hr_sem, ys_sem, yr_sem, bs_sem, br_sem, fs_sem, fr_sem,
        ds_sem, dr_sem,
    ) = sems
    c, f = lax.axis_index("ctx"), lax.axis_index("fsdp")
    xl, co = c // 2, c % 2
    col, z = f // RING, f % RING
    wa, wb = x_a[0].shape[3], x_b[0].shape[3]
    wo = yxo.shape[2]
    share = 2 * wa + wb

    def on_z(d):
        return (c, col * RING + (z + d + RING) % RING)

    def column(r, sign):
        dx, dy = SOURCES[r]
        return (col // 4 + dx) % 2 * 4 + (col % 4 + sign * dy + 4) % 4

    def in_column(e):
        return (c, e * RING + z)

    sibling = (c + 1 - 2 * co, f)
    across = ((c + 2) % 4, f)

    def remote(src, dst, ssem, rsem, dev):
        return pltpu.make_async_remote_copy(
            src_ref=src, dst_ref=dst, send_sem=ssem, recv_sem=rsem, device_id=dev, device_id_type=MESH
        )

    def column_of(core, blk):
        quarter = (blk % 2) * 2 + core
        return pl.multiple_of(quarter * (wa + wb) + (wa if blk >= 2 else 0), 128)

    def columns(ref, core, blk):
        return ref.at[:, pl.ds(column_of(core, blk), wb if blk >= 2 else wa)]

    own_b = pl.multiple_of((xl * 2 + co) * (wa + wb) + wa, 128)
    share_refs = [columns(tok_ref, co, 0), columns(tok_ref, co, 1), tok_ref.at[:, pl.ds(own_b, wb)]]
    spans = ((0, wa), (wa, 2 * wa), (2 * wa, share))
    get_tok = [
        pltpu.make_async_copy(share_refs[p], tok.at[:, spans[p][0]:spans[p][1]], t_sem.at[p]) for p in range(3)
    ]
    for cp in get_tok:
        cp.start()

    barrier = pltpu.get_barrier_semaphore()
    partners = [on_z(1), on_z(-1), sibling, across] + [in_column((col + i) % EXPERTS) for i in range(1, EXPERTS)]
    for dev in partners:
        pl.semaphore_signal(barrier, inc=1, device_id=dev, device_id_type=MESH)

    def weight_slot(m, unit_core, blk):
        if m == 2:
            return (wdn_b if blk >= 2 else wdn_a).at[unit_core, blk % 2]
        return (wgu_b if blk >= 2 else wgu_a).at[m, unit_core, blk % 2]

    w_refs = (wg_ref, wu_ref, wd_ref)
    own_w = [
        pltpu.make_async_copy(columns(w_refs[m], co, blk), weight_slot(m, co, blk), w_sem.at[m, blk])
        for m in range(3) for blk in range(4)
    ]
    other_w = [
        remote(
            columns(w_refs[m], 1 - co, blk), weight_slot(m, co, blk),
            ws_sem.at[m, blk], wr_sem.at[m, blk], sibling,
        )
        for m in range(3) for blk in range(4)
    ]

    n_tok = tok.shape[0]
    rows_i = lax.broadcasted_iota(jnp.int32, (n_tok, n_tok), 0)
    cols_i = lax.broadcasted_iota(jnp.int32, (n_tok, n_tok), 1)
    ids_row = ids_ref[...]
    ids_col = jnp.sum(jnp.where(rows_i == cols_i, ids_row, 0), axis=1, keepdims=True)
    same = (ids_row == ids_col) & (cols_i < rows_i)
    rank = jnp.sum(same.astype(jnp.int32), axis=1, keepdims=True)
    main = ((cols_i == ids_col * MAIN + rank) & (rank < MAIN)).astype(F32)
    last = ((cols_i == ids_col) & (rank == MAIN)).astype(F32)
    sel[0] = main.astype(BF16)
    sel[1] = last.astype(BF16)
    pack = jnp.transpose(main).astype(BF16)
    for p in range(3):
        lo, hi = spans[p]
        get_tok[p].wait()
        send[:, :, lo:hi] = dot(pack, tok[:, lo:hi]).astype(BF16).reshape(EXPERTS, MAIN, hi - lo)

    pl.semaphore_wait(barrier, len(partners))

    def phase_a(r):
        e = column(r, -1)
        return remote(send.at[e], staged.at[r], as_sem.at[0, r], ar_sem.at[0, r], in_column(e))

    def phase_a_last(r):
        e = column(r, -1)
        return remote(send_x.at[e], staged_x.at[r], as_sem.at[1, r], ar_sem.at[1, r], in_column(e))

    def x_block(w, pi, p):
        return x_b[w].at[pi, xl] if p == 2 else x_a[w].at[pi, p]

    def y_block(w, pi, p):
        if p == 3:
            return yo.at[pi, xl]
        return y_b[w].at[pi, xl] if p == 2 else y_a[w].at[pi, p]

    def land(w):
        for q in range(4):
            r = 4 * w + q
            if r:
                phase_a(r).wait_recv()
            here = send.at[col] if r == 0 else staged.at[r]
            for p in range(3):
                x_block(w, z, p)[q * MAIN:(q + 1) * MAIN, :] = here[:, spans[p][0]:spans[p][1]]

    def land_last():
        for r in range(1, EXPERTS):
            phase_a_last(r).wait_recv()
        staged_x[0] = send_x[col]
        tiles = [
            staged_x[:, :, lo:lo + 128].reshape(EXPERTS * MAIN, 128) for lo in range(0, staged_x.shape[2], 128)
        ]
        extra = unfold(tiles, share // 128).astype(F32)[:8]
        xo[z, xl, :, :wa] = pair_up(extra[:, :wa], extra[:, wa:2 * wa]).astype(BF16)
        xo[z, xl, :, wa:] = pair_up(extra[:, 2 * wa:2 * wa + wo], extra[:, 2 * wa + wo:]).astype(BF16)

    def plane(d):
        return (z + d + RING) % RING

    def z_send(w, side, k, p):
        d = 1 - 2 * side
        pi = plane(-d * (k - 1))
        blk = xo.at[pi, xl] if p == 3 else x_block(w, pi, p)
        if k == 4 and p < 3:
            blk = blk.at[pl.ds(*HALF[side])]
        return remote(blk, blk, zs_sem.at[w, side, k - 1, p], zr_sem.at[w, side, k - 1, p], on_z(d))

    def goes(w, side, k, p):
        return p < 3 or (w == 1 and not (k == 4 and side == 1))

    def x_send(w, i):
        if i < 7:
            blk = x_b[w].at[plane(ORDER[i]), xl]
        else:
            blk = x_b[w].at[plane(4), xl].at[pl.ds(*HALF[i - 7])]
        return remote(blk, blk, xs_sem.at[w, i], xr_sem.at[w, i], across)

    def x_send_last(i):
        blk = xo.at[plane(ORDER[i]), xl, :, wa:]
        return remote(blk, blk, xs_sem.at[2, i], xr_sem.at[2, i], across)

    def z_step(w, k):
        for p in (2, 3, 0, 1):
            for side in range(2):
                if k > 1 and goes(w, side, k - 1, p):
                    z_send(w, side, k - 1, p).wait_recv()
                if k < 5 and goes(w, side, k, p):
                    z_send(w, side, k, p).start()
                if p == 2 and (k > 1 or side == 0):
                    x_send(w, 2 * (k - 1) - 1 + side if k > 1 else 0).start()
                if p == 3 and w == 1 and not (k in (1, 5) and side == 1):
                    x_send_last(2 * (k - 1) - 1 + side if k > 1 else 0).start()

    def gu_send(w, g):
        lo, n, _ = group_rows(w, g)
        rows = pl.ds(lo, n)
        return remote(gu_out[w].at[:, rows], gu_in[w].at[:, rows], gs_sem.at[w, g], gr_sem.at[w, g], sibling)

    def hid_send(w, g):
        lo, n, _ = group_rows(w, g)
        mine = hid[w].at[co, pl.ds(lo, n)]
        return remote(mine, mine, hs_sem.at[w, g], hr_sem.at[w, g], sibling)

    def last_rows(pi, blk):
        if blk < 2:
            return xo[pi, xl, :, :wa].astype(F32)[8 * blk:8 * blk + 8]
        both = xo[pi, blk - 2, :, wa:].astype(F32)
        return jnp.concatenate([both[:8], both[8:, :wb - wo]], axis=1)

    def gate_up(w, g):
        lo, n, extra = group_rows(w, g)
        ids = range(*GROUPS[w][g])
        for i in ids:
            x_send(w, i).wait_recv()
            if i == 7:
                x_send(w, 8).wait_recv()
            if w == 1:
                x_send_last(i).wait_recv()
        for blk in range(4):
            xs, wgu = (x_b[w], wgu_b) if blk >= 2 else (x_a[w], wgu_a)
            parts = [xs[plane(ORDER[i]), blk % 2] for i in ids]
            if extra:
                lasts = [last_rows(plane(ORDER[i]), blk) for i in ids]
                if len(lasts) % 2:
                    lasts.append(jnp.zeros_like(lasts[0]))
                parts.append(jnp.concatenate(lasts, axis=0).astype(BF16))
            rows = jnp.concatenate(parts, axis=0)
            for m in range(2):
                for acc, u in ((gu_own[w], co), (gu_out[w], 1 - co)):
                    term = nt_dot(rows, wgu[m, u, blk % 2])
                    acc[m, lo:lo + n] = acc[m, lo:lo + n] + term if blk else term
        gu_send(w, g).start()

    def hidden(w, g):
        lo, n, _ = group_rows(w, g)
        gu_send(w, g).wait_recv()
        gate = gu_own[w][0, lo:lo + n] + gu_in[w][0, lo:lo + n]
        up = gu_own[w][1, lo:lo + n] + gu_in[w][1, lo:lo + n]
        hid[w][co, lo:lo + n] = (gate / (1.0 + jnp.exp(-gate)) * up).astype(BF16)
        hid_send(w, g).start()

    def down(w, g):
        lo, n, extra = group_rows(w, g)
        ids = range(*GROUPS[w][g])
        hid_send(w, g).wait_recv()
        lasts = {}
        for blk in (2, 3, 0, 1):
            wdn, ys = (wdn_b, y_b[w]) if blk >= 2 else (wdn_a, y_a[w])
            part = dot(hid[w][0, lo:lo + n], wdn[0, blk % 2]) + dot(hid[w][1, lo:lo + n], wdn[1, blk % 2])
            for at, i in enumerate(ids):
                ys[plane(ORDER[i]), blk % 2] = part[at * N:(at + 1) * N].astype(BF16)
                if extra:
                    at8 = len(ids) * N + 8 * at
                    mine = part[at8:at8 + 8]
                    if blk >= 2:
                        yo[plane(ORDER[i]), blk - 2, :, wa:] = pair_up(mine[:, :wo], mine[:, wo:]).astype(BF16)
                    elif blk == 0:
                        lasts[i] = mine
                    else:
                        yo[plane(ORDER[i]), xl, :, :wa] = pair_up(lasts[i], mine).astype(BF16)

    def y_send(w, i):
        return remote(y_b[w].at[plane(ORDER[i]), 1 - xl], yx[w].at[i], ys_sem.at[w, i], yr_sem.at[w, i], across)

    def y_send_last(i):
        return remote(
            yo.at[plane(ORDER[i]), 1 - xl, :, wa:], yxo.at[i], ys_sem.at[2, i], yr_sem.at[2, i], across
        )

    def cross(w, *idx):
        for i in idx:
            y_send(w, i).start()
            if w == 1:
                y_send_last(i).start()

    def add_across(w, i):
        pi = plane(ORDER[i])
        y_send(w, i).wait()
        y_b[w][pi, xl] = (y_b[w][pi, xl].astype(F32) + yx[w][i].astype(F32)).astype(BF16)

    def add_across_last(i):
        pi = plane(ORDER[i])
        y_send_last(i).wait()
        yo[pi, xl, :, wa:] = (yo[pi, xl, :, wa:].astype(F32) + yxo[i].astype(F32)).astype(BF16)

    def back_block(w, side, j, p):
        if p == 3:
            return back_o.at[side, j - 1]
        return back_b[w].at[side, j - 1] if p == 2 else back_a[w].at[side, j - 1, p]

    def back_send(w, side, j, p):
        d = 1 - 2 * side
        src = y_block(w, plane(d * (5 - j)), p)
        dst = back_block(w, side, j, p)
        if j == 1 and p < 3:
            src, dst = src.at[pl.ds(*HALF[side])], dst.at[pl.ds(*HALF[side])]
        return remote(src, dst, bs_sem.at[w, side, j - 1, p], br_sem.at[w, side, j - 1, p], on_z(d))

    def comes(w, side, j, p):
        return p < 3 or (w == 1 and not (j == 1 and side == 1))

    def ret(w, j, *ps):
        for p in ps:
            for side in range(2):
                if not comes(w, side, j, p):
                    continue
                d = 1 - 2 * side
                if p >= 2 and (j > 1 or side == 0):
                    (add_across_last if p == 3 else functools.partial(add_across, w))(ORDER.index(d * (5 - j)))
                if j > 1 and comes(w, side, j - 1, p):
                    back_send(w, side, j - 1, p).wait_recv()
                    here, came = y_block(w, plane(d * (5 - j)), p), back_block(w, side, j - 1, p)
                    if j == 2 and p < 3:
                        here, came = here.at[pl.ds(*HALF[side])], came.at[pl.ds(*HALF[side])]
                    here[...] = (here[...].astype(F32) + came[...].astype(F32)).astype(BF16)
                back_send(w, side, j, p).start()

    def f_send(w):
        return remote(final_a[w].at[1 - xl], fx[w], fs_sem.at[w], fr_sem.at[w], across)

    def f_send_last():
        return remote(final_o.at[:, :wa], fxo, fs_sem.at[2], fr_sem.at[2], across)

    def finish(w, *ps):
        for p in ps:
            if p == 2:
                add_across(w, 0)
            if p == 3:
                add_across_last(0)
            total = y_block(w, z, p)[...].astype(F32)
            for side in range(2):
                back_send(w, side, 4, p).wait_recv()
                total += back_block(w, side, 4, p)[...].astype(F32)
            if p == 3:
                final_o[...] = total.astype(BF16)
                f_send_last().start()
            elif p == 2:
                final_b[w][...] = total.astype(BF16)
            else:
                final_a[w][p] = total.astype(BF16)
                if p == 1:
                    f_send(w).start()

    def deliver(r, kind):
        parcel, result = ((parcel_a, result_a), (parcel_b, result_b), (parcel_x, result_x))[kind]
        return remote(
            parcel.at[r], result.at[col], ds_sem.at[kind, r], dr_sem.at[kind, r], in_column(column(r, 1))
        )

    def hand_out(w, kind):
        if kind == 0:
            f_send(w).wait()
            mine = (final_a[w][xl].astype(F32) + fx[w][...].astype(F32)).astype(BF16)
        else:
            mine = final_b[w][...]
        parcel, result = ((parcel_a, result_a), (parcel_b, result_b))[kind]
        parcel[4 * w:4 * w + 4] = mine.reshape(4, MAIN, mine.shape[1])
        for q in range(4):
            if w or q:
                deliver(4 * w + q, kind).start()
        if w == 0:
            result[col] = parcel[0]

    def hand_out_last():
        f_send_last().wait()
        both = final_o[:, :wa].astype(F32) + fxo[...].astype(F32)
        mine = jnp.where(xl == 0, both[:8], both[8:])
        over = final_o[:, wa:].astype(F32)
        mine = jnp.concatenate([mine, over[:8], over[8:, :wb - wo]], axis=1)
        mine = jnp.concatenate([mine, jnp.zeros_like(mine)], axis=0).astype(BF16)
        parcel_x[...] = fold(mine)[0].reshape(EXPERTS, MAIN, 128)
        for r in range(1, EXPERTS):
            deliver(r, 2).start()
        result_x[col] = parcel_x[0]

    for r in range(1, 4):
        phase_a(r).start()
    for cp in own_w + other_w:
        cp.start()
    for r in range(4, EXPERTS):
        phase_a(r).start()
    pack_last = jnp.transpose(last)[:16].astype(BF16)
    for t, tile in enumerate(fold(dot(pack_last, tok[...]).astype(BF16))):
        send_x[:, :, t * 128:(t + 1) * 128] = tile.reshape(EXPERTS, MAIN, 128)
    for r in range(1, EXPERTS):
        phase_a_last(r).start()

    land(0)
    z_step(0, 1)
    land(1)
    land_last()
    for cp in own_w + other_w:
        cp.wait()
    z_step(0, 2)
    z_step(0, 3)
    gate_up(0, 0)
    z_step(0, 4)
    z_step(1, 1)
    hidden(0, 0)
    down(0, 0)
    z_step(0, 5)
    z_step(1, 2)
    gate_up(0, 1)
    hidden(0, 1)
    z_step(1, 3)
    down(0, 1)
    cross(0, 7, 5, 6)
    gate_up(1, 0)
    z_step(1, 4)
    hidden(1, 0)
    ret(0, 1, 0, 1)
    cross(0, 3, 4)
    z_step(1, 5)
    ret(0, 1, 2)
    ret(0, 2, 0, 1)
    gate_up(1, 1)
    ret(0, 2, 2)
    ret(0, 3, 0, 1)
    gate_up(1, 2)
    hidden(1, 1)
    cross(0, 1, 2)
    hidden(1, 2)
    down(1, 0)
    ret(0, 3, 2)
    ret(0, 4, 0, 1)
    down(1, 2)
    cross(1, 7)
    ret(1, 1, 0, 1)
    cross(0, 0)
    down(1, 1)
    cross(1, 5, 6)
    ret(0, 4, 2)
    ret(1, 2, 0, 1)
    ret(1, 1, 3, 2)
    finish(0, 0, 1)
    cross(1, 3, 4)
    ret(1, 3, 0, 1)
    ret(1, 2, 3, 2)
    finish(0, 2)
    cross(1, 1, 2, 0)
    hand_out(0, 0)
    hand_out(0, 1)
    ret(1, 4, 0, 1)
    ret(1, 3, 3, 2)
    finish(1, 0, 1)
    ret(1, 4, 3, 2)
    hand_out(1, 0)
    finish(1, 3)
    finish(1, 2)
    hand_out(1, 1)
    hand_out_last()
    for r in range(1, EXPERTS):
        phase_a(r).wait_send()
        phase_a_last(r).wait_send()
    for w in range(2):
        for i in range(9):
            x_send(w, i).wait_send()
        for g in range(len(GROUPS[w])):
            gu_send(w, g).wait_send()
            hid_send(w, g).wait_send()
        for side in range(2):
            for k in range(1, 5):
                for p in range(4):
                    if goes(w, side, k, p):
                        z_send(w, side, k, p).wait_send()
                    if comes(w, side, k, p):
                        back_send(w, side, k, p).wait_send()
    for i in range(8):
        x_send_last(i).wait_send()
    for r in range(1, EXPERTS):
        deliver(r, 2).wait()
    gate_col = jnp.sum(jnp.where(rows_i == cols_i, gate_ref[...], 0.0), axis=1, keepdims=True)
    extra = unfold([result_x[...].reshape(EXPERTS * MAIN, 128)], (wa + wb) // 128)
    for kind, result, lo, hi in ((0, result_a, 0, wa), (1, result_b, wa, wa + wb)):
        for r in range(1, EXPERTS):
            deliver(r, kind).wait()
        rows = dot(sel[0], result[...].reshape(EXPERTS * MAIN, hi - lo)) + dot(sel[1][:, :16], extra[:, lo:hi])
        out_ref[:, lo:hi] = (gate_col * rows).astype(BF16)


def local(tokens, expert_ids, router_gate, w_gate, w_up, w_down):
    n_tok, dmodel = tokens.shape
    units = w_gate.shape[0]
    wa, wb, wo = widths_of(dmodel)
    share = 2 * wa + wb
    folded = -(-share // 2048) * 128
    vmem, dma = pltpu.VMEM, pltpu.SemaphoreType.DMA
    n_rows = [group_rows(w, len(GROUPS[w]))[0] for w in range(2)]

    def waves(*shape, dtype=BF16):
        return [vmem(shape, dtype)] * 2

    def per_row(*shape, dtype=F32):
        return [vmem((2, n, units), dtype) for n in n_rows]

    return pl.pallas_call(
        kernel,
        out_shape=jax.ShapeDtypeStruct((n_tok, wa + wb), BF16),
        in_specs=[pl.BlockSpec(memory_space=pl.ANY)] + [pl.BlockSpec(memory_space=pltpu.VMEM)] * 2
        + [pl.BlockSpec(memory_space=pl.ANY)] * 3,
        out_specs=pl.BlockSpec(memory_space=pltpu.VMEM),
        scratch_shapes=[
            vmem((n_tok, share), BF16),
            vmem((2, n_tok, EXPERTS * MAIN), BF16),
            vmem((EXPERTS, MAIN, share), BF16),
            vmem((EXPERTS, MAIN, folded), BF16),
            vmem((EXPERTS, MAIN, share), BF16),
            vmem((EXPERTS, MAIN, folded), BF16),
            vmem((2, 2, 2, units, wa), BF16),
            vmem((2, 2, 2, units, wb), BF16),
            vmem((2, 2, units, wa), BF16),
            vmem((2, 2, units, wb), BF16),
            vmem((EXPERTS, MAIN, wa), BF16),
            vmem((EXPERTS, MAIN, wb), BF16),
            vmem((EXPERTS, MAIN, 128), BF16),
            vmem((EXPERTS, MAIN, wa), BF16),
            vmem((EXPERTS, MAIN, wb), BF16),
            vmem((EXPERTS, MAIN, 128), BF16),
            vmem((RING, 2, 16, wa + wo), BF16),
            vmem((RING, 2, 16, wa + wo), BF16),
            vmem((RING, 16, wo), BF16),
            vmem((2, 4, 16, wa + wo), BF16),
            vmem((16, wa + wo), BF16),
            vmem((16, wa), BF16),
            *waves(RING, 2, N, wa),
            *waves(RING, 2, N, wb),
            *per_row(),
            *per_row(),
            *per_row(),
            *per_row(dtype=BF16),
            *waves(RING, 2, N, wa),
            *waves(RING, 2, N, wb),
            *waves(RING, N, wb),
            *waves(2, 4, 2, N, wa),
            *waves(2, 4, N, wb),
            *waves(2, N, wa),
            *waves(N, wb),
            *waves(N, wa),
            dma((3,)),
            dma((3, 4)), dma((3, 4)), dma((3, 4)),
            dma((2, 8)), dma((2, 8)),
            dma((2, 2, 4, 4)), dma((2, 2, 4, 4)),
            dma((3, 9)), dma((3, 9)),
            dma((2, 4)), dma((2, 4)),
            dma((2, 4)), dma((2, 4)),
            dma((3, 8)), dma((3, 8)),
            dma((2, 2, 4, 4)), dma((2, 2, 4, 4)),
            dma((3,)), dma((3,)),
            dma((3, 8)), dma((3, 8)),
        ],
        compiler_params=pltpu.CompilerParams(
            collective_id=0, has_side_effects=True, vmem_limit_bytes=60 * 2**20
        ),
        cost_estimate=pl.CostEstimate(flops=7 * 10**9, bytes_accessed=10**7, transcendentals=200000),
        name="routed_experts",
    )(tokens, expert_ids.reshape(1, n_tok), router_gate.reshape(1, n_tok), w_gate, w_up, w_down)


def solution(mesh):
    placed = (
        P("fsdp", None),
        P("fsdp", None),
        P("fsdp"),
        P(("fsdp", "ctx"), None),
        P(("fsdp", "ctx"), None),
        P(("fsdp", "ctx"), None),
    )
    return jax.shard_map(
        local, mesh=mesh, in_specs=placed, out_specs=P("fsdp", "ctx"), check_vma=False
    )
```

```python
import functools

import jax
import jax.numpy as jnp
from jax import lax
from jax.experimental import pallas as pl
from jax.experimental.pallas import tpu as pltpu
from jax.sharding import PartitionSpec as P

MESH = pl.DeviceIdType.MESH
EXPERTS = 8
MAIN = 16
RING = 8
N = 4 * MAIN
BF16, F32 = jnp.bfloat16, jnp.float32
SOURCES = ((0, 0), (0, 2), (1, 0), (1, 2), (0, 1), (0, 3), (1, 1), (1, 3))
UNITS = (
    (0, 0, 16, (2, 4), ((0, 16), (0, 16))),
    (0, 16, 48, (2, 0, 1), ((16, 16), (32, 32))),
    (1, 0, 64, (2, 3, 0, 1), ((0, 32), (32, 32))),
)
LAST_SPLIT = ((0, 32), (32, 32))
CROSSED = ((0,), (1, 2), (3, 4), (5, 6), (7,))
ORDER = (0, -1, 1, -2, 2, -3, 3, 4)
GROUPS = (((0, 5), (5, 8)), ((0, 5), (5, 7), (7, 8)))
B_BLOCKS = 6


def nt_dot(a, b):
    return lax.dot_general(a, b, (((1,), (1,)), ((), ())), preferred_element_type=F32)


def dot(a, b):
    return jnp.dot(a, b, preferred_element_type=F32)


def transposition(shape):
    r = lax.broadcasted_iota(jnp.int32, shape, 0)
    q = lax.broadcasted_iota(jnp.int32, shape, 1)
    return (((r >> 4) == (q & 15)) & ((r & 15) == (q >> 4))).astype(F32).astype(BF16)


def fold(rows):
    tiles = []
    for lo in range(0, rows.shape[1], 2048):
        part = rows[:, lo:lo + 2048]
        n = part.shape[1] // 128
        stack = jnp.concatenate([part[:, j * 128:(j + 1) * 128] for j in range(n)], axis=0)
        tiles.append(dot(transposition((128, n * 16)), stack).astype(BF16))
    return tiles


def unfold(tiles, n_blocks):
    blocks = []
    for t, tile in enumerate(tiles):
        n = min(16, n_blocks - 16 * t)
        stack = dot(transposition((n * 16, 128)), tile).astype(BF16)
        blocks += [stack[j * 16:(j + 1) * 16] for j in range(n)]
    return jnp.concatenate(blocks, axis=1)


def widths_of(dmodel):
    wb = B_BLOCKS * 128
    wa = dmodel // 4 - wb
    return wa, wb, -(-B_BLOCKS // 2) * 128


def group_rows(w, g):
    at = 0
    for h, (lo, hi) in enumerate(GROUPS[w]):
        main, extra = (hi - lo) * N, w * (-(-(hi - lo) // 2) * 16)
        if h == g:
            return at, main + extra, extra
        at += main + extra
    return at, 0, 0


def pair_up(left, right):
    if right.shape[1] < left.shape[1]:
        pad = jnp.zeros((8, left.shape[1] - right.shape[1]), F32)
        right = jnp.concatenate([right, pad], axis=1)
    return jnp.concatenate([left, right], axis=0)


def moves(u, side, k, p):
    if p not in UNITS[u][3]:
        return False
    if k < 4:
        return True
    if u == 0:
        return side == (0 if p == 2 else 1)
    return p != 3 or side == 0


def rows_of(u, side, k):
    return UNITS[u][4][side] if k == 4 else UNITS[u][1:3]


def kernel(
    tok_ref, ids_ref, gate_ref, wg_ref, wu_ref, wd_ref,
    out_ref,
    tok, sel, send, send_x, staged, staged_x, wgu_a, wgu_b, wdn_a, wdn_b,
    parcel_a, parcel_b, parcel_x, result_a, result_b, result_x, xo, yo, yxo, back_o, final_o, fxo, *rest,
):
    per_wave, sems = rest[:28], rest[28:]
    (
        x_a, x_b, gu_own, gu_out, gu_in, hid, y_a, y_b, yx, back_a, back_b, final_a, final_b, fx,
    ) = [per_wave[2 * i:2 * i + 2] for i in range(14)]
    (
        t_sem, w_sem, ws_sem, wr_sem, as_sem, ar_sem, zs_sem, zr_sems, xs_sem, xr_sem,
        gs_sem, gr_sem, hs_sem, hr_sem, ys_sem, yr_sem, bs_sem, br_sems, fs_sem, fr_sem,
        ds_sem, dr_sem,
    ) = sems

    def wait_for(sem, ref):
        pltpu.make_async_copy(ref, ref, sem).wait()

    c, f = lax.axis_index("ctx"), lax.axis_index("fsdp")
    xl, co = c // 2, c % 2
    col, z = f // RING, f % RING
    wa, wb = x_a[0].shape[3], x_b[0].shape[3]
    wo = yxo.shape[2]
    share = 2 * wa + wb

    def on_z(d):
        return (c, col * RING + (z + d + RING) % RING)

    def column(r, sign):
        dx, dy = SOURCES[r]
        return (col // 4 + dx) % 2 * 4 + (col % 4 + sign * dy + 4) % 4

    def in_column(e):
        return (c, e * RING + z)

    sibling = (c + 1 - 2 * co, f)
    across = ((c + 2) % 4, f)

    def remote(src, dst, ssem, rsem, dev):
        return pltpu.make_async_remote_copy(
            src_ref=src, dst_ref=dst, send_sem=ssem, recv_sem=rsem, device_id=dev, device_id_type=MESH
        )

    def column_of(core, blk):
        quarter = (blk % 2) * 2 + core
        return pl.multiple_of(quarter * (wa + wb) + (wa if blk >= 2 else 0), 128)

    def columns(ref, core, blk):
        return ref.at[:, pl.ds(column_of(core, blk), wb if blk >= 2 else wa)]

    own_b = pl.multiple_of((xl * 2 + co) * (wa + wb) + wa, 128)
    share_refs = [columns(tok_ref, co, 0), columns(tok_ref, co, 1), tok_ref.at[:, pl.ds(own_b, wb)]]
    spans = ((0, wa), (wa, 2 * wa), (2 * wa, share))
    get_tok = [
        pltpu.make_async_copy(share_refs[p], tok.at[:, spans[p][0]:spans[p][1]], t_sem.at[p]) for p in range(3)
    ]
    for cp in get_tok:
        cp.start()

    barrier = pltpu.get_barrier_semaphore()
    partners = [on_z(1), on_z(-1), sibling, across] + [in_column((col + i) % EXPERTS) for i in range(1, EXPERTS)]
    for dev in partners:
        pl.semaphore_signal(barrier, inc=1, device_id=dev, device_id_type=MESH)

    def weight_slot(m, unit_core, blk):
        if m == 2:
            return (wdn_b if blk >= 2 else wdn_a).at[unit_core, blk % 2]
        return (wgu_b if blk >= 2 else wgu_a).at[m, unit_core, blk % 2]

    w_refs = (wg_ref, wu_ref, wd_ref)
    own_w = [
        pltpu.make_async_copy(columns(w_refs[m], co, blk), weight_slot(m, co, blk), w_sem.at[m // 2, blk // 2])
        for m in range(3) for blk in range(4)
    ]
    other_w = [
        remote(
            columns(w_refs[m], 1 - co, blk), weight_slot(m, co, blk),
            ws_sem.at[m // 2, blk // 2], wr_sem.at[m // 2, blk // 2], sibling,
        )
        for m in range(3) for blk in range(4)
    ]

    def weights_wait(sem):
        for m, arrays in ((0, (wgu_a.at[:, 0], wgu_b.at[:, 0])), (1, (wdn_a.at[0], wdn_b.at[0]))):
            for part in range(2):
                wait_for(sem.at[m, part], arrays[part])


    n_tok = tok.shape[0]
    rows_i = lax.broadcasted_iota(jnp.int32, (n_tok, n_tok), 0)
    cols_i = lax.broadcasted_iota(jnp.int32, (n_tok, n_tok), 1)
    ids_row = ids_ref[...]
    ids_col = jnp.sum(jnp.where(rows_i == cols_i, ids_row, 0), axis=1, keepdims=True)
    same = (ids_row == ids_col) & (cols_i < rows_i)
    rank = jnp.sum(same.astype(jnp.int32), axis=1, keepdims=True)
    main = ((cols_i == ids_col * MAIN + rank) & (rank < MAIN)).astype(F32)
    last = ((cols_i == ids_col) & (rank == MAIN)).astype(F32)
    sel[0] = main.astype(BF16)
    sel[1] = last.astype(BF16)
    pack = jnp.transpose(main).astype(BF16)
    for p in range(3):
        lo, hi = spans[p]
        get_tok[p].wait()
        send[:, :, lo:hi] = dot(pack, tok[:, lo:hi]).astype(BF16).reshape(EXPERTS, MAIN, hi - lo)

    for p in range(3):
        x_block = (x_b[0].at[z, xl] if p == 2 else x_a[0].at[z, p])
        x_block[:MAIN, :] = send[col, :, spans[p][0]:spans[p][1]]

    pl.semaphore_wait(barrier, len(partners))

    def phase_a(r):
        e = column(r, -1)
        return remote(send.at[e], staged.at[r], as_sem.at[0], ar_sem.at[r // 4], in_column(e))

    def phase_a_last(r):
        e = column(r, -1)
        return remote(send_x.at[e], staged_x.at[r], as_sem.at[1], ar_sem.at[2], in_column(e))

    def block(arrays, w, pi, p, rows):
        a, b, last = arrays
        if p == 3:
            return last.at[pi, xl]
        if p == 2:
            return b[w].at[pi, xl, pl.ds(*rows)]
        return a[w].at[pi, :, pl.ds(*rows)] if p == 4 else a[w].at[pi, p, pl.ds(*rows)]

    x_all, y_all = (x_a, x_b, xo), (y_a, y_b, yo)

    def land(w):
        first = 1 - w
        wait_for(ar_sem.at[w], staged.at[pl.ds(first, 4 - first)])
        for p in range(3):
            got = staged[4 * w + first:4 * w + 4, :, spans[p][0]:spans[p][1]]
            here = block(x_all, w, z, p, (first * MAIN, (4 - first) * MAIN))
            here[...] = got.reshape((4 - first) * MAIN, got.shape[2])

    def land_last():
        wait_for(ar_sem.at[2], staged_x.at[pl.ds(1, 7)])
        staged_x[0] = send_x[col]
        tiles = [
            staged_x[:, :, lo:lo + 128].reshape(EXPERTS * MAIN, 128) for lo in range(0, staged_x.shape[2], 128)
        ]
        extra = unfold(tiles, share // 128).astype(F32)[:8]
        xo[z, xl, :, :wa] = pair_up(extra[:, :wa], extra[:, wa:2 * wa]).astype(BF16)
        xo[z, xl, :, wa:] = pair_up(extra[:, 2 * wa:2 * wa + wo], extra[:, 2 * wa + wo:]).astype(BF16)

    def plane(d):
        return (z + d + RING) % RING

    def lane(sems_of, u, side, k, p):
        return sems_of[u].at[side, k - 1, UNITS[u][3].index(p)]

    def sent(sem, w, p):
        return sem.at[4 if p == 3 else 2 * w + int(p == 2)]

    def z_send(u, side, k, p):
        d = 1 - 2 * side
        w = UNITS[u][0]
        blk = block(x_all, w, plane(-d * (k - 1)), p, rows_of(u, side, k))
        return remote(blk, blk, sent(zs_sem, w, p), lane(zr_sems, u, side, k, p), on_z(d))

    def group_of(w, i):
        return [g for g, (lo, hi) in enumerate(GROUPS[w]) if lo <= i < hi][0]

    def x_send(w, i):
        if i < 7:
            blk = x_b[w].at[plane(ORDER[i]), xl]
        else:
            blk = x_b[w].at[plane(4), xl].at[pl.ds(*LAST_SPLIT[i - 7])]
        return remote(blk, blk, xs_sem.at[w], xr_sem.at[w, group_of(w, min(i, 7))], across)

    def x_send_last(i):
        blk = xo.at[plane(ORDER[i]), xl, :, wa:]
        return remote(blk, blk, xs_sem.at[2], xr_sem.at[2, group_of(1, i)], across)

    def z_step(u, k):
        w = UNITS[u][0]
        for p in UNITS[u][3]:
            for side in range(2):
                if k > 1 and moves(u, side, k - 1, p):
                    z_send(u, side, k - 1, p).wait_recv()
                if k < 5 and moves(u, side, k, p):
                    z_send(u, side, k, p).start()
                if u and p == 2 and (k > 1 or side == 0):
                    x_send(w, 2 * (k - 1) - 1 + side if k > 1 else 0).start()
                if p == 3 and not (k in (1, 5) and side == 1):
                    x_send_last(2 * (k - 1) - 1 + side if k > 1 else 0).start()

    def gu_send(w, g):
        lo, n, _ = group_rows(w, g)
        rows = pl.ds(lo, n)
        return remote(gu_out[w].at[:, rows], gu_in[w].at[:, rows], gs_sem.at[w], gr_sem.at[w, g], sibling)

    def hid_send(w, g):
        lo, n, _ = group_rows(w, g)
        mine = hid[w].at[co, pl.ds(lo, n)]
        return remote(mine, mine, hs_sem.at[w], hr_sem.at[w, g], sibling)

    def last_rows(pi, blk):
        if blk < 2:
            return xo[pi, xl, :, :wa].astype(F32)[8 * blk:8 * blk + 8]
        both = xo[pi, blk - 2, :, wa:].astype(F32)
        return jnp.concatenate([both[:8], both[8:, :wb - wo]], axis=1)

    def gate_up(w, g):
        lo, n, extra = group_rows(w, g)
        ids = range(*GROUPS[w][g])
        wait_for(xr_sem.at[w, g], yx[w].at[pl.ds(0, len(ids))])
        if w == 1:
            wait_for(xr_sem.at[2, g], yxo.at[pl.ds(0, len(ids))])
        for blk in range(4):
            xs, wgu = (x_b[w], wgu_b) if blk >= 2 else (x_a[w], wgu_a)
            parts = [xs[plane(ORDER[i]), blk % 2] for i in ids]
            if extra:
                lasts = [last_rows(plane(ORDER[i]), blk) for i in ids]
                if len(lasts) % 2:
                    lasts.append(jnp.zeros_like(lasts[0]))
                parts.append(jnp.concatenate(lasts, axis=0).astype(BF16))
            rows = jnp.concatenate(parts, axis=0)
            for m in range(2):
                for acc, u in ((gu_own[w], co), (gu_out[w], 1 - co)):
                    term = nt_dot(rows, wgu[m, u, blk % 2])
                    acc[m, lo:lo + n] = acc[m, lo:lo + n] + term if blk else term
        gu_send(w, g).start()

    def hidden(w, g):
        lo, n, _ = group_rows(w, g)
        gu_send(w, g).wait_recv()
        gate = gu_own[w][0, lo:lo + n] + gu_in[w][0, lo:lo + n]
        up = gu_own[w][1, lo:lo + n] + gu_in[w][1, lo:lo + n]
        hid[w][co, lo:lo + n] = (gate / (1.0 + jnp.exp(-gate)) * up).astype(BF16)
        hid_send(w, g).start()

    def down(w, g):
        lo, n, extra = group_rows(w, g)
        ids = range(*GROUPS[w][g])
        hid_send(w, g).wait_recv()
        lasts = {}
        for blk in (2, 3, 0, 1):
            wdn, ys = (wdn_b, y_b[w]) if blk >= 2 else (wdn_a, y_a[w])
            part = dot(hid[w][0, lo:lo + n], wdn[0, blk % 2]) + dot(hid[w][1, lo:lo + n], wdn[1, blk % 2])
            for at, i in enumerate(ids):
                ys[plane(ORDER[i]), blk % 2] = part[at * N:(at + 1) * N].astype(BF16)
                if extra:
                    at8 = len(ids) * N + 8 * at
                    mine = part[at8:at8 + 8]
                    if blk >= 2:
                        yo[plane(ORDER[i]), blk - 2, :, wa:] = pair_up(mine[:, :wo], mine[:, wo:]).astype(BF16)
                    elif blk == 0:
                        lasts[i] = mine
                    else:
                        yo[plane(ORDER[i]), xl, :, :wa] = pair_up(lasts[i], mine).astype(BF16)

    def far(i):
        return [n for n, ids in enumerate(CROSSED) if i in ids][0]

    def y_send(w, i):
        return remote(
            y_b[w].at[plane(ORDER[i]), 1 - xl], yx[w].at[i], ys_sem.at[w], yr_sem.at[w, far(i)], across
        )

    def y_send_last(i):
        return remote(
            yo.at[plane(ORDER[i]), 1 - xl, :, wa:], yxo.at[i], ys_sem.at[2], yr_sem.at[2, far(i)], across
        )

    def cross(w, *idx):
        for i in idx:
            y_send(w, i).start()
            if w == 1:
                y_send_last(i).start()

    crossed = set()

    def add_across(w, p, n):
        if (w, p, n) in crossed:
            return
        crossed.add((w, p, n))
        ids = CROSSED[n]
        came = yxo if p == 3 else yx[w]
        wait_for(yr_sem.at[2 if p == 3 else w, n], came.at[pl.ds(ids[0], len(ids))])
        for i in ids:
            pi = plane(ORDER[i])
            here = yo.at[pi, xl, :, pl.ds(wa, wo)] if p == 3 else y_b[w].at[pi, xl]
            here[...] = (here[...].astype(F32) + came[i].astype(F32)).astype(BF16)

    def back_block(u, side, j, p):
        w, rows = UNITS[u][0], rows_of(u, side, 5 - j)
        if p == 3:
            return back_o.at[side, j - 1]
        if p == 2:
            return back_b[w].at[side, j - 1, pl.ds(*rows)]
        if p == 4:
            return back_a[w].at[side, j - 1, :, pl.ds(*rows)]
        return back_a[w].at[side, j - 1, p, pl.ds(*rows)]

    def back_send(u, side, j, p):
        d = 1 - 2 * side
        w = UNITS[u][0]
        here = block(y_all, w, plane(d * (5 - j)), p, rows_of(u, side, 5 - j))
        return remote(here, back_block(u, side, j, p), sent(bs_sem, w, p), lane(br_sems, u, side, j, p), on_z(d))

    def ret(u, j, *ps):
        w = UNITS[u][0]
        for p in ps:
            for side in range(2):
                if not moves(u, side, 5 - j, p):
                    continue
                d = 1 - 2 * side
                if p in (2, 3):
                    add_across(w, p, 5 - j)
                if j > 1 and moves(u, side, 6 - j, p):
                    back_send(u, side, j - 1, p).wait_recv()
                    here = block(y_all, w, plane(d * (5 - j)), p, rows_of(u, side, 6 - j))
                    here[...] = (here[...].astype(F32) + back_block(u, side, j - 1, p)[...].astype(F32)).astype(BF16)
                back_send(u, side, j, p).start()

    def f_send(u):
        w, lo, n = UNITS[u][:3]
        return remote(
            final_a[w].at[1 - xl, pl.ds(lo, n)], fx[w].at[pl.ds(lo, n)], fs_sem.at[u], fr_sem.at[u], across
        )

    def f_send_last():
        return remote(final_o.at[:, :wa], fxo, fs_sem.at[3], fr_sem.at[3], across)

    def finish(u, *ps):
        w, lo, n = UNITS[u][:3]
        for p in ps:
            if p in (2, 3):
                add_across(w, p, 0)
            total = block(y_all, w, z, p, (lo, n))[...].astype(F32)
            for side in range(2):
                back_send(u, side, 4, p).wait_recv()
                total += back_block(u, side, 4, p)[...].astype(F32)
            total = total.astype(BF16)
            if p == 3:
                final_o[...] = total
                f_send_last().start()
            elif p == 2:
                final_b[w][lo:lo + n] = total
            else:
                if p == 4:
                    final_a[w][:, lo:lo + n] = total
                else:
                    final_a[w][p, lo:lo + n] = total
                if p:
                    f_send(u).start()

    def deliver(r, kind):
        parcel, result = ((parcel_a, result_a), (parcel_b, result_b), (parcel_x, result_x))[kind]
        return remote(
            parcel.at[r], result.at[col], ds_sem.at[kind], dr_sem.at[kind], in_column(column(r, 1))
        )

    def hand_out(u, kind):
        w, lo, n = UNITS[u][:3]
        if kind == 0:
            f_send(u).wait()
            mine = (final_a[w][xl, lo:lo + n].astype(F32) + fx[w][lo:lo + n].astype(F32)).astype(BF16)
        else:
            mine = final_b[w][lo:lo + n]
        if u == 0:
            ((result_a, result_b)[kind])[col] = mine
            return
        parcel = (parcel_a, parcel_b)[kind]
        first = 4 * w + lo // MAIN
        parcel[first:first + n // MAIN] = mine.reshape(n // MAIN, MAIN, mine.shape[1])
        for r in range(first, first + n // MAIN):
            deliver(r, kind).start()

    def hand_out_last():
        f_send_last().wait()
        both = final_o[:, :wa].astype(F32) + fxo[...].astype(F32)
        mine = jnp.where(xl == 0, both[:8], both[8:])
        over = final_o[:, wa:].astype(F32)
        mine = jnp.concatenate([mine, over[:8], over[8:, :wb - wo]], axis=1)
        mine = jnp.concatenate([mine, jnp.zeros_like(mine)], axis=0).astype(BF16)
        parcel_x[...] = fold(mine)[0].reshape(EXPERTS, MAIN, 128)
        for r in range(1, EXPERTS):
            deliver(r, 2).start()
        result_x[col] = parcel_x[0]

    for r in range(1, 4):
        phase_a(r).start()

    def start_rest():
        for cp in own_w + other_w:
            cp.start()
        for r in range(4, EXPERTS):
            phase_a(r).start()
        pack_last = jnp.transpose(last)[:16].astype(BF16)
        for t, tile in enumerate(fold(dot(pack_last, tok[...]).astype(BF16))):
            send_x[:, :, t * 128:(t + 1) * 128] = tile.reshape(EXPERTS, MAIN, 128)
        for r in range(1, EXPERTS):
            phase_a_last(r).start()

    z_step(0, 1)
    start_rest()
    z_step(0, 2)
    z_step(0, 3)
    land(0)
    z_step(1, 1)
    z_step(0, 4)
    z_step(0, 5)
    land(1)
    land_last()
    weights_wait(w_sem)
    weights_wait(wr_sem)
    z_step(1, 2)
    z_step(1, 3)
    gate_up(0, 0)
    z_step(1, 4)
    z_step(2, 1)
    hidden(0, 0)
    down(0, 0)
    z_step(1, 5)
    z_step(2, 2)
    gate_up(0, 1)
    hidden(0, 1)
    z_step(2, 3)
    down(0, 1)
    cross(0, 7, 5, 6)
    gate_up(1, 0)
    z_step(2, 4)
    hidden(1, 0)
    ret(1, 1, 0, 1)
    cross(0, 3, 4)
    z_step(2, 5)
    ret(1, 1, 2)
    ret(1, 2, 0, 1)
    gate_up(1, 1)
    ret(1, 2, 2)
    ret(1, 3, 0, 1)
    gate_up(1, 2)
    hidden(1, 1)
    cross(0, 1, 2)
    hidden(1, 2)
    down(1, 0)
    ret(1, 3, 2)
    ret(1, 4, 0, 1)
    down(1, 2)
    cross(1, 7)
    ret(2, 1, 0, 1)
    cross(0, 0)
    down(1, 1)
    cross(1, 5, 6)
    ret(1, 4, 2)
    ret(2, 2, 0, 1)
    ret(2, 1, 3, 2)
    finish(1, 0, 1)
    cross(1, 3, 4)
    ret(0, 1, 4)
    ret(2, 3, 0, 1)
    ret(2, 2, 3, 2)
    ret(0, 1, 2)
    ret(0, 2, 4)
    finish(1, 2)
    cross(1, 1, 2, 0)
    hand_out(1, 0)
    hand_out(1, 1)
    ret(2, 4, 0, 1)
    ret(2, 3, 3, 2)
    ret(0, 2, 2)
    ret(0, 3, 4)
    finish(2, 0, 1)
    ret(2, 4, 3, 2)
    ret(0, 3, 2)
    ret(0, 4, 4)
    hand_out(2, 0)
    finish(2, 3)
    finish(2, 2)
    hand_out(2, 1)
    ret(0, 4, 2)
    hand_out_last()
    finish(0, 4, 2)
    hand_out(0, 0)
    hand_out(0, 1)
    seven = pl.ds(0, 7)
    wait_for(as_sem.at[0], send.at[seven])
    wait_for(as_sem.at[1], send_x.at[seven])
    weights_wait(ws_sem)
    for w in range(2):
        wait_for(xs_sem.at[w], yx[w])
        wait_for(ys_sem.at[w], yx[w])
        wait_for(gs_sem.at[w], gu_out[w])
        wait_for(hs_sem.at[w], hid[w].at[0])
        for sem in (zs_sem, bs_sem):
            wait_for(sem.at[2 * w], x_a[w].at[seven])
            wait_for(sem.at[2 * w + 1], yx[w].at[seven])
    for sem in (zs_sem, bs_sem):
        wait_for(sem.at[4], xo.at[seven, 0])
    for sem in (xs_sem, ys_sem):
        wait_for(sem.at[2], yxo)
    gate_col = jnp.sum(jnp.where(rows_i == cols_i, gate_ref[...], 0.0), axis=1, keepdims=True)
    wait_for(dr_sem.at[2], result_x.at[seven])
    extra = unfold([result_x[...].reshape(EXPERTS * MAIN, 128)], (wa + wb) // 128)
    for kind, result, lo, hi in ((0, result_a, 0, wa), (1, result_b, wa, wa + wb)):
        wait_for(dr_sem.at[kind], result.at[seven])
        rows = dot(sel[0], result[...].reshape(EXPERTS * MAIN, hi - lo)) + dot(sel[1][:, :16], extra[:, lo:hi])
        out_ref[:, lo:hi] = (gate_col * rows).astype(BF16)
    for kind, parcel in enumerate((parcel_a, parcel_b, parcel_x)):
        wait_for(ds_sem.at[kind], parcel.at[seven])


def local(tokens, expert_ids, router_gate, w_gate, w_up, w_down):
    n_tok, dmodel = tokens.shape
    units = w_gate.shape[0]
    wa, wb, wo = widths_of(dmodel)
    share = 2 * wa + wb
    folded = -(-share // 2048) * 128
    vmem, dma = pltpu.VMEM, pltpu.SemaphoreType.DMA
    n_rows = [group_rows(w, len(GROUPS[w]))[0] for w in range(2)]

    def waves(*shape, dtype=BF16):
        return [vmem(shape, dtype)] * 2

    def per_row(*shape, dtype=F32):
        return [vmem((2, n, units), dtype) for n in n_rows]

    return pl.pallas_call(
        kernel,
        out_shape=jax.ShapeDtypeStruct((n_tok, wa + wb), BF16),
        in_specs=[pl.BlockSpec(memory_space=pl.ANY)] + [pl.BlockSpec(memory_space=pltpu.VMEM)] * 2
        + [pl.BlockSpec(memory_space=pl.ANY)] * 3,
        out_specs=pl.BlockSpec(memory_space=pltpu.VMEM),
        scratch_shapes=[
            vmem((n_tok, share), BF16),
            vmem((2, n_tok, EXPERTS * MAIN), BF16),
            vmem((EXPERTS, MAIN, share), BF16),
            vmem((EXPERTS, MAIN, folded), BF16),
            vmem((EXPERTS, MAIN, share), BF16),
            vmem((EXPERTS, MAIN, folded), BF16),
            vmem((2, 2, 2, units, wa), BF16),
            vmem((2, 2, 2, units, wb), BF16),
            vmem((2, 2, units, wa), BF16),
            vmem((2, 2, units, wb), BF16),
            vmem((EXPERTS, MAIN, wa), BF16),
            vmem((EXPERTS, MAIN, wb), BF16),
            vmem((EXPERTS, MAIN, 128), BF16),
            vmem((EXPERTS, MAIN, wa), BF16),
            vmem((EXPERTS, MAIN, wb), BF16),
            vmem((EXPERTS, MAIN, 128), BF16),
            vmem((RING, 2, 16, wa + wo), BF16),
            vmem((RING, 2, 16, wa + wo), BF16),
            vmem((RING, 16, wo), BF16),
            vmem((2, 4, 16, wa + wo), BF16),
            vmem((16, wa + wo), BF16),
            vmem((16, wa), BF16),
            *waves(RING, 2, N, wa),
            *waves(RING, 2, N, wb),
            *per_row(),
            *per_row(),
            *per_row(),
            *per_row(dtype=BF16),
            *waves(RING, 2, N, wa),
            *waves(RING, 2, N, wb),
            *waves(RING, N, wb),
            *waves(2, 4, 2, N, wa),
            *waves(2, 4, N, wb),
            *waves(2, N, wa),
            *waves(N, wb),
            *waves(N, wa),
            dma((3,)),
            dma((2, 2)), dma((2, 2)), dma((2, 2)),
            dma((2,)), dma((3,)),
            dma((5,)), [dma((2, 4, len(unit[3]))) for unit in UNITS],
            dma((3,)), dma((3, 3)),
            dma((2,)), dma((2, 3)),
            dma((2,)), dma((2, 3)),
            dma((3,)), dma((3, 5)),
            dma((5,)), [dma((2, 4, len(unit[3]))) for unit in UNITS],
            dma((4,)), dma((4,)),
            dma((3,)), dma((3,)),
        ],
        compiler_params=pltpu.CompilerParams(
            collective_id=0, has_side_effects=True, vmem_limit_bytes=60 * 2**20
        ),
        cost_estimate=pl.CostEstimate(flops=7 * 10**9, bytes_accessed=10**7, transcendentals=200000),
        name="routed_experts",
    )(tokens, expert_ids.reshape(1, n_tok), router_gate.reshape(1, n_tok), w_gate, w_up, w_down)


def solution(mesh):
    placed = (
        P("fsdp", None),
        P("fsdp", None),
        P("fsdp"),
        P(("fsdp", "ctx"), None),
        P(("fsdp", "ctx"), None),
        P(("fsdp", "ctx"), None),
    )
    return jax.shard_map(
        local, mesh=mesh, in_specs=placed, out_specs=P("fsdp", "ctx"), check_vma=False
    )
```

```python
import functools

import jax
import jax.numpy as jnp
from jax import lax
from jax.experimental import pallas as pl
from jax.experimental.pallas import tpu as pltpu
from jax.sharding import PartitionSpec as P

MESH = pl.DeviceIdType.MESH
EXPERTS = 8
MAIN = 16
RING = 8
N = 4 * MAIN
BF16, F32 = jnp.bfloat16, jnp.float32
SOURCES = ((0, 0), (0, 2), (1, 0), (1, 2), (0, 1), (0, 3), (1, 1), (1, 3))
UNITS = (
    (0, 0, 16, (2, 4), ((0, 16), (0, 16))),
    (0, 16, 48, (2, 0, 1), ((16, 16), (32, 32))),
    (1, 0, 64, (2, 3, 0, 1), ((0, 32), (32, 32))),
)
LAST_SPLIT = ((0, 32), (32, 32))
CROSSED = ((0,), (1, 2), (3, 4), (5, 6), (7,))
ORDER = (0, -1, 1, -2, 2, -3, 3, 4)
GROUPS = (((0, 5), (5, 8)), ((0, 5), (5, 7), (7, 8)))
B_BLOCKS = 6


def nt_dot(a, b):
    return lax.dot_general(a, b, (((1,), (1,)), ((), ())), preferred_element_type=F32)


def dot(a, b):
    return jnp.dot(a, b, preferred_element_type=F32)


def transposition(shape):
    r = lax.broadcasted_iota(jnp.int32, shape, 0)
    q = lax.broadcasted_iota(jnp.int32, shape, 1)
    return (((r >> 4) == (q & 15)) & ((r & 15) == (q >> 4))).astype(F32).astype(BF16)


def fold(rows):
    tiles = []
    for lo in range(0, rows.shape[1], 2048):
        part = rows[:, lo:lo + 2048]
        n = part.shape[1] // 128
        stack = jnp.concatenate([part[:, j * 128:(j + 1) * 128] for j in range(n)], axis=0)
        tiles.append(dot(transposition((128, n * 16)), stack).astype(BF16))
    return tiles


def unfold(tiles, n_blocks):
    blocks = []
    for t, tile in enumerate(tiles):
        n = min(16, n_blocks - 16 * t)
        stack = dot(transposition((n * 16, 128)), tile).astype(BF16)
        blocks += [stack[j * 16:(j + 1) * 16] for j in range(n)]
    return jnp.concatenate(blocks, axis=1)


def widths_of(dmodel):
    wb = B_BLOCKS * 128
    wa = dmodel // 4 - wb
    return wa, wb, -(-B_BLOCKS // 2) * 128


def group_rows(w, g):
    at = 0
    for h, (lo, hi) in enumerate(GROUPS[w]):
        main, extra = (hi - lo) * N, w * (-(-(hi - lo) // 2) * 16)
        if h == g:
            return at, main + extra, extra
        at += main + extra
    return at, 0, 0


def pair_up(left, right):
    if right.shape[1] < left.shape[1]:
        pad = jnp.zeros((8, left.shape[1] - right.shape[1]), F32)
        right = jnp.concatenate([right, pad], axis=1)
    return jnp.concatenate([left, right], axis=0)


def moves(u, side, k, p):
    if p not in UNITS[u][3]:
        return False
    if k < 4:
        return True
    if u == 0:
        return side == 0
    return p != 3 or side == 0


def rows_of(u, side, k):
    return UNITS[u][4][side] if k == 4 else UNITS[u][1:3]


def kernel(
    tok_ref, ids_ref, gate_ref, wg_ref, wu_ref, wd_ref,
    out_ref,
    tok, sel, send, send_x, staged, staged_x, wgu_a, wgu_b, wdn_a, wdn_b,
    parcel_a, parcel_b, parcel_x, result_a, result_b, result_x, xo, yo, yxo, back_o, final_o, fxo, *rest,
):
    per_wave, sems = rest[:28], rest[28:]
    (
        x_a, x_b, gu_own, gu_out, gu_in, hid, y_a, y_b, yx, back_a, back_b, final_a, final_b, fx,
    ) = [per_wave[2 * i:2 * i + 2] for i in range(14)]
    (
        t_sem, w_sem, ws_sem, wr_sem, as_sem, ar_sem, zs_sem, zr_sems, xs_sem, xr_sem,
        gs_sem, gr_sem, hs_sem, hr_sem, ys_sem, yr_sem, bs_sem, br_sems, fs_sem, fr_sem,
        ds_sem, dr_sem,
    ) = sems

    def wait_for(sem, ref):
        pltpu.make_async_copy(ref, ref, sem).wait()

    c, f = lax.axis_index("ctx"), lax.axis_index("fsdp")
    xl, co = c // 2, c % 2
    col, z = f // RING, f % RING
    wa, wb = x_a[0].shape[3], x_b[0].shape[3]
    wo = yxo.shape[2]
    share = 2 * wa + wb

    def on_z(d):
        return (c, col * RING + (z + d + RING) % RING)

    def column(r, sign):
        dx, dy = SOURCES[r]
        return (col // 4 + dx) % 2 * 4 + (col % 4 + sign * dy + 4) % 4

    def in_column(e):
        return (c, e * RING + z)

    sibling = (c + 1 - 2 * co, f)
    across = ((c + 2) % 4, f)

    def remote(src, dst, ssem, rsem, dev):
        return pltpu.make_async_remote_copy(
            src_ref=src, dst_ref=dst, send_sem=ssem, recv_sem=rsem, device_id=dev, device_id_type=MESH
        )

    def column_of(core, blk):
        quarter = (blk % 2) * 2 + core
        return pl.multiple_of(quarter * (wa + wb) + (wa if blk >= 2 else 0), 128)

    def columns(ref, core, blk):
        return ref.at[:, pl.ds(column_of(core, blk), wb if blk >= 2 else wa)]

    own_b = pl.multiple_of((xl * 2 + co) * (wa + wb) + wa, 128)
    share_refs = [columns(tok_ref, co, 0), columns(tok_ref, co, 1), tok_ref.at[:, pl.ds(own_b, wb)]]
    spans = ((0, wa), (wa, 2 * wa), (2 * wa, share))
    get_tok = [
        pltpu.make_async_copy(share_refs[p], tok.at[:, spans[p][0]:spans[p][1]], t_sem.at[p]) for p in range(3)
    ]
    for cp in get_tok:
        cp.start()

    barrier = pltpu.get_barrier_semaphore()
    partners = [on_z(1), on_z(-1), sibling, across] + [in_column((col + i) % EXPERTS) for i in range(1, EXPERTS)]
    for dev in partners:
        pl.semaphore_signal(barrier, inc=1, device_id=dev, device_id_type=MESH)

    def weight_slot(m, unit_core, blk):
        if m == 2:
            return (wdn_b if blk >= 2 else wdn_a).at[unit_core, blk % 2]
        return (wgu_b if blk >= 2 else wgu_a).at[m, unit_core, blk % 2]

    w_refs = (wg_ref, wu_ref, wd_ref)
    own_w = [
        pltpu.make_async_copy(columns(w_refs[m], co, blk), weight_slot(m, co, blk), w_sem.at[m // 2, blk // 2])
        for m in range(3) for blk in range(4)
    ]
    other_w = [
        remote(
            columns(w_refs[m], 1 - co, blk), weight_slot(m, co, blk),
            ws_sem.at[m // 2, blk // 2], wr_sem.at[m // 2, blk // 2], sibling,
        )
        for m in range(3) for blk in range(4)
    ]

    def weights_wait(sem):
        for m, arrays in ((0, (wgu_a.at[:, 0], wgu_b.at[:, 0])), (1, (wdn_a.at[0], wdn_b.at[0]))):
            for part in range(2):
                wait_for(sem.at[m, part], arrays[part])


    n_tok = tok.shape[0]
    rows_i = lax.broadcasted_iota(jnp.int32, (n_tok, n_tok), 0)
    cols_i = lax.broadcasted_iota(jnp.int32, (n_tok, n_tok), 1)
    ids_row = ids_ref[...]
    ids_col = jnp.sum(jnp.where(rows_i == cols_i, ids_row, 0), axis=1, keepdims=True)
    same = (ids_row == ids_col) & (cols_i < rows_i)
    rank = jnp.sum(same.astype(jnp.int32), axis=1, keepdims=True)
    main = ((cols_i == ids_col * MAIN + rank) & (rank < MAIN)).astype(F32)
    last = ((cols_i == ids_col) & (rank == MAIN)).astype(F32)
    sel[0] = main.astype(BF16)
    sel[1] = last.astype(BF16)
    pack = jnp.transpose(main).astype(BF16)
    for p in range(3):
        lo, hi = spans[p]
        get_tok[p].wait()
        send[:, :, lo:hi] = dot(pack, tok[:, lo:hi]).astype(BF16).reshape(EXPERTS, MAIN, hi - lo)

    for p in range(3):
        x_block = (x_b[0].at[z, xl] if p == 2 else x_a[0].at[z, p])
        x_block[:MAIN, :] = send[col, :, spans[p][0]:spans[p][1]]

    pl.semaphore_wait(barrier, len(partners))

    def phase_a(r):
        e = column(r, -1)
        return remote(send.at[e], staged.at[r], as_sem.at[0], ar_sem.at[r // 4], in_column(e))

    def phase_a_last(r):
        e = column(r, -1)
        return remote(send_x.at[e], staged_x.at[r], as_sem.at[1], ar_sem.at[2], in_column(e))

    def block(arrays, w, pi, p, rows):
        a, b, last = arrays
        if p == 3:
            return last.at[pi, xl]
        if p == 2:
            return b[w].at[pi, xl, pl.ds(*rows)]
        return a[w].at[pi, :, pl.ds(*rows)] if p == 4 else a[w].at[pi, p, pl.ds(*rows)]

    x_all, y_all = (x_a, x_b, xo), (y_a, y_b, yo)

    def land(w):
        first = 1 - w
        wait_for(ar_sem.at[w], staged.at[pl.ds(first, 4 - first)])
        for p in range(3):
            got = staged[4 * w + first:4 * w + 4, :, spans[p][0]:spans[p][1]]
            here = block(x_all, w, z, p, (first * MAIN, (4 - first) * MAIN))
            here[...] = got.reshape((4 - first) * MAIN, got.shape[2])

    def land_last():
        wait_for(ar_sem.at[2], staged_x.at[pl.ds(1, 7)])
        staged_x[0] = send_x[col]
        tiles = [
            staged_x[:, :, lo:lo + 128].reshape(EXPERTS * MAIN, 128) for lo in range(0, staged_x.shape[2], 128)
        ]
        extra = unfold(tiles, share // 128).astype(F32)[:8]
        xo[z, xl, :, :wa] = pair_up(extra[:, :wa], extra[:, wa:2 * wa]).astype(BF16)
        xo[z, xl, :, wa:] = pair_up(extra[:, 2 * wa:2 * wa + wo], extra[:, 2 * wa + wo:]).astype(BF16)

    def plane(d):
        return (z + d + RING) % RING

    def lane(sems_of, u, side, k, p):
        return sems_of[u].at[side, k - 1, UNITS[u][3].index(p)]

    def sent(sem, w, p):
        return sem.at[4 if p == 3 else 2 * w + int(p == 2)]

    def z_send(u, side, k, p):
        d = 1 - 2 * side
        w = UNITS[u][0]
        blk = block(x_all, w, plane(-d * (k - 1)), p, rows_of(u, side, k))
        return remote(blk, blk, sent(zs_sem, w, p), lane(zr_sems, u, side, k, p), on_z(d))

    def group_of(w, i):
        return [g for g, (lo, hi) in enumerate(GROUPS[w]) if lo <= i < hi][0]

    def x_send(w, i):
        if i < 7:
            blk = x_b[w].at[plane(ORDER[i]), xl]
        else:
            blk = x_b[w].at[plane(4), xl].at[pl.ds(*LAST_SPLIT[i - 7])]
        return remote(blk, blk, xs_sem.at[w], xr_sem.at[w, group_of(w, min(i, 7))], across)

    def x_send_last(i):
        blk = xo.at[plane(ORDER[i]), xl, :, wa:]
        return remote(blk, blk, xs_sem.at[2], xr_sem.at[2, group_of(1, i)], across)

    def z_task(u, side, k, p):
        if k > 1 and moves(u, side, k - 1, p):
            z_send(u, side, k - 1, p).wait_recv()
        if k < 5 and moves(u, side, k, p):
            z_send(u, side, k, p).start()

    def gu_send(w, g):
        lo, n, _ = group_rows(w, g)
        rows = pl.ds(lo, n)
        return remote(gu_out[w].at[:, rows], gu_in[w].at[:, rows], gs_sem.at[w], gr_sem.at[w, g], sibling)

    def hid_send(w, g):
        lo, n, _ = group_rows(w, g)
        mine = hid[w].at[co, pl.ds(lo, n)]
        return remote(mine, mine, hs_sem.at[w], hr_sem.at[w, g], sibling)

    def last_rows(pi, blk):
        if blk < 2:
            return xo[pi, xl, :, :wa].astype(F32)[8 * blk:8 * blk + 8]
        both = xo[pi, blk - 2, :, wa:].astype(F32)
        return jnp.concatenate([both[:8], both[8:, :wb - wo]], axis=1)

    def gate_up(w, g, blk):
        lo, n, extra = group_rows(w, g)
        ids = range(*GROUPS[w][g])
        if blk == 2:
            wait_for(xr_sem.at[w, g], yx[w].at[pl.ds(0, len(ids))])
            if w == 1:
                wait_for(xr_sem.at[2, g], yxo.at[pl.ds(0, len(ids))])
        xs, wgu = (x_b[w], wgu_b) if blk >= 2 else (x_a[w], wgu_a)
        parts = [xs[plane(ORDER[i]), blk % 2] for i in ids]
        if extra:
            lasts = [last_rows(plane(ORDER[i]), blk) for i in ids]
            if len(lasts) % 2:
                lasts.append(jnp.zeros_like(lasts[0]))
            parts.append(jnp.concatenate(lasts, axis=0).astype(BF16))
        rows = jnp.concatenate(parts, axis=0)
        for m in range(2):
            for acc, u in ((gu_own[w], co), (gu_out[w], 1 - co)):
                term = nt_dot(rows, wgu[m, u, blk % 2])
                acc[m, lo:lo + n] = acc[m, lo:lo + n] + term if blk else term
        if blk == 3:
            gu_send(w, g).start()

    def hidden(w, g):
        lo, n, _ = group_rows(w, g)
        gu_send(w, g).wait_recv()
        gate = gu_own[w][0, lo:lo + n] + gu_in[w][0, lo:lo + n]
        up = gu_own[w][1, lo:lo + n] + gu_in[w][1, lo:lo + n]
        hid[w][co, lo:lo + n] = (gate / (1.0 + jnp.exp(-gate)) * up).astype(BF16)
        hid_send(w, g).start()

    def down(w, g, kind):
        lo, n, extra = group_rows(w, g)
        ids = range(*GROUPS[w][g])
        if kind == "b":
            hid_send(w, g).wait_recv()
        lasts = {}
        for blk in ((2, 3) if kind == "b" else (0, 1)):
            wdn, ys = (wdn_b, y_b[w]) if blk >= 2 else (wdn_a, y_a[w])
            part = dot(hid[w][0, lo:lo + n], wdn[0, blk % 2]) + dot(hid[w][1, lo:lo + n], wdn[1, blk % 2])
            for at, i in enumerate(ids):
                ys[plane(ORDER[i]), blk % 2] = part[at * N:(at + 1) * N].astype(BF16)
                if extra:
                    at8 = len(ids) * N + 8 * at
                    mine = part[at8:at8 + 8]
                    if blk >= 2:
                        yo[plane(ORDER[i]), blk - 2, :, wa:] = pair_up(mine[:, :wo], mine[:, wo:]).astype(BF16)
                    elif blk == 0:
                        lasts[i] = mine
                    else:
                        yo[plane(ORDER[i]), xl, :, :wa] = pair_up(lasts[i], mine).astype(BF16)

    def far(i):
        return [n for n, ids in enumerate(CROSSED) if i in ids][0]

    def y_send(w, i):
        return remote(
            y_b[w].at[plane(ORDER[i]), 1 - xl], yx[w].at[i], ys_sem.at[w], yr_sem.at[w, far(i)], across
        )

    def y_send_last(i):
        return remote(
            yo.at[plane(ORDER[i]), 1 - xl, :, wa:], yxo.at[i], ys_sem.at[2], yr_sem.at[2, far(i)], across
        )

    def cross(w, *idx):
        for i in idx:
            y_send(w, i).start()
            if w == 1:
                y_send_last(i).start()

    crossed = set()

    def add_across(w, p, n):
        if (w, p, n) in crossed:
            return
        crossed.add((w, p, n))
        ids = CROSSED[n]
        came = yxo if p == 3 else yx[w]
        wait_for(yr_sem.at[2 if p == 3 else w, n], came.at[pl.ds(ids[0], len(ids))])
        for i in ids:
            pi = plane(ORDER[i])
            here = yo.at[pi, xl, :, pl.ds(wa, wo)] if p == 3 else y_b[w].at[pi, xl]
            here[...] = (here[...].astype(F32) + came[i].astype(F32)).astype(BF16)

    def back_block(u, side, j, p):
        w, rows = UNITS[u][0], rows_of(u, side, 5 - j)
        if p == 3:
            return back_o.at[side, j - 1]
        if p == 2:
            return back_b[w].at[side, j - 1, pl.ds(*rows)]
        if p == 4:
            return back_a[w].at[side, j - 1, :, pl.ds(*rows)]
        return back_a[w].at[side, j - 1, p, pl.ds(*rows)]

    def back_send(u, side, j, p):
        d = 1 - 2 * side
        w = UNITS[u][0]
        here = block(y_all, w, plane(d * (5 - j)), p, rows_of(u, side, 5 - j))
        return remote(here, back_block(u, side, j, p), sent(bs_sem, w, p), lane(br_sems, u, side, j, p), on_z(d))

    def ret_task(u, side, j, p):
        w, d = UNITS[u][0], 1 - 2 * side
        if p in (2, 3):
            add_across(w, p, 5 - j)
        if j > 1 and moves(u, side, 6 - j, p):
            back_send(u, side, j - 1, p).wait_recv()
            here = block(y_all, w, plane(d * (5 - j)), p, rows_of(u, side, 6 - j))
            here[...] = (here[...].astype(F32) + back_block(u, side, j - 1, p)[...].astype(F32)).astype(BF16)
        back_send(u, side, j, p).start()

    def f_send(u):
        w, lo, n = UNITS[u][:3]
        return remote(
            final_a[w].at[1 - xl, pl.ds(lo, n)], fx[w].at[pl.ds(lo, n)], fs_sem.at[u], fr_sem.at[u], across
        )

    def f_send_last():
        return remote(final_o.at[:, :wa], fxo, fs_sem.at[3], fr_sem.at[3], across)

    def finish(u, *ps):
        w, lo, n = UNITS[u][:3]
        for p in ps:
            if p in (2, 3):
                add_across(w, p, 0)
            total = block(y_all, w, z, p, (lo, n))[...].astype(F32)
            for side in range(2):
                back_send(u, side, 4, p).wait_recv()
                total += back_block(u, side, 4, p)[...].astype(F32)
            total = total.astype(BF16)
            if p == 3:
                final_o[...] = total
                f_send_last().start()
            elif p == 2:
                final_b[w][lo:lo + n] = total
            else:
                if p == 4:
                    final_a[w][:, lo:lo + n] = total
                else:
                    final_a[w][p, lo:lo + n] = total
                if p:
                    f_send(u).start()

    def deliver(r, kind):
        parcel, result = ((parcel_a, result_a), (parcel_b, result_b), (parcel_x, result_x))[kind]
        return remote(
            parcel.at[r], result.at[col], ds_sem.at[kind], dr_sem.at[kind], in_column(column(r, 1))
        )

    def hand_out(u, kind):
        w, lo, n = UNITS[u][:3]
        if kind == 0:
            f_send(u).wait()
            mine = (final_a[w][xl, lo:lo + n].astype(F32) + fx[w][lo:lo + n].astype(F32)).astype(BF16)
        else:
            mine = final_b[w][lo:lo + n]
        if u == 0:
            ((result_a, result_b)[kind])[col] = mine
            return
        parcel = (parcel_a, parcel_b)[kind]
        first = 4 * w + lo // MAIN
        parcel[first:first + n // MAIN] = mine.reshape(n // MAIN, MAIN, mine.shape[1])
        for r in range(first, first + n // MAIN):
            deliver(r, kind).start()

    def hand_out_last():
        f_send_last().wait()
        both = final_o[:, :wa].astype(F32) + fxo[...].astype(F32)
        mine = jnp.where(xl == 0, both[:8], both[8:])
        over = final_o[:, wa:].astype(F32)
        mine = jnp.concatenate([mine, over[:8], over[8:, :wb - wo]], axis=1)
        mine = jnp.concatenate([mine, jnp.zeros_like(mine)], axis=0).astype(BF16)
        parcel_x[...] = fold(mine)[0].reshape(EXPERTS, MAIN, 128)
        for r in range(1, EXPERTS):
            deliver(r, 2).start()
        result_x[col] = parcel_x[0]

    for r in range(1, 4):
        phase_a(r).start()

    def start_rest():
        for cp in own_w + other_w:
            cp.start()
        for r in range(4, EXPERTS):
            phase_a(r).start()
        pack_last = jnp.transpose(last)[:16].astype(BF16)
        for t, tile in enumerate(fold(dot(pack_last, tok[...]).astype(BF16))):
            send_x[:, :, t * 128:(t + 1) * 128] = tile.reshape(EXPERTS, MAIN, 128)
        for r in range(1, EXPERTS):
            phase_a_last(r).start()

    z_task(0, 0, 1, 2)
    z_task(0, 1, 1, 2)
    z_task(0, 1, 1, 4)
    z_task(0, 0, 1, 4)
    start_rest()
    z_task(0, 0, 2, 2)
    z_task(0, 1, 2, 2)
    z_task(0, 0, 2, 4)
    z_task(0, 1, 2, 4)
    z_task(0, 0, 3, 2)
    z_task(0, 1, 3, 2)
    z_task(0, 0, 3, 4)
    z_task(0, 1, 3, 4)
    z_task(0, 0, 4, 2)
    z_task(0, 1, 4, 2)
    land(0)
    z_task(1, 0, 1, 2)
    z_task(1, 1, 1, 2)
    x_send(0, 0).start()
    z_task(1, 1, 1, 0)
    z_task(1, 0, 1, 0)
    z_task(1, 0, 1, 1)
    z_task(0, 0, 4, 4)
    z_task(1, 1, 1, 1)
    z_task(0, 1, 4, 4)
    z_task(0, 0, 5, 2)
    land(1)
    land_last()
    weights_wait(w_sem)
    weights_wait(wr_sem)
    z_task(1, 0, 2, 2)
    x_send(0, 1).start()
    z_task(1, 1, 2, 2)
    x_send(0, 2).start()
    z_task(1, 0, 2, 0)
    z_task(1, 1, 2, 0)
    z_task(1, 0, 2, 1)
    z_task(1, 1, 2, 1)
    z_task(0, 0, 5, 4)
    z_task(1, 1, 3, 2)
    x_send(0, 4).start()
    z_task(1, 0, 3, 2)
    x_send(0, 3).start()
    z_task(1, 1, 3, 0)
    z_task(1, 0, 3, 0)
    z_task(1, 1, 3, 1)
    z_task(1, 0, 3, 1)
    gate_up(0, 0, 0)
    z_task(1, 1, 4, 2)
    x_send(0, 6).start()
    z_task(2, 1, 1, 2)
    z_task(2, 1, 1, 3)
    gate_up(0, 0, 1)
    z_task(1, 1, 4, 0)
    z_task(2, 1, 1, 0)
    z_task(1, 0, 4, 2)
    x_send(0, 5).start()
    z_task(2, 0, 1, 2)
    x_send(1, 0).start()
    z_task(2, 0, 1, 3)
    x_send_last(0).start()
    z_task(1, 0, 4, 0)
    z_task(2, 0, 1, 0)
    gate_up(0, 0, 2)
    z_task(1, 1, 4, 1)
    z_task(2, 1, 1, 1)
    z_task(1, 0, 4, 1)
    z_task(2, 0, 1, 1)
    z_task(1, 1, 5, 2)
    x_send(0, 8).start()
    gate_up(0, 0, 3)
    z_task(1, 0, 5, 2)
    x_send(0, 7).start()
    z_task(2, 1, 2, 2)
    x_send(1, 2).start()
    z_task(2, 0, 2, 2)
    x_send(1, 1).start()
    z_task(2, 1, 2, 3)
    x_send_last(2).start()
    z_task(2, 0, 2, 3)
    x_send_last(1).start()
    hidden(0, 0)
    z_task(1, 1, 5, 0)
    z_task(1, 0, 5, 0)
    z_task(2, 0, 2, 0)
    z_task(2, 1, 2, 0)
    down(0, 0, 'b')
    z_task(1, 0, 5, 1)
    z_task(1, 1, 5, 1)
    gate_up(0, 1, 0)
    down(0, 0, 'a')
    z_task(2, 0, 2, 1)
    gate_up(0, 1, 1)
    z_task(2, 1, 2, 1)
    cross(0, 4)
    cross(0, 3)
    gate_up(0, 1, 2)
    gate_up(0, 1, 3)
    z_task(2, 1, 3, 2)
    x_send(1, 4).start()
    z_task(2, 0, 3, 3)
    x_send_last(3).start()
    z_task(2, 0, 3, 2)
    x_send(1, 3).start()
    z_task(2, 1, 3, 3)
    x_send_last(4).start()
    cross(0, 1)
    cross(0, 2)
    cross(0, 0)
    z_task(2, 0, 3, 0)
    hidden(0, 1)
    z_task(2, 1, 3, 0)
    z_task(2, 0, 3, 1)
    down(0, 1, 'b')
    z_task(2, 0, 4, 3)
    x_send_last(5).start()
    z_task(2, 1, 3, 1)
    gate_up(1, 0, 0)
    gate_up(1, 0, 1)
    z_task(2, 1, 4, 2)
    z_task(2, 0, 4, 2)
    x_send(1, 5).start()
    x_send(1, 6).start()
    down(0, 1, 'a')
    ret_task(1, 1, 1, 0)
    z_task(2, 1, 4, 3)
    x_send_last(6).start()
    ret_task(1, 0, 1, 1)
    ret_task(1, 0, 1, 0)
    gate_up(1, 0, 2)
    gate_up(1, 0, 3)
    z_task(2, 0, 4, 1)
    ret_task(1, 1, 1, 1)
    ret_task(0, 0, 1, 4)
    z_task(2, 1, 4, 1)
    z_task(2, 0, 5, 3)
    x_send_last(7).start()
    z_task(2, 0, 4, 0)
    ret_task(0, 1, 2, 4)
    z_task(2, 1, 4, 0)
    gate_up(1, 1, 0)
    gate_up(1, 1, 1)
    hidden(1, 0)
    ret_task(1, 1, 2, 0)
    ret_task(1, 0, 2, 0)
    z_task(2, 0, 5, 1)
    ret_task(1, 0, 2, 1)
    z_task(2, 1, 5, 2)
    x_send(1, 8).start()
    z_task(2, 0, 5, 2)
    x_send(1, 7).start()
    ret_task(1, 1, 2, 1)
    ret_task(0, 0, 2, 4)
    down(1, 0, 'b')
    down(1, 0, 'a')
    ret_task(0, 1, 3, 4)
    z_task(2, 0, 5, 0)
    z_task(2, 1, 5, 0)
    z_task(2, 1, 5, 1)
    gate_up(1, 2, 0)
    ret_task(1, 0, 3, 0)
    gate_up(1, 2, 1)
    ret_task(1, 1, 3, 0)
    gate_up(1, 1, 2)
    ret_task(1, 0, 3, 1)
    gate_up(1, 1, 3)
    ret_task(1, 1, 3, 1)
    ret_task(0, 0, 3, 4)
    ret_task(0, 1, 4, 4)
    gate_up(1, 2, 2)
    gate_up(1, 2, 3)
    ret_task(1, 0, 4, 0)
    hidden(1, 1)
    ret_task(1, 1, 4, 0)
    ret_task(1, 0, 4, 1)
    cross(0, 7)
    cross(0, 6)
    hidden(1, 2)
    ret_task(0, 0, 4, 4)
    ret_task(1, 1, 4, 1)
    down(1, 1, 'b')
    down(1, 1, 'a')
    down(1, 2, 'b')
    down(1, 2, 'a')
    ret_task(2, 0, 1, 1)
    ret_task(2, 1, 1, 0)
    ret_task(1, 0, 1, 2)
    ret_task(2, 0, 1, 0)
    ret_task(0, 0, 1, 2)
    finish(0, 4)
    ret_task(2, 1, 1, 1)
    finish(1, 0)
    finish(1, 1)
    ret_task(1, 1, 1, 2)
    ret_task(2, 0, 2, 1)
    ret_task(2, 1, 2, 0)
    cross(1, 7)
    hand_out(0, 0)
    cross(1, 5)
    ret_task(2, 0, 2, 0)
    ret_task(2, 1, 2, 1)
    cross(1, 6)
    cross(1, 3)
    cross(1, 4)
    cross(0, 5)
    hand_out(1, 0)
    cross(1, 1)
    cross(1, 2)
    cross(1, 0)
    ret_task(2, 0, 3, 1)
    ret_task(2, 1, 3, 0)
    ret_task(2, 0, 1, 3)
    ret_task(2, 0, 1, 2)
    ret_task(2, 1, 1, 2)
    ret_task(2, 0, 3, 0)
    ret_task(2, 1, 3, 1)
    ret_task(2, 0, 4, 1)
    ret_task(2, 1, 4, 0)
    ret_task(2, 0, 2, 3)
    ret_task(2, 1, 2, 3)
    ret_task(2, 1, 2, 2)
    ret_task(2, 0, 2, 2)
    ret_task(2, 1, 4, 1)
    ret_task(2, 0, 4, 0)
    ret_task(2, 1, 3, 3)
    ret_task(2, 0, 3, 3)
    ret_task(1, 1, 2, 2)
    ret_task(1, 0, 2, 2)
    ret_task(2, 0, 3, 2)
    ret_task(0, 0, 2, 2)
    ret_task(2, 1, 3, 2)
    ret_task(0, 1, 2, 2)
    finish(2, 0)
    finish(2, 1)
    ret_task(2, 1, 4, 3)
    ret_task(2, 0, 4, 3)
    ret_task(1, 0, 3, 2)
    ret_task(1, 1, 3, 2)
    ret_task(2, 1, 4, 2)
    ret_task(2, 0, 4, 2)
    ret_task(0, 1, 3, 2)
    ret_task(0, 0, 3, 2)
    finish(2, 3)
    hand_out(2, 0)
    ret_task(1, 1, 4, 2)
    ret_task(1, 0, 4, 2)
    hand_out_last()
    finish(2, 2)
    hand_out(2, 1)
    ret_task(0, 0, 4, 2)
    ret_task(0, 1, 4, 2)
    finish(1, 2)
    hand_out(1, 1)
    finish(0, 2)
    hand_out(0, 1)

    seven = pl.ds(0, 7)
    wait_for(as_sem.at[0], send.at[seven])
    wait_for(as_sem.at[1], send_x.at[seven])
    weights_wait(ws_sem)
    for w in range(2):
        wait_for(xs_sem.at[w], yx[w])
        wait_for(ys_sem.at[w], yx[w])
        wait_for(gs_sem.at[w], gu_out[w])
        wait_for(hs_sem.at[w], hid[w].at[0])
        for sem in (zs_sem, bs_sem):
            wait_for(sem.at[2 * w], x_a[w].at[seven])
            wait_for(sem.at[2 * w + 1], yx[w].at[seven])
    for sem in (zs_sem, bs_sem):
        wait_for(sem.at[4], xo.at[seven, 0])
    for sem in (xs_sem, ys_sem):
        wait_for(sem.at[2], yxo)
    gate_col = jnp.sum(jnp.where(rows_i == cols_i, gate_ref[...], 0.0), axis=1, keepdims=True)
    wait_for(dr_sem.at[2], result_x.at[seven])
    extra = unfold([result_x[...].reshape(EXPERTS * MAIN, 128)], (wa + wb) // 128)
    for kind, result, lo, hi in ((0, result_a, 0, wa), (1, result_b, wa, wa + wb)):
        wait_for(dr_sem.at[kind], result.at[seven])
        rows = dot(sel[0], result[...].reshape(EXPERTS * MAIN, hi - lo)) + dot(sel[1][:, :16], extra[:, lo:hi])
        out_ref[:, lo:hi] = (gate_col * rows).astype(BF16)
    for kind, parcel in enumerate((parcel_a, parcel_b, parcel_x)):
        wait_for(ds_sem.at[kind], parcel.at[seven])


def local(tokens, expert_ids, router_gate, w_gate, w_up, w_down):
    n_tok, dmodel = tokens.shape
    units = w_gate.shape[0]
    wa, wb, wo = widths_of(dmodel)
    share = 2 * wa + wb
    folded = -(-share // 2048) * 128
    vmem, dma = pltpu.VMEM, pltpu.SemaphoreType.DMA
    n_rows = [group_rows(w, len(GROUPS[w]))[0] for w in range(2)]

    def waves(*shape, dtype=BF16):
        return [vmem(shape, dtype)] * 2

    def per_row(*shape, dtype=F32):
        return [vmem((2, n, units), dtype) for n in n_rows]

    return pl.pallas_call(
        kernel,
        out_shape=jax.ShapeDtypeStruct((n_tok, wa + wb), BF16),
        in_specs=[pl.BlockSpec(memory_space=pl.ANY)] + [pl.BlockSpec(memory_space=pltpu.VMEM)] * 2
        + [pl.BlockSpec(memory_space=pl.ANY)] * 3,
        out_specs=pl.BlockSpec(memory_space=pltpu.VMEM),
        scratch_shapes=[
            vmem((n_tok, share), BF16),
            vmem((2, n_tok, EXPERTS * MAIN), BF16),
            vmem((EXPERTS, MAIN, share), BF16),
            vmem((EXPERTS, MAIN, folded), BF16),
            vmem((EXPERTS, MAIN, share), BF16),
            vmem((EXPERTS, MAIN, folded), BF16),
            vmem((2, 2, 2, units, wa), BF16),
            vmem((2, 2, 2, units, wb), BF16),
            vmem((2, 2, units, wa), BF16),
            vmem((2, 2, units, wb), BF16),
            vmem((EXPERTS, MAIN, wa), BF16),
            vmem((EXPERTS, MAIN, wb), BF16),
            vmem((EXPERTS, MAIN, 128), BF16),
            vmem((EXPERTS, MAIN, wa), BF16),
            vmem((EXPERTS, MAIN, wb), BF16),
            vmem((EXPERTS, MAIN, 128), BF16),
            vmem((RING, 2, 16, wa + wo), BF16),
            vmem((RING, 2, 16, wa + wo), BF16),
            vmem((RING, 16, wo), BF16),
            vmem((2, 4, 16, wa + wo), BF16),
            vmem((16, wa + wo), BF16),
            vmem((16, wa), BF16),
            *waves(RING, 2, N, wa),
            *waves(RING, 2, N, wb),
            *per_row(),
            *per_row(),
            *per_row(),
            *per_row(dtype=BF16),
            *waves(RING, 2, N, wa),
            *waves(RING, 2, N, wb),
            *waves(RING, N, wb),
            *waves(2, 4, 2, N, wa),
            *waves(2, 4, N, wb),
            *waves(2, N, wa),
            *waves(N, wb),
            *waves(N, wa),
            dma((3,)),
            dma((2, 2)), dma((2, 2)), dma((2, 2)),
            dma((2,)), dma((3,)),
            dma((5,)), [dma((2, 4, len(unit[3]))) for unit in UNITS],
            dma((3,)), dma((3, 3)),
            dma((2,)), dma((2, 3)),
            dma((2,)), dma((2, 3)),
            dma((3,)), dma((3, 5)),
            dma((5,)), [dma((2, 4, len(unit[3]))) for unit in UNITS],
            dma((4,)), dma((4,)),
            dma((3,)), dma((3,)),
        ],
        compiler_params=pltpu.CompilerParams(
            collective_id=0, has_side_effects=True, vmem_limit_bytes=60 * 2**20
        ),
        cost_estimate=pl.CostEstimate(flops=7 * 10**9, bytes_accessed=10**7, transcendentals=200000),
        name="routed_experts",
    )(tokens, expert_ids.reshape(1, n_tok), router_gate.reshape(1, n_tok), w_gate, w_up, w_down)


def solution(mesh):
    placed = (
        P("fsdp", None),
        P("fsdp", None),
        P("fsdp"),
        P(("fsdp", "ctx"), None),
        P(("fsdp", "ctx"), None),
        P(("fsdp", "ctx"), None),
    )
    return jax.shard_map(
        local, mesh=mesh, in_specs=placed, out_specs=P("fsdp", "ctx"), check_vma=False
    )
```

```python
import functools

import jax
import jax.numpy as jnp
from jax import lax
from jax.experimental import pallas as pl
from jax.experimental.pallas import tpu as pltpu
from jax.sharding import PartitionSpec as P

MESH = pl.DeviceIdType.MESH
EXPERTS = 8
MAIN = 16
RING = 8
N = 4 * MAIN
BF16, F32 = jnp.bfloat16, jnp.float32
SOURCES = ((0, 0), (0, 2), (1, 0), (1, 2), (0, 1), (0, 3), (1, 1), (1, 3))
UNITS = (
    (0, 0, 16, (2, 4), ((0, 16), (0, 16))),
    (0, 16, 48, (2, 0, 1), ((16, 16), (32, 32))),
    (1, 0, 64, (2, 3, 0, 1), ((0, 32), (32, 32))),
)
LAST_SPLIT = ((0, 32), (32, 32))
CROSSED = ((0,), (1, 2), (3, 4), (5, 6), (7,))
ORDER = (0, -1, 1, -2, 2, -3, 3, 4)
GROUPS = (((0, 5), (5, 8)), ((0, 5), (5, 7), (7, 8)))
B_BLOCKS = 6


def nt_dot(a, b):
    return lax.dot_general(a, b, (((1,), (1,)), ((), ())), preferred_element_type=F32)


def dot(a, b):
    return jnp.dot(a, b, preferred_element_type=F32)


def transposition(shape):
    r = lax.broadcasted_iota(jnp.int32, shape, 0)
    q = lax.broadcasted_iota(jnp.int32, shape, 1)
    return (((r >> 4) == (q & 15)) & ((r & 15) == (q >> 4))).astype(F32).astype(BF16)


def fold(rows):
    tiles = []
    for lo in range(0, rows.shape[1], 2048):
        part = rows[:, lo:lo + 2048]
        n = part.shape[1] // 128
        stack = jnp.concatenate([part[:, j * 128:(j + 1) * 128] for j in range(n)], axis=0)
        tiles.append(dot(transposition((128, n * 16)), stack).astype(BF16))
    return tiles


def unfold(tiles, n_blocks):
    blocks = []
    for t, tile in enumerate(tiles):
        n = min(16, n_blocks - 16 * t)
        stack = dot(transposition((n * 16, 128)), tile).astype(BF16)
        blocks += [stack[j * 16:(j + 1) * 16] for j in range(n)]
    return jnp.concatenate(blocks, axis=1)


def widths_of(dmodel):
    wb = B_BLOCKS * 128
    wa = dmodel // 4 - wb
    return wa, wb, -(-B_BLOCKS // 2) * 128


def group_rows(w, g):
    at = 0
    for h, (lo, hi) in enumerate(GROUPS[w]):
        main, extra = (hi - lo) * N, w * (-(-(hi - lo) // 2) * 16)
        if h == g:
            return at, main + extra, extra
        at += main + extra
    return at, 0, 0


def pair_up(left, right):
    if right.shape[1] < left.shape[1]:
        pad = jnp.zeros((8, left.shape[1] - right.shape[1]), F32)
        right = jnp.concatenate([right, pad], axis=1)
    return jnp.concatenate([left, right], axis=0)


def moves(u, side, k, p):
    if p not in UNITS[u][3]:
        return False
    if k < 4:
        return True
    if u == 0:
        return side == 0
    return p != 3 or side == 0


def rows_of(u, side, k):
    return UNITS[u][4][side] if k == 4 else UNITS[u][1:3]


def kernel(
    tok_ref, ids_ref, gate_ref, wg_ref, wu_ref, wd_ref,
    out_ref,
    tok, sel, send, send_x, staged, staged_x, wgu_a, wgu_b, wdn_a, wdn_b,
    parcel_a, parcel_b, parcel_x, result_a, result_b, result_x, xo, yo, yxo, back_o, final_o, fxo, *rest,
):
    per_wave, sems = rest[:28], rest[28:]
    (
        x_a, x_b, gu_own, gu_out, gu_in, hid, y_a, y_b, yx, back_a, back_b, final_a, final_b, fx,
    ) = [per_wave[2 * i:2 * i + 2] for i in range(14)]
    (
        t_sem, w_sem, ws_sem, wr_sem, as_sem, ar_sem, zs_sem, zr_sems, xs_sem, xr_sem,
        gs_sem, gr_sem, hs_sem, hr_sem, ys_sem, yr_sem, bs_sem, br_sems, fs_sem, fr_sem,
        ds_sem, dr_sem,
    ) = sems

    def wait_for(sem, ref):
        pltpu.make_async_copy(ref, ref, sem).wait()

    c, f = lax.axis_index("ctx"), lax.axis_index("fsdp")
    xl, co = c // 2, c % 2
    col, z = f // RING, f % RING
    wa, wb = x_a[0].shape[3], x_b[0].shape[3]
    wo = yxo.shape[2]
    share = 2 * wa + wb

    def on_z(d):
        return (c, col * RING + (z + d + RING) % RING)

    def column(r, sign):
        dx, dy = SOURCES[r]
        return (col // 4 + dx) % 2 * 4 + (col % 4 + sign * dy + 4) % 4

    def in_column(e):
        return (c, e * RING + z)

    sibling = (c + 1 - 2 * co, f)
    across = ((c + 2) % 4, f)

    def remote(src, dst, ssem, rsem, dev):
        return pltpu.make_async_remote_copy(
            src_ref=src, dst_ref=dst, send_sem=ssem, recv_sem=rsem, device_id=dev, device_id_type=MESH
        )

    def column_of(core, blk):
        quarter = (blk % 2) * 2 + core
        return pl.multiple_of(quarter * (wa + wb) + (wa if blk >= 2 else 0), 128)

    def columns(ref, core, blk):
        return ref.at[:, pl.ds(column_of(core, blk), wb if blk >= 2 else wa)]

    own_b = pl.multiple_of((xl * 2 + co) * (wa + wb) + wa, 128)
    share_refs = [columns(tok_ref, co, 0), columns(tok_ref, co, 1), tok_ref.at[:, pl.ds(own_b, wb)]]
    spans = ((0, wa), (wa, 2 * wa), (2 * wa, share))
    get_tok = [
        pltpu.make_async_copy(share_refs[p], tok.at[:, spans[p][0]:spans[p][1]], t_sem.at[p]) for p in range(3)
    ]
    for cp in get_tok:
        cp.start()

    barrier = pltpu.get_barrier_semaphore()
    partners = [on_z(1), on_z(-1), sibling, across] + [in_column((col + i) % EXPERTS) for i in range(1, EXPERTS)]
    for dev in partners:
        pl.semaphore_signal(barrier, inc=1, device_id=dev, device_id_type=MESH)

    def weight_slot(m, unit_core, blk):
        if m == 2:
            return (wdn_b if blk >= 2 else wdn_a).at[unit_core, blk % 2]
        return (wgu_b if blk >= 2 else wgu_a).at[m, unit_core, blk % 2]

    w_refs = (wg_ref, wu_ref, wd_ref)
    own_w = [
        pltpu.make_async_copy(columns(w_refs[m], co, blk), weight_slot(m, co, blk), w_sem.at[m // 2, blk // 2])
        for m in range(3) for blk in range(4)
    ]
    other_w = [
        remote(
            columns(w_refs[m], 1 - co, blk), weight_slot(m, co, blk),
            ws_sem.at[m // 2, blk // 2], wr_sem.at[m // 2, blk // 2], sibling,
        )
        for m in range(3) for blk in range(4)
    ]

    def weights_wait(sem):
        for m, arrays in ((0, (wgu_a.at[:, 0], wgu_b.at[:, 0])), (1, (wdn_a.at[0], wdn_b.at[0]))):
            for part in range(2):
                wait_for(sem.at[m, part], arrays[part])


    n_tok = tok.shape[0]
    rows_i = lax.broadcasted_iota(jnp.int32, (n_tok, n_tok), 0)
    cols_i = lax.broadcasted_iota(jnp.int32, (n_tok, n_tok), 1)
    ids_row = ids_ref[...]
    ids_col = jnp.sum(jnp.where(rows_i == cols_i, ids_row, 0), axis=1, keepdims=True)
    same = (ids_row == ids_col) & (cols_i < rows_i)
    rank = jnp.sum(same.astype(jnp.int32), axis=1, keepdims=True)
    main = ((cols_i == ids_col * MAIN + rank) & (rank < MAIN)).astype(F32)
    last = ((cols_i == ids_col) & (rank == MAIN)).astype(F32)
    sel[0] = main.astype(BF16)
    sel[1] = last.astype(BF16)
    pack = jnp.transpose(main).astype(BF16)
    for p in range(3):
        lo, hi = spans[p]
        get_tok[p].wait()
        send[:, :, lo:hi] = dot(pack, tok[:, lo:hi]).astype(BF16).reshape(EXPERTS, MAIN, hi - lo)

    for p in range(3):
        x_block = (x_b[0].at[z, xl] if p == 2 else x_a[0].at[z, p])
        x_block[:MAIN, :] = send[col, :, spans[p][0]:spans[p][1]]

    pl.semaphore_wait(barrier, len(partners))

    def phase_a(r):
        e = column(r, -1)
        return remote(send.at[e], staged.at[r], as_sem.at[0], ar_sem.at[r // 4], in_column(e))

    def phase_a_last(r):
        e = column(r, -1)
        return remote(send_x.at[e], staged_x.at[r], as_sem.at[1], ar_sem.at[2], in_column(e))

    def block(arrays, w, pi, p, rows):
        a, b, last = arrays
        if p == 3:
            return last.at[pi, xl]
        if p == 2:
            return b[w].at[pi, xl, pl.ds(*rows)]
        return a[w].at[pi, :, pl.ds(*rows)] if p == 4 else a[w].at[pi, p, pl.ds(*rows)]

    x_all, y_all = (x_a, x_b, xo), (y_a, y_b, yo)

    def land(w):
        first = 1 - w
        wait_for(ar_sem.at[w], staged.at[pl.ds(first, 4 - first)])
        for p in range(3):
            got = staged[4 * w + first:4 * w + 4, :, spans[p][0]:spans[p][1]]
            here = block(x_all, w, z, p, (first * MAIN, (4 - first) * MAIN))
            here[...] = got.reshape((4 - first) * MAIN, got.shape[2])

    def land_last():
        wait_for(ar_sem.at[2], staged_x.at[pl.ds(1, 7)])
        staged_x[0] = send_x[col]
        tiles = [
            staged_x[:, :, lo:lo + 128].reshape(EXPERTS * MAIN, 128) for lo in range(0, staged_x.shape[2], 128)
        ]
        extra = unfold(tiles, share // 128).astype(F32)[:8]
        xo[z, xl, :, :wa] = pair_up(extra[:, :wa], extra[:, wa:2 * wa]).astype(BF16)
        xo[z, xl, :, wa:] = pair_up(extra[:, 2 * wa:2 * wa + wo], extra[:, 2 * wa + wo:]).astype(BF16)

    def plane(d):
        return (z + d + RING) % RING

    def lane(sems_of, u, side, k, p):
        return sems_of[u].at[side, k - 1, UNITS[u][3].index(p)]

    def sent(sem, w, p):
        return sem.at[4 if p == 3 else 2 * w + int(p == 2)]

    def z_send(u, side, k, p):
        d = 1 - 2 * side
        w = UNITS[u][0]
        blk = block(x_all, w, plane(-d * (k - 1)), p, rows_of(u, side, k))
        return remote(blk, blk, sent(zs_sem, w, p), lane(zr_sems, u, side, k, p), on_z(d))

    def group_of(w, i):
        return [g for g, (lo, hi) in enumerate(GROUPS[w]) if lo <= i < hi][0]

    def x_send(w, i):
        if i < 7:
            blk = x_b[w].at[plane(ORDER[i]), xl]
        else:
            blk = x_b[w].at[plane(4), xl].at[pl.ds(*LAST_SPLIT[i - 7])]
        return remote(blk, blk, xs_sem.at[w], xr_sem.at[w, group_of(w, min(i, 7))], across)

    def x_send_last(i):
        blk = xo.at[plane(ORDER[i]), xl, :, wa:]
        return remote(blk, blk, xs_sem.at[2], xr_sem.at[2, group_of(1, i)], across)

    def z_task(u, side, k, p):
        if k > 1 and moves(u, side, k - 1, p):
            z_send(u, side, k - 1, p).wait_recv()
        if k < 5 and moves(u, side, k, p):
            z_send(u, side, k, p).start()

    def gu_send(w, g):
        lo, n, _ = group_rows(w, g)
        rows = pl.ds(lo, n)
        return remote(gu_out[w].at[:, rows], gu_in[w].at[:, rows], gs_sem.at[w], gr_sem.at[w, g], sibling)

    def hid_send(w, g):
        lo, n, _ = group_rows(w, g)
        mine = hid[w].at[co, pl.ds(lo, n)]
        return remote(mine, mine, hs_sem.at[w], hr_sem.at[w, g], sibling)

    def last_rows(pi, blk):
        if blk < 2:
            return xo[pi, xl, :, :wa].astype(F32)[8 * blk:8 * blk + 8]
        both = xo[pi, blk - 2, :, wa:].astype(F32)
        return jnp.concatenate([both[:8], both[8:, :wb - wo]], axis=1)

    def gate_up(w, g, blk):
        lo, n, extra = group_rows(w, g)
        ids = range(*GROUPS[w][g])
        if blk == 2:
            wait_for(xr_sem.at[w, g], yx[w].at[pl.ds(0, len(ids))])
            if w == 1:
                wait_for(xr_sem.at[2, g], yxo.at[pl.ds(0, len(ids))])
        xs, wgu = (x_b[w], wgu_b) if blk >= 2 else (x_a[w], wgu_a)
        parts = [xs[plane(ORDER[i]), blk % 2] for i in ids]
        if extra:
            lasts = [last_rows(plane(ORDER[i]), blk) for i in ids]
            if len(lasts) % 2:
                lasts.append(jnp.zeros_like(lasts[0]))
            parts.append(jnp.concatenate(lasts, axis=0).astype(BF16))
        rows = jnp.concatenate(parts, axis=0)
        for m in range(2):
            for acc, u in ((gu_own[w], co), (gu_out[w], 1 - co)):
                term = nt_dot(rows, wgu[m, u, blk % 2])
                acc[m, lo:lo + n] = acc[m, lo:lo + n] + term if blk else term
        if blk == 3:
            gu_send(w, g).start()

    def hidden(w, g):
        lo, n, _ = group_rows(w, g)
        gu_send(w, g).wait_recv()
        gate = gu_own[w][0, lo:lo + n] + gu_in[w][0, lo:lo + n]
        up = gu_own[w][1, lo:lo + n] + gu_in[w][1, lo:lo + n]
        hid[w][co, lo:lo + n] = (gate / (1.0 + jnp.exp(-gate)) * up).astype(BF16)
        hid_send(w, g).start()

    def down(w, g, kind):
        lo, n, extra = group_rows(w, g)
        ids = range(*GROUPS[w][g])
        if kind == "b":
            hid_send(w, g).wait_recv()
        lasts = {}
        for blk in ((2, 3) if kind == "b" else (0, 1)):
            wdn, ys = (wdn_b, y_b[w]) if blk >= 2 else (wdn_a, y_a[w])
            part = dot(hid[w][0, lo:lo + n], wdn[0, blk % 2]) + dot(hid[w][1, lo:lo + n], wdn[1, blk % 2])
            for at, i in enumerate(ids):
                ys[plane(ORDER[i]), blk % 2] = part[at * N:(at + 1) * N].astype(BF16)
                if extra:
                    at8 = len(ids) * N + 8 * at
                    mine = part[at8:at8 + 8]
                    if blk >= 2:
                        yo[plane(ORDER[i]), blk - 2, :, wa:] = pair_up(mine[:, :wo], mine[:, wo:]).astype(BF16)
                    elif blk == 0:
                        lasts[i] = mine
                    else:
                        yo[plane(ORDER[i]), xl, :, :wa] = pair_up(lasts[i], mine).astype(BF16)

    def far(i):
        return [n for n, ids in enumerate(CROSSED) if i in ids][0]

    def y_send(w, i):
        return remote(
            y_b[w].at[plane(ORDER[i]), 1 - xl], yx[w].at[i], ys_sem.at[w], yr_sem.at[w, far(i)], across
        )

    def y_send_last(i):
        return remote(
            yo.at[plane(ORDER[i]), 1 - xl, :, wa:], yxo.at[i], ys_sem.at[2], yr_sem.at[2, far(i)], across
        )

    def cross(w, *idx):
        for i in idx:
            y_send(w, i).start()
            if w == 1:
                y_send_last(i).start()

    crossed = set()

    def add_across(w, p, n):
        if (w, p, n) in crossed:
            return
        crossed.add((w, p, n))
        ids = CROSSED[n]
        came = yxo if p == 3 else yx[w]
        wait_for(yr_sem.at[2 if p == 3 else w, n], came.at[pl.ds(ids[0], len(ids))])
        for i in ids:
            pi = plane(ORDER[i])
            here = yo.at[pi, xl, :, pl.ds(wa, wo)] if p == 3 else y_b[w].at[pi, xl]
            here[...] = (here[...].astype(F32) + came[i].astype(F32)).astype(BF16)

    def back_block(u, side, j, p):
        w, rows = UNITS[u][0], rows_of(u, side, 5 - j)
        if p == 3:
            return back_o.at[side, j - 1]
        if p == 2:
            return back_b[w].at[side, j - 1, pl.ds(*rows)]
        if p == 4:
            return back_a[w].at[side, j - 1, :, pl.ds(*rows)]
        return back_a[w].at[side, j - 1, p, pl.ds(*rows)]

    def back_send(u, side, j, p):
        d = 1 - 2 * side
        w = UNITS[u][0]
        here = block(y_all, w, plane(d * (5 - j)), p, rows_of(u, side, 5 - j))
        return remote(here, back_block(u, side, j, p), sent(bs_sem, w, p), lane(br_sems, u, side, j, p), on_z(d))

    def ret_task(u, side, j, p):
        w, d = UNITS[u][0], 1 - 2 * side
        if p in (2, 3):
            add_across(w, p, 5 - j)
        if j > 1 and moves(u, side, 6 - j, p):
            back_send(u, side, j - 1, p).wait_recv()
            here = block(y_all, w, plane(d * (5 - j)), p, rows_of(u, side, 6 - j))
            here[...] = (here[...].astype(F32) + back_block(u, side, j - 1, p)[...].astype(F32)).astype(BF16)
        back_send(u, side, j, p).start()

    def f_send(u):
        w, lo, n = UNITS[u][:3]
        return remote(
            final_a[w].at[1 - xl, pl.ds(lo, n)], fx[w].at[pl.ds(lo, n)], fs_sem.at[u], fr_sem.at[u], across
        )

    def f_send_last():
        return remote(final_o.at[:, :wa], fxo, fs_sem.at[3], fr_sem.at[3], across)

    def finish(u, *ps):
        w, lo, n = UNITS[u][:3]
        for p in ps:
            if p in (2, 3):
                add_across(w, p, 0)
            total = block(y_all, w, z, p, (lo, n))[...].astype(F32)
            for side in range(2):
                back_send(u, side, 4, p).wait_recv()
                total += back_block(u, side, 4, p)[...].astype(F32)
            total = total.astype(BF16)
            if p == 3:
                final_o[...] = total
                f_send_last().start()
            elif p == 2:
                final_b[w][lo:lo + n] = total
            else:
                if p == 4:
                    final_a[w][:, lo:lo + n] = total
                else:
                    final_a[w][p, lo:lo + n] = total
                if p:
                    f_send(u).start()

    def deliver(r, kind):
        parcel, result = ((parcel_a, result_a), (parcel_b, result_b), (parcel_x, result_x))[kind]
        return remote(
            parcel.at[r], result.at[col], ds_sem.at[kind], dr_sem.at[kind], in_column(column(r, 1))
        )

    def hand_out(u, kind):
        w, lo, n = UNITS[u][:3]
        if kind == 0:
            f_send(u).wait()
            mine = (final_a[w][xl, lo:lo + n].astype(F32) + fx[w][lo:lo + n].astype(F32)).astype(BF16)
        else:
            mine = final_b[w][lo:lo + n]
        if u == 0:
            ((result_a, result_b)[kind])[col] = mine
            return
        parcel = (parcel_a, parcel_b)[kind]
        first = 4 * w + lo // MAIN
        parcel[first:first + n // MAIN] = mine.reshape(n // MAIN, MAIN, mine.shape[1])
        for r in range(first, first + n // MAIN):
            deliver(r, kind).start()

    def hand_out_last():
        f_send_last().wait()
        both = final_o[:, :wa].astype(F32) + fxo[...].astype(F32)
        mine = jnp.where(xl == 0, both[:8], both[8:])
        over = final_o[:, wa:].astype(F32)
        mine = jnp.concatenate([mine, over[:8], over[8:, :wb - wo]], axis=1)
        mine = jnp.concatenate([mine, jnp.zeros_like(mine)], axis=0).astype(BF16)
        parcel_x[...] = fold(mine)[0].reshape(EXPERTS, MAIN, 128)
        for r in range(1, EXPERTS):
            deliver(r, 2).start()
        result_x[col] = parcel_x[0]

    for r in range(1, 4):
        phase_a(r).start()

    def start_rest():
        for cp in own_w + other_w:
            cp.start()
        for r in range(4, EXPERTS):
            phase_a(r).start()
        pack_last = jnp.transpose(last)[:16].astype(BF16)
        for t, tile in enumerate(fold(dot(pack_last, tok[...]).astype(BF16))):
            send_x[:, :, t * 128:(t + 1) * 128] = tile.reshape(EXPERTS, MAIN, 128)
        for r in range(1, EXPERTS):
            phase_a_last(r).start()

    z_task(0, 1, 1, 4)
    z_task(0, 0, 1, 2)
    z_task(0, 0, 1, 4)
    z_task(0, 1, 1, 2)
    z_task(0, 0, 2, 2)
    z_task(0, 0, 2, 4)
    z_task(0, 1, 2, 4)
    z_task(0, 0, 3, 2)
    z_task(0, 1, 2, 2)
    start_rest()
    z_task(0, 1, 3, 4)
    z_task(0, 0, 3, 4)
    z_task(0, 0, 4, 2)
    z_task(0, 1, 3, 2)
    land(0)
    z_task(1, 0, 1, 0)
    z_task(1, 1, 1, 1)
    z_task(1, 0, 1, 2)
    z_task(1, 1, 1, 2)
    z_task(1, 1, 1, 0)
    land(1)
    land_last()
    x_send(0, 0).start()
    weights_wait(w_sem)
    weights_wait(wr_sem)
    z_task(1, 0, 1, 1)
    z_task(2, 0, 1, 2)
    z_task(1, 1, 2, 1)
    z_task(1, 1, 2, 2)
    z_task(1, 0, 2, 2)
    z_task(1, 0, 2, 1)
    z_task(1, 1, 2, 0)
    z_task(2, 0, 1, 3)
    z_task(0, 1, 4, 4)
    z_task(1, 1, 3, 1)
    z_task(0, 1, 4, 2)
    z_task(2, 1, 1, 3)
    z_task(1, 1, 3, 2)
    x_send(0, 2).start()
    z_task(1, 0, 3, 2)
    z_task(2, 1, 1, 2)
    x_send(0, 1).start()
    z_task(1, 1, 3, 0)
    x_send(0, 4).start()
    z_task(1, 0, 2, 0)
    x_send(0, 3).start()
    z_task(1, 0, 3, 1)
    z_task(0, 0, 5, 2)
    z_task(2, 1, 2, 3)
    z_task(2, 0, 2, 3)
    z_task(1, 0, 4, 2)
    z_task(1, 0, 3, 0)
    gate_up(0, 0, 0)
    z_task(1, 1, 4, 2)
    z_task(1, 0, 4, 1)
    x_send(0, 5).start()
    z_task(0, 0, 4, 4)
    gate_up(0, 0, 1)
    z_task(2, 0, 3, 3)
    z_task(2, 1, 2, 2)
    z_task(1, 0, 5, 2)
    z_task(1, 1, 4, 1)
    z_task(1, 1, 4, 0)
    z_task(2, 0, 2, 2)
    x_send(0, 6).start()
    gate_up(0, 0, 2)
    z_task(2, 1, 1, 1)
    gate_up(0, 0, 3)
    z_task(2, 1, 1, 0)
    x_send(0, 7).start()
    z_task(1, 0, 4, 0)
    z_task(2, 0, 1, 1)
    z_task(1, 1, 5, 1)
    z_task(1, 1, 5, 2)
    z_task(1, 0, 5, 1)
    x_send(0, 8).start()
    x_send_last(1).start()
    x_send(1, 0).start()
    z_task(2, 0, 4, 3)
    z_task(2, 0, 1, 0)
    z_task(2, 0, 3, 2)
    z_task(0, 0, 5, 4)
    z_task(1, 0, 5, 0)
    x_send(1, 1).start()
    z_task(2, 1, 3, 2)
    hidden(0, 0)
    z_task(1, 1, 5, 0)
    x_send_last(5).start()
    gate_up(0, 1, 0)
    gate_up(0, 1, 1)
    gate_up(0, 1, 2)
    z_task(2, 0, 5, 3)
    z_task(2, 1, 3, 3)
    x_send(1, 2).start()
    gate_up(0, 1, 3)
    z_task(2, 0, 2, 1)
    z_task(2, 1, 2, 0)
    down(0, 0, 'b')
    z_task(2, 1, 2, 1)
    z_task(2, 1, 4, 2)
    z_task(2, 0, 2, 0)
    x_send(1, 6).start()
    x_send_last(2).start()
    z_task(2, 1, 4, 3)
    hidden(0, 1)
    down(0, 0, 'a')
    z_task(2, 0, 4, 2)
    x_send(1, 5).start()
    x_send(1, 4).start()
    x_send_last(3).start()
    down(0, 1, 'b')
    z_task(2, 0, 3, 1)
    x_send_last(6).start()
    z_task(2, 1, 3, 0)
    down(0, 1, 'a')
    x_send_last(7).start()
    z_task(2, 1, 3, 1)
    z_task(2, 0, 3, 0)
    cross(0, 6)
    ret_task(1, 1, 1, 0)
    ret_task(1, 0, 1, 0)
    ret_task(1, 0, 1, 1)
    ret_task(0, 0, 1, 4)
    cross(0, 7)
    x_send_last(0).start()
    x_send_last(4).start()
    gate_up(1, 0, 0)
    z_task(2, 0, 5, 2)
    x_send(1, 7).start()
    z_task(2, 1, 5, 2)
    z_task(2, 1, 4, 0)
    z_task(2, 0, 4, 1)
    x_send(1, 8).start()
    gate_up(1, 0, 1)
    cross(0, 5)
    ret_task(1, 1, 1, 1)
    cross(0, 1)
    x_send(1, 3).start()
    z_task(2, 1, 4, 1)
    z_task(2, 0, 4, 0)
    gate_up(1, 1, 0)
    gate_up(1, 1, 1)
    ret_task(0, 1, 2, 4)
    ret_task(1, 0, 2, 1)
    ret_task(1, 0, 2, 0)
    z_task(2, 1, 5, 0)
    gate_up(1, 1, 2)
    ret_task(1, 1, 2, 0)
    gate_up(1, 1, 3)
    ret_task(1, 0, 1, 2)
    ret_task(1, 1, 2, 1)
    z_task(2, 0, 5, 0)
    z_task(2, 1, 5, 1)
    z_task(2, 0, 5, 1)
    gate_up(1, 2, 0)
    gate_up(1, 2, 1)
    ret_task(1, 0, 3, 1)
    ret_task(1, 1, 1, 2)
    ret_task(0, 0, 2, 4)
    gate_up(1, 2, 2)
    ret_task(0, 0, 1, 2)
    ret_task(1, 1, 3, 0)
    cross(0, 4)
    gate_up(1, 2, 3)
    ret_task(1, 0, 3, 0)
    hidden(1, 1)
    ret_task(1, 0, 2, 2)
    ret_task(1, 1, 3, 1)
    ret_task(1, 0, 4, 1)
    hidden(1, 2)
    ret_task(1, 1, 2, 2)
    down(1, 1, 'b')
    ret_task(0, 0, 3, 4)
    ret_task(0, 1, 3, 4)
    down(1, 2, 'b')
    down(1, 2, 'a')
    ret_task(1, 1, 4, 0)
    cross(1, 7)
    ret_task(2, 0, 1, 0)
    gate_up(1, 0, 2)
    ret_task(2, 1, 1, 1)
    cross(1, 5)
    ret_task(1, 1, 4, 1)
    ret_task(1, 0, 4, 0)
    gate_up(1, 0, 3)
    ret_task(2, 0, 1, 1)
    ret_task(2, 1, 1, 0)
    down(1, 1, 'a')
    ret_task(2, 0, 1, 3)
    cross(1, 6)
    ret_task(2, 1, 1, 2)
    ret_task(2, 0, 2, 0)
    hidden(1, 0)
    ret_task(0, 1, 2, 2)
    ret_task(2, 1, 2, 1)
    ret_task(2, 0, 1, 2)
    cross(0, 3)
    ret_task(2, 0, 2, 1)
    cross(0, 2)
    ret_task(2, 1, 2, 0)
    down(1, 0, 'b')
    down(1, 0, 'a')
    ret_task(2, 0, 3, 0)
    ret_task(2, 0, 2, 2)
    ret_task(2, 1, 2, 3)
    cross(1, 4)
    ret_task(2, 1, 3, 1)
    ret_task(2, 0, 3, 1)
    ret_task(2, 1, 3, 0)
    cross(1, 2)
    ret_task(2, 0, 4, 0)
    finish(1, 0)
    ret_task(2, 1, 2, 2)
    ret_task(2, 0, 2, 3)
    cross(1, 3)
    finish(1, 1)
    ret_task(2, 1, 4, 0)
    ret_task(2, 0, 4, 1)
    ret_task(2, 1, 4, 1)
    cross(1, 1)
    ret_task(2, 1, 3, 3)
    ret_task(1, 1, 3, 2)
    ret_task(2, 1, 3, 2)
    cross(1, 0)
    ret_task(2, 0, 3, 3)
    ret_task(1, 0, 3, 2)
    ret_task(2, 0, 3, 2)
    finish(2, 0)
    finish(2, 1)
    ret_task(2, 0, 4, 3)
    cross(0, 0)
    hand_out(1, 0)
    ret_task(2, 1, 4, 3)
    ret_task(1, 0, 4, 2)
    ret_task(0, 0, 2, 2)
    ret_task(1, 1, 4, 2)
    ret_task(2, 0, 4, 2)
    ret_task(2, 1, 4, 2)
    hand_out(2, 0)
    ret_task(0, 1, 3, 2)
    ret_task(0, 0, 4, 4)
    finish(2, 3)
    finish(1, 2)
    hand_out(1, 1)
    ret_task(0, 0, 3, 2)
    ret_task(0, 1, 4, 4)
    hand_out_last()
    finish(2, 2)
    hand_out(2, 1)
    ret_task(0, 0, 4, 2)
    finish(0, 4)
    ret_task(0, 1, 4, 2)
    finish(0, 2)
    hand_out(0, 0)
    hand_out(0, 1)

    seven = pl.ds(0, 7)
    wait_for(as_sem.at[0], send.at[seven])
    wait_for(as_sem.at[1], send_x.at[seven])
    weights_wait(ws_sem)
    for w in range(2):
        wait_for(xs_sem.at[w], yx[w])
        wait_for(ys_sem.at[w], yx[w])
        wait_for(gs_sem.at[w], gu_out[w])
        wait_for(hs_sem.at[w], hid[w].at[0])
        for sem in (zs_sem, bs_sem):
            wait_for(sem.at[2 * w], x_a[w].at[seven])
            wait_for(sem.at[2 * w + 1], yx[w].at[seven])
    for sem in (zs_sem, bs_sem):
        wait_for(sem.at[4], xo.at[seven, 0])
    for sem in (xs_sem, ys_sem):
        wait_for(sem.at[2], yxo)
    gate_col = jnp.sum(jnp.where(rows_i == cols_i, gate_ref[...], 0.0), axis=1, keepdims=True)
    wait_for(dr_sem.at[2], result_x.at[seven])
    extra = unfold([result_x[...].reshape(EXPERTS * MAIN, 128)], (wa + wb) // 128)
    for kind, result, lo, hi in ((0, result_a, 0, wa), (1, result_b, wa, wa + wb)):
        wait_for(dr_sem.at[kind], result.at[seven])
        rows = dot(sel[0], result[...].reshape(EXPERTS * MAIN, hi - lo)) + dot(sel[1][:, :16], extra[:, lo:hi])
        out_ref[:, lo:hi] = (gate_col * rows).astype(BF16)
    for kind, parcel in enumerate((parcel_a, parcel_b, parcel_x)):
        wait_for(ds_sem.at[kind], parcel.at[seven])


def local(tokens, expert_ids, router_gate, w_gate, w_up, w_down):
    n_tok, dmodel = tokens.shape
    units = w_gate.shape[0]
    wa, wb, wo = widths_of(dmodel)
    share = 2 * wa + wb
    folded = -(-share // 2048) * 128
    vmem, dma = pltpu.VMEM, pltpu.SemaphoreType.DMA
    n_rows = [group_rows(w, len(GROUPS[w]))[0] for w in range(2)]

    def waves(*shape, dtype=BF16):
        return [vmem(shape, dtype)] * 2

    def per_row(*shape, dtype=F32):
        return [vmem((2, n, units), dtype) for n in n_rows]

    return pl.pallas_call(
        kernel,
        out_shape=jax.ShapeDtypeStruct((n_tok, wa + wb), BF16),
        in_specs=[pl.BlockSpec(memory_space=pl.ANY)] + [pl.BlockSpec(memory_space=pltpu.VMEM)] * 2
        + [pl.BlockSpec(memory_space=pl.ANY)] * 3,
        out_specs=pl.BlockSpec(memory_space=pltpu.VMEM),
        scratch_shapes=[
            vmem((n_tok, share), BF16),
            vmem((2, n_tok, EXPERTS * MAIN), BF16),
            vmem((EXPERTS, MAIN, share), BF16),
            vmem((EXPERTS, MAIN, folded), BF16),
            vmem((EXPERTS, MAIN, share), BF16),
            vmem((EXPERTS, MAIN, folded), BF16),
            vmem((2, 2, 2, units, wa), BF16),
            vmem((2, 2, 2, units, wb), BF16),
            vmem((2, 2, units, wa), BF16),
            vmem((2, 2, units, wb), BF16),
            vmem((EXPERTS, MAIN, wa), BF16),
            vmem((EXPERTS, MAIN, wb), BF16),
            vmem((EXPERTS, MAIN, 128), BF16),
            vmem((EXPERTS, MAIN, wa), BF16),
            vmem((EXPERTS, MAIN, wb), BF16),
            vmem((EXPERTS, MAIN, 128), BF16),
            vmem((RING, 2, 16, wa + wo), BF16),
            vmem((RING, 2, 16, wa + wo), BF16),
            vmem((RING, 16, wo), BF16),
            vmem((2, 4, 16, wa + wo), BF16),
            vmem((16, wa + wo), BF16),
            vmem((16, wa), BF16),
            *waves(RING, 2, N, wa),
            *waves(RING, 2, N, wb),
            *per_row(),
            *per_row(),
            *per_row(),
            *per_row(dtype=BF16),
            *waves(RING, 2, N, wa),
            *waves(RING, 2, N, wb),
            *waves(RING, N, wb),
            *waves(2, 4, 2, N, wa),
            *waves(2, 4, N, wb),
            *waves(2, N, wa),
            *waves(N, wb),
            *waves(N, wa),
            dma((3,)),
            dma((2, 2)), dma((2, 2)), dma((2, 2)),
            dma((2,)), dma((3,)),
            dma((5,)), [dma((2, 4, len(unit[3]))) for unit in UNITS],
            dma((3,)), dma((3, 3)),
            dma((2,)), dma((2, 3)),
            dma((2,)), dma((2, 3)),
            dma((3,)), dma((3, 5)),
            dma((5,)), [dma((2, 4, len(unit[3]))) for unit in UNITS],
            dma((4,)), dma((4,)),
            dma((3,)), dma((3,)),
        ],
        compiler_params=pltpu.CompilerParams(
            collective_id=0, has_side_effects=True, vmem_limit_bytes=60 * 2**20
        ),
        cost_estimate=pl.CostEstimate(flops=7 * 10**9, bytes_accessed=10**7, transcendentals=200000),
        name="routed_experts",
    )(tokens, expert_ids.reshape(1, n_tok), router_gate.reshape(1, n_tok), w_gate, w_up, w_down)


def solution(mesh):
    placed = (
        P("fsdp", None),
        P("fsdp", None),
        P("fsdp"),
        P(("fsdp", "ctx"), None),
        P(("fsdp", "ctx"), None),
        P(("fsdp", "ctx"), None),
    )
    return jax.shard_map(
        local, mesh=mesh, in_specs=placed, out_specs=P("fsdp", "ctx"), check_vma=False
    )
```

```python
import functools

import jax
import jax.numpy as jnp
from jax import lax
from jax.experimental import pallas as pl
from jax.experimental.pallas import tpu as pltpu
from jax.sharding import PartitionSpec as P

MESH = pl.DeviceIdType.MESH
EXPERTS = 8
MAIN = 16
RING = 8
N = 4 * MAIN
BF16, F32 = jnp.bfloat16, jnp.float32
SOURCES = ((0, 0), (0, 1), (0, 3), (1, 0), (0, 2), (1, 1), (1, 3), (1, 2))
UNITS = (
    (0, 0, 16, (2, 4), ((0, 16), (0, 16))),
    (0, 16, 48, (2, 0, 1), ((16, 16), (32, 32))),
    (1, 0, 64, (2, 3, 0, 1), ((0, 32), (32, 32))),
)
LAST_SPLIT = ((0, 32), (32, 32))
CROSSED = ((0,), (1, 2), (3, 4), (5, 6), (7,))
ORDER = (0, -1, 1, -2, 2, -3, 3, 4)
GROUPS = (((0, 5), (5, 8)), ((0, 5), (5, 7), (7, 8)))
B_BLOCKS = 6


def nt_dot(a, b):
    return lax.dot_general(a, b, (((1,), (1,)), ((), ())), preferred_element_type=F32)


def dot(a, b):
    return jnp.dot(a, b, preferred_element_type=F32)


def transposition(shape):
    r = lax.broadcasted_iota(jnp.int32, shape, 0)
    q = lax.broadcasted_iota(jnp.int32, shape, 1)
    return (((r >> 4) == (q & 15)) & ((r & 15) == (q >> 4))).astype(F32).astype(BF16)


def fold(rows):
    tiles = []
    for lo in range(0, rows.shape[1], 2048):
        part = rows[:, lo:lo + 2048]
        n = part.shape[1] // 128
        stack = jnp.concatenate([part[:, j * 128:(j + 1) * 128] for j in range(n)], axis=0)
        tiles.append(dot(transposition((128, n * 16)), stack).astype(BF16))
    return tiles


def unfold(tiles, n_blocks):
    blocks = []
    for t, tile in enumerate(tiles):
        n = min(16, n_blocks - 16 * t)
        stack = dot(transposition((n * 16, 128)), tile).astype(BF16)
        blocks += [stack[j * 16:(j + 1) * 16] for j in range(n)]
    return jnp.concatenate(blocks, axis=1)


def widths_of(dmodel):
    wb = B_BLOCKS * 128
    wa = dmodel // 4 - wb
    return wa, wb, -(-B_BLOCKS // 2) * 128


def group_rows(w, g):
    at = 0
    for h, (lo, hi) in enumerate(GROUPS[w]):
        main, extra = (hi - lo) * N, w * (-(-(hi - lo) // 2) * 16)
        if h == g:
            return at, main + extra, extra
        at += main + extra
    return at, 0, 0


def pair_up(left, right):
    if right.shape[1] < left.shape[1]:
        pad = jnp.zeros((8, left.shape[1] - right.shape[1]), F32)
        right = jnp.concatenate([right, pad], axis=1)
    return jnp.concatenate([left, right], axis=0)


def moves(u, side, k, p):
    if p not in UNITS[u][3]:
        return False
    if k < 4:
        return True
    if u == 0:
        return side == 0
    return p != 3 or side == 0


def rows_of(u, side, k):
    return UNITS[u][4][side] if k == 4 else UNITS[u][1:3]


def kernel(
    tok_ref, ids_ref, gate_ref, wg_ref, wu_ref, wd_ref,
    out_ref,
    tok, sel, send, send_x, staged, staged_x, wgu_a, wgu_b, wdn_a, wdn_b,
    parcel_a, parcel_b, parcel_x, result_a, result_b, result_x, xo, yo, yxo, back_o, final_o, fxo, *rest,
):
    per_wave, sems = rest[:28], rest[28:]
    (
        x_a, x_b, gu_own, gu_out, gu_in, hid, y_a, y_b, yx, back_a, back_b, final_a, final_b, fx,
    ) = [per_wave[2 * i:2 * i + 2] for i in range(14)]
    (
        t_sem, w_sem, ws_sem, wr_sem, as_sem, ar_sem, zs_sem, zr_sems, xs_sem, xr_sem,
        gs_sem, gr_sem, hs_sem, hr_sem, ys_sem, yr_sem, bs_sem, br_sems, fs_sem, fr_sem,
        ds_sem, dr_sem,
    ) = sems

    def wait_for(sem, ref):
        pltpu.make_async_copy(ref, ref, sem).wait()

    c, f = lax.axis_index("ctx"), lax.axis_index("fsdp")
    xl, co = c // 2, c % 2
    col, z = f // RING, f % RING
    wa, wb = x_a[0].shape[3], x_b[0].shape[3]
    wo = yxo.shape[2]
    share = 2 * wa + wb

    def on_z(d):
        return (c, col * RING + (z + d + RING) % RING)

    def column(r, sign):
        dx, dy = SOURCES[r]
        return (col // 4 + dx) % 2 * 4 + (col % 4 + sign * dy + 4) % 4

    def in_column(e):
        return (c, e * RING + z)

    sibling = (c + 1 - 2 * co, f)
    across = ((c + 2) % 4, f)

    def remote(src, dst, ssem, rsem, dev):
        return pltpu.make_async_remote_copy(
            src_ref=src, dst_ref=dst, send_sem=ssem, recv_sem=rsem, device_id=dev, device_id_type=MESH
        )

    def column_of(core, blk):
        quarter = (blk % 2) * 2 + core
        return pl.multiple_of(quarter * (wa + wb) + (wa if blk >= 2 else 0), 128)

    def columns(ref, core, blk):
        return ref.at[:, pl.ds(column_of(core, blk), wb if blk >= 2 else wa)]

    own_b = pl.multiple_of((xl * 2 + co) * (wa + wb) + wa, 128)
    share_refs = [columns(tok_ref, co, 0), columns(tok_ref, co, 1), tok_ref.at[:, pl.ds(own_b, wb)]]
    spans = ((0, wa), (wa, 2 * wa), (2 * wa, share))
    get_tok = [
        pltpu.make_async_copy(share_refs[p], tok.at[:, spans[p][0]:spans[p][1]], t_sem.at[p]) for p in range(3)
    ]
    for cp in get_tok:
        cp.start()

    barrier = pltpu.get_barrier_semaphore()
    partners = [on_z(1), on_z(-1), sibling, across] + [in_column((col + i) % EXPERTS) for i in range(1, EXPERTS)]
    for dev in partners:
        pl.semaphore_signal(barrier, inc=1, device_id=dev, device_id_type=MESH)

    def weight_slot(m, unit_core, blk):
        if m == 2:
            return (wdn_b if blk >= 2 else wdn_a).at[unit_core, blk % 2]
        return (wgu_b if blk >= 2 else wgu_a).at[m, unit_core, blk % 2]

    w_refs = (wg_ref, wu_ref, wd_ref)
    own_w = [
        pltpu.make_async_copy(columns(w_refs[m], co, blk), weight_slot(m, co, blk), w_sem.at[m // 2, blk // 2])
        for m in range(3) for blk in range(4)
    ]
    other_w = [
        remote(
            columns(w_refs[m], 1 - co, blk), weight_slot(m, co, blk),
            ws_sem.at[m // 2, blk // 2], wr_sem.at[m // 2, blk // 2], sibling,
        )
        for m in range(3) for blk in range(4)
    ]

    def weights_wait(sem):
        for m, arrays in ((0, (wgu_a.at[:, 0], wgu_b.at[:, 0])), (1, (wdn_a.at[0], wdn_b.at[0]))):
            for part in range(2):
                wait_for(sem.at[m, part], arrays[part])


    n_tok = tok.shape[0]
    rows_i = lax.broadcasted_iota(jnp.int32, (n_tok, n_tok), 0)
    cols_i = lax.broadcasted_iota(jnp.int32, (n_tok, n_tok), 1)
    ids_row = ids_ref[...]
    ids_col = jnp.sum(jnp.where(rows_i == cols_i, ids_row, 0), axis=1, keepdims=True)
    same = (ids_row == ids_col) & (cols_i < rows_i)
    rank = jnp.sum(same.astype(jnp.int32), axis=1, keepdims=True)
    main = ((cols_i == ids_col * MAIN + rank) & (rank < MAIN)).astype(F32)
    last = ((cols_i == ids_col) & (rank == MAIN)).astype(F32)
    sel[0] = main.astype(BF16)
    sel[1] = last.astype(BF16)
    pack = jnp.transpose(main).astype(BF16)
    for p in range(3):
        lo, hi = spans[p]
        get_tok[p].wait()
        send[:, :, lo:hi] = dot(pack, tok[:, lo:hi]).astype(BF16).reshape(EXPERTS, MAIN, hi - lo)

    for p in range(3):
        x_block = (x_b[0].at[z, xl] if p == 2 else x_a[0].at[z, p])
        x_block[:MAIN, :] = send[col, :, spans[p][0]:spans[p][1]]

    pl.semaphore_wait(barrier, len(partners))

    def phase_a(r):
        e = column(r, -1)
        return remote(send.at[e], staged.at[r], as_sem.at[0], ar_sem.at[r // 4], in_column(e))

    def phase_a_last(r):
        e = column(r, -1)
        return remote(send_x.at[e], staged_x.at[r], as_sem.at[1], ar_sem.at[2], in_column(e))

    def block(arrays, w, pi, p, rows):
        a, b, last = arrays
        if p == 3:
            return last.at[pi, xl]
        if p == 2:
            return b[w].at[pi, xl, pl.ds(*rows)]
        return a[w].at[pi, :, pl.ds(*rows)] if p == 4 else a[w].at[pi, p, pl.ds(*rows)]

    x_all, y_all = (x_a, x_b, xo), (y_a, y_b, yo)

    def land(w):
        first = 1 - w
        wait_for(ar_sem.at[w], staged.at[pl.ds(first, 4 - first)])
        for p in range(3):
            got = staged[4 * w + first:4 * w + 4, :, spans[p][0]:spans[p][1]]
            here = block(x_all, w, z, p, (first * MAIN, (4 - first) * MAIN))
            here[...] = got.reshape((4 - first) * MAIN, got.shape[2])

    def land_last():
        wait_for(ar_sem.at[2], staged_x.at[pl.ds(1, 7)])
        staged_x[0] = send_x[col]
        tiles = [
            staged_x[:, :, lo:lo + 128].reshape(EXPERTS * MAIN, 128) for lo in range(0, staged_x.shape[2], 128)
        ]
        extra = unfold(tiles, share // 128).astype(F32)[:8]
        xo[z, xl, :, :wa] = pair_up(extra[:, :wa], extra[:, wa:2 * wa]).astype(BF16)
        xo[z, xl, :, wa:] = pair_up(extra[:, 2 * wa:2 * wa + wo], extra[:, 2 * wa + wo:]).astype(BF16)

    def plane(d):
        return (z + d + RING) % RING

    def lane(sems_of, u, side, k, p):
        return sems_of[u].at[side, k - 1, UNITS[u][3].index(p)]

    def sent(sem, w, p):
        return sem.at[4 if p == 3 else 2 * w + int(p == 2)]

    def z_send(u, side, k, p):
        d = 1 - 2 * side
        w = UNITS[u][0]
        blk = block(x_all, w, plane(-d * (k - 1)), p, rows_of(u, side, k))
        return remote(blk, blk, sent(zs_sem, w, p), lane(zr_sems, u, side, k, p), on_z(d))

    def group_of(w, i):
        return [g for g, (lo, hi) in enumerate(GROUPS[w]) if lo <= i < hi][0]

    def x_send(w, i):
        if i < 7:
            blk = x_b[w].at[plane(ORDER[i]), xl]
        else:
            blk = x_b[w].at[plane(4), xl].at[pl.ds(*LAST_SPLIT[i - 7])]
        return remote(blk, blk, xs_sem.at[w], xr_sem.at[w, group_of(w, min(i, 7))], across)

    def x_send_last(i):
        blk = xo.at[plane(ORDER[i]), xl, :, wa:]
        return remote(blk, blk, xs_sem.at[2], xr_sem.at[2, group_of(1, i)], across)

    def z_task(u, side, k, p):
        if k > 1 and moves(u, side, k - 1, p):
            z_send(u, side, k - 1, p).wait_recv()
        if k < 5 and moves(u, side, k, p):
            z_send(u, side, k, p).start()

    def gu_send(w, g):
        lo, n, _ = group_rows(w, g)
        rows = pl.ds(lo, n)
        return remote(gu_out[w].at[:, rows], gu_in[w].at[:, rows], gs_sem.at[w], gr_sem.at[w, g], sibling)

    def hid_send(w, g):
        lo, n, _ = group_rows(w, g)
        mine = hid[w].at[co, pl.ds(lo, n)]
        return remote(mine, mine, hs_sem.at[w], hr_sem.at[w, g], sibling)

    def last_rows(pi, blk):
        if blk < 2:
            return xo[pi, xl, :, :wa].astype(F32)[8 * blk:8 * blk + 8]
        both = xo[pi, blk - 2, :, wa:].astype(F32)
        return jnp.concatenate([both[:8], both[8:, :wb - wo]], axis=1)

    def gate_up(w, g, blk):
        lo, n, extra = group_rows(w, g)
        ids = range(*GROUPS[w][g])
        if blk == 2:
            wait_for(xr_sem.at[w, g], yx[w].at[pl.ds(0, len(ids))])
            if w == 1:
                wait_for(xr_sem.at[2, g], yxo.at[pl.ds(0, len(ids))])
        xs, wgu = (x_b[w], wgu_b) if blk >= 2 else (x_a[w], wgu_a)
        parts = [xs[plane(ORDER[i]), blk % 2] for i in ids]
        if extra:
            lasts = [last_rows(plane(ORDER[i]), blk) for i in ids]
            if len(lasts) % 2:
                lasts.append(jnp.zeros_like(lasts[0]))
            parts.append(jnp.concatenate(lasts, axis=0).astype(BF16))
        rows = jnp.concatenate(parts, axis=0)
        for m in range(2):
            for acc, u in ((gu_own[w], co), (gu_out[w], 1 - co)):
                term = nt_dot(rows, wgu[m, u, blk % 2])
                acc[m, lo:lo + n] = acc[m, lo:lo + n] + term if blk else term
        if blk == 3:
            gu_send(w, g).start()

    def hidden(w, g):
        lo, n, _ = group_rows(w, g)
        gu_send(w, g).wait_recv()
        gate = gu_own[w][0, lo:lo + n] + gu_in[w][0, lo:lo + n]
        up = gu_own[w][1, lo:lo + n] + gu_in[w][1, lo:lo + n]
        hid[w][co, lo:lo + n] = (gate / (1.0 + jnp.exp(-gate)) * up).astype(BF16)
        hid_send(w, g).start()

    def down(w, g, kind):
        lo, n, extra = group_rows(w, g)
        ids = range(*GROUPS[w][g])
        if kind == "b":
            hid_send(w, g).wait_recv()
        lasts = {}
        for blk in ((2, 3) if kind == "b" else (0, 1)):
            wdn, ys = (wdn_b, y_b[w]) if blk >= 2 else (wdn_a, y_a[w])
            part = dot(hid[w][0, lo:lo + n], wdn[0, blk % 2]) + dot(hid[w][1, lo:lo + n], wdn[1, blk % 2])
            for at, i in enumerate(ids):
                ys[plane(ORDER[i]), blk % 2] = part[at * N:(at + 1) * N].astype(BF16)
                if extra:
                    at8 = len(ids) * N + 8 * at
                    mine = part[at8:at8 + 8]
                    if blk >= 2:
                        yo[plane(ORDER[i]), blk - 2, :, wa:] = pair_up(mine[:, :wo], mine[:, wo:]).astype(BF16)
                    elif blk == 0:
                        lasts[i] = mine
                    else:
                        yo[plane(ORDER[i]), xl, :, :wa] = pair_up(lasts[i], mine).astype(BF16)

    def far(i):
        return [n for n, ids in enumerate(CROSSED) if i in ids][0]

    def y_send(w, i):
        return remote(
            y_b[w].at[plane(ORDER[i]), 1 - xl], yx[w].at[i], ys_sem.at[w], yr_sem.at[w, far(i)], across
        )

    def y_send_last(i):
        return remote(
            yo.at[plane(ORDER[i]), 1 - xl, :, wa:], yxo.at[i], ys_sem.at[2], yr_sem.at[2, far(i)], across
        )

    def cross(w, *idx):
        for i in idx:
            y_send(w, i).start()
            if w == 1:
                y_send_last(i).start()

    crossed = set()

    def add_across(w, p, n):
        if (w, p, n) in crossed:
            return
        crossed.add((w, p, n))
        ids = CROSSED[n]
        came = yxo if p == 3 else yx[w]
        wait_for(yr_sem.at[2 if p == 3 else w, n], came.at[pl.ds(ids[0], len(ids))])
        for i in ids:
            pi = plane(ORDER[i])
            here = yo.at[pi, xl, :, pl.ds(wa, wo)] if p == 3 else y_b[w].at[pi, xl]
            here[...] = (here[...].astype(F32) + came[i].astype(F32)).astype(BF16)

    def back_block(u, side, j, p):
        w, rows = UNITS[u][0], rows_of(u, side, 5 - j)
        if p == 3:
            return back_o.at[side, j - 1]
        if p == 2:
            return back_b[w].at[side, j - 1, pl.ds(*rows)]
        if p == 4:
            return back_a[w].at[side, j - 1, :, pl.ds(*rows)]
        return back_a[w].at[side, j - 1, p, pl.ds(*rows)]

    def back_send(u, side, j, p):
        d = 1 - 2 * side
        w = UNITS[u][0]
        here = block(y_all, w, plane(d * (5 - j)), p, rows_of(u, side, 5 - j))
        return remote(here, back_block(u, side, j, p), sent(bs_sem, w, p), lane(br_sems, u, side, j, p), on_z(d))

    def ret_task(u, side, j, p):
        w, d = UNITS[u][0], 1 - 2 * side
        if p in (2, 3):
            add_across(w, p, 5 - j)
        if j > 1 and moves(u, side, 6 - j, p):
            back_send(u, side, j - 1, p).wait_recv()
            here = block(y_all, w, plane(d * (5 - j)), p, rows_of(u, side, 6 - j))
            here[...] = (here[...].astype(F32) + back_block(u, side, j - 1, p)[...].astype(F32)).astype(BF16)
        back_send(u, side, j, p).start()

    def f_send(u):
        w, lo, n = UNITS[u][:3]
        return remote(
            final_a[w].at[1 - xl, pl.ds(lo, n)], fx[w].at[pl.ds(lo, n)], fs_sem.at[u], fr_sem.at[u], across
        )

    def f_send_last():
        return remote(final_o.at[:, :wa], fxo, fs_sem.at[3], fr_sem.at[3], across)

    def finish(u, *ps):
        w, lo, n = UNITS[u][:3]
        for p in ps:
            if p in (2, 3):
                add_across(w, p, 0)
            total = block(y_all, w, z, p, (lo, n))[...].astype(F32)
            for side in range(2):
                back_send(u, side, 4, p).wait_recv()
                total += back_block(u, side, 4, p)[...].astype(F32)
            total = total.astype(BF16)
            if p == 3:
                final_o[...] = total
                f_send_last().start()
            elif p == 2:
                final_b[w][lo:lo + n] = total
            else:
                if p == 4:
                    final_a[w][:, lo:lo + n] = total
                else:
                    final_a[w][p, lo:lo + n] = total
                if p:
                    f_send(u).start()

    def deliver(r, kind):
        parcel, result = ((parcel_a, result_a), (parcel_b, result_b), (parcel_x, result_x))[kind]
        return remote(
            parcel.at[r], result.at[col], ds_sem.at[kind], dr_sem.at[kind], in_column(column(r, 1))
        )

    def hand_out(u, kind):
        w, lo, n = UNITS[u][:3]
        if kind == 0:
            f_send(u).wait()
            mine = (final_a[w][xl, lo:lo + n].astype(F32) + fx[w][lo:lo + n].astype(F32)).astype(BF16)
        else:
            mine = final_b[w][lo:lo + n]
        if u == 0:
            ((result_a, result_b)[kind])[col] = mine
            return
        parcel = (parcel_a, parcel_b)[kind]
        first = 4 * w + lo // MAIN
        parcel[first:first + n // MAIN] = mine.reshape(n // MAIN, MAIN, mine.shape[1])
        for r in range(first, first + n // MAIN):
            deliver(r, kind).start()

    def hand_out_last():
        f_send_last().wait()
        both = final_o[:, :wa].astype(F32) + fxo[...].astype(F32)
        mine = jnp.where(xl == 0, both[:8], both[8:])
        over = final_o[:, wa:].astype(F32)
        mine = jnp.concatenate([mine, over[:8], over[8:, :wb - wo]], axis=1)
        mine = jnp.concatenate([mine, jnp.zeros_like(mine)], axis=0).astype(BF16)
        parcel_x[...] = fold(mine)[0].reshape(EXPERTS, MAIN, 128)
        for r in range(1, EXPERTS):
            deliver(r, 2).start()
        result_x[col] = parcel_x[0]

    for r in range(1, 4):
        phase_a(r).start()

    def start_rest():
        for cp in own_w + other_w:
            cp.start()
        for r in range(4, EXPERTS):
            phase_a(r).start()
        pack_last = jnp.transpose(last)[:16].astype(BF16)
        for t, tile in enumerate(fold(dot(pack_last, tok[...]).astype(BF16))):
            send_x[:, :, t * 128:(t + 1) * 128] = tile.reshape(EXPERTS, MAIN, 128)
        for r in range(1, EXPERTS):
            phase_a_last(r).start()

    z_task(0, 0, 1, 4)
    z_task(0, 0, 1, 2)
    z_task(0, 1, 1, 2)
    z_task(0, 1, 1, 4)
    start_rest()
    z_task(0, 1, 2, 2)
    z_task(0, 0, 2, 4)
    z_task(0, 1, 2, 4)
    z_task(0, 0, 2, 2)
    z_task(0, 0, 3, 4)
    z_task(0, 1, 3, 2)
    z_task(0, 1, 3, 4)
    z_task(0, 0, 3, 2)
    land(0)
    z_task(1, 0, 1, 1)
    z_task(1, 0, 1, 0)
    z_task(1, 1, 1, 2)
    z_task(1, 1, 1, 1)
    z_task(1, 1, 1, 0)
    z_task(1, 0, 1, 2)
    z_task(1, 1, 2, 2)
    x_send(0, 2).start()
    z_task(1, 0, 2, 1)
    z_task(0, 0, 4, 2)
    land(1)
    land_last()
    z_task(2, 1, 1, 3)
    z_task(1, 0, 2, 2)
    z_task(1, 0, 2, 0)
    x_send(0, 1).start()
    z_task(0, 1, 4, 2)
    z_task(1, 1, 2, 1)
    z_task(1, 1, 2, 0)
    z_task(2, 0, 1, 3)
    x_send(0, 0).start()
    z_task(2, 1, 1, 2)
    z_task(1, 0, 3, 2)
    z_task(1, 1, 3, 2)
    x_send(0, 3).start()
    z_task(1, 0, 3, 1)
    z_task(1, 0, 3, 0)
    z_task(1, 1, 3, 1)
    x_send(0, 4).start()
    z_task(0, 1, 4, 4)
    z_task(2, 0, 1, 2)
    z_task(1, 1, 3, 0)
    z_task(0, 0, 4, 4)
    z_task(1, 1, 4, 2)
    weights_wait(w_sem)
    weights_wait(wr_sem)
    x_send(1, 0).start()
    x_send(0, 6).start()
    z_task(0, 0, 5, 2)
    gate_up(0, 0, 0)
    z_task(1, 1, 4, 1)
    z_task(1, 0, 4, 2)
    z_task(1, 0, 4, 1)
    gate_up(0, 0, 1)
    z_task(2, 1, 2, 2)
    z_task(1, 0, 4, 0)
    z_task(2, 0, 1, 0)
    gate_up(0, 0, 2)
    z_task(2, 0, 2, 3)
    z_task(1, 1, 4, 0)
    z_task(1, 1, 5, 2)
    x_send(0, 5).start()
    z_task(2, 0, 2, 2)
    gate_up(0, 0, 3)
    z_task(2, 1, 1, 1)
    z_task(1, 1, 5, 1)
    x_send(0, 8).start()
    z_task(1, 0, 5, 2)
    z_task(2, 0, 1, 1)
    z_task(2, 1, 2, 3)
    x_send(0, 7).start()
    z_task(2, 1, 1, 0)
    hidden(0, 0)
    x_send(1, 2).start()
    z_task(1, 0, 5, 0)
    z_task(2, 0, 2, 0)
    z_task(0, 0, 5, 4)
    z_task(1, 1, 5, 0)
    z_task(2, 1, 3, 2)
    x_send(1, 1).start()
    z_task(2, 0, 3, 3)
    z_task(1, 0, 5, 1)
    x_send(1, 4).start()
    gate_up(0, 1, 0)
    gate_up(0, 1, 1)
    gate_up(0, 1, 2)
    z_task(2, 1, 2, 1)
    gate_up(0, 1, 3)
    z_task(2, 1, 3, 3)
    x_send_last(3).start()
    x_send_last(4).start()
    x_send_last(0).start()
    z_task(2, 0, 2, 1)
    down(0, 0, 'b')
    down(0, 0, 'a')
    z_task(2, 0, 3, 2)
    z_task(2, 1, 2, 0)
    x_send_last(2).start()
    x_send_last(1).start()
    hidden(0, 1)
    z_task(2, 0, 4, 3)
    z_task(2, 1, 4, 2)
    x_send(1, 6).start()
    x_send(1, 3).start()
    z_task(2, 0, 3, 1)
    z_task(2, 1, 3, 1)
    down(0, 1, 'b')
    cross(0, 6)
    down(0, 1, 'a')
    ret_task(1, 1, 1, 0)
    z_task(2, 0, 3, 0)
    z_task(2, 1, 3, 0)
    ret_task(1, 1, 1, 1)
    gate_up(1, 0, 0)
    cross(0, 5)
    ret_task(1, 0, 1, 1)
    z_task(2, 1, 5, 2)
    gate_up(1, 0, 1)
    cross(0, 7)
    z_task(2, 0, 5, 3)
    ret_task(1, 0, 1, 0)
    z_task(2, 1, 4, 3)
    z_task(2, 0, 4, 2)
    gate_up(1, 0, 2)
    x_send_last(5).start()
    x_send_last(7).start()
    z_task(2, 0, 4, 0)
    ret_task(0, 0, 1, 4)
    ret_task(1, 1, 2, 0)
    z_task(2, 1, 4, 1)
    gate_up(1, 0, 3)
    z_task(2, 1, 4, 0)
    ret_task(1, 0, 2, 0)
    z_task(2, 0, 5, 2)
    x_send(1, 8).start()
    z_task(2, 0, 4, 1)
    ret_task(1, 1, 2, 1)
    cross(0, 1)
    gate_up(1, 1, 0)
    ret_task(1, 0, 1, 2)
    x_send_last(6).start()
    ret_task(1, 0, 2, 1)
    ret_task(0, 0, 2, 4)
    ret_task(0, 1, 2, 2)
    x_send(1, 7).start()
    x_send(1, 5).start()
    ret_task(1, 1, 1, 2)
    z_task(2, 0, 5, 0)
    ret_task(1, 1, 3, 0)
    z_task(2, 1, 5, 1)
    gate_up(1, 1, 1)
    z_task(2, 1, 5, 0)
    ret_task(1, 0, 3, 0)
    z_task(2, 0, 5, 1)
    cross(0, 4)
    cross(0, 3)
    gate_up(1, 2, 0)
    ret_task(1, 1, 3, 1)
    ret_task(1, 0, 2, 2)
    gate_up(1, 2, 1)
    gate_up(1, 2, 2)
    gate_up(1, 2, 3)
    ret_task(1, 1, 2, 2)
    ret_task(1, 0, 3, 1)
    cross(0, 2)
    hidden(1, 0)
    ret_task(1, 0, 4, 0)
    ret_task(0, 0, 1, 2)
    hidden(1, 2)
    ret_task(0, 1, 2, 4)
    ret_task(1, 1, 4, 0)
    ret_task(1, 1, 4, 1)
    gate_up(1, 1, 2)
    gate_up(1, 1, 3)
    ret_task(1, 0, 4, 1)
    down(1, 2, 'b')
    down(1, 2, 'a')
    ret_task(2, 0, 1, 0)
    cross(1, 7)
    hidden(1, 1)
    ret_task(2, 1, 1, 0)
    ret_task(1, 0, 3, 2)
    ret_task(2, 1, 1, 1)
    ret_task(1, 1, 3, 2)
    ret_task(2, 0, 1, 1)
    down(1, 1, 'b')
    down(1, 1, 'a')
    ret_task(2, 0, 2, 0)
    cross(1, 6)
    ret_task(2, 1, 2, 0)
    ret_task(1, 0, 4, 2)
    down(1, 0, 'b')
    ret_task(2, 1, 1, 2)
    cross(1, 5)
    ret_task(2, 0, 1, 2)
    finish(1, 0)
    cross(0, 0)
    ret_task(2, 1, 2, 1)
    cross(1, 4)
    ret_task(2, 0, 1, 3)
    down(1, 0, 'a')
    ret_task(2, 0, 3, 0)
    ret_task(2, 1, 3, 0)
    ret_task(2, 1, 2, 2)
    ret_task(2, 0, 2, 1)
    ret_task(2, 1, 3, 1)
    cross(1, 2)
    cross(1, 3)
    ret_task(2, 0, 2, 2)
    ret_task(2, 0, 3, 1)
    ret_task(1, 1, 4, 2)
    finish(1, 1)
    ret_task(2, 1, 2, 3)
    ret_task(2, 0, 4, 0)
    ret_task(2, 1, 4, 0)
    ret_task(2, 0, 2, 3)
    ret_task(2, 0, 4, 1)
    cross(1, 1)
    ret_task(2, 1, 3, 3)
    ret_task(2, 1, 4, 1)
    ret_task(2, 1, 3, 2)
    cross(1, 0)
    ret_task(2, 0, 3, 3)
    ret_task(2, 0, 3, 2)
    finish(1, 2)
    finish(2, 0)
    ret_task(2, 1, 4, 3)
    hand_out(1, 0)
    finish(2, 1)
    ret_task(2, 0, 4, 3)
    ret_task(0, 0, 3, 4)
    ret_task(0, 1, 3, 4)
    ret_task(0, 0, 2, 2)
    hand_out(1, 1)
    ret_task(0, 1, 3, 2)
    ret_task(2, 1, 4, 2)
    ret_task(2, 0, 4, 2)
    finish(2, 3)
    hand_out(2, 0)
    ret_task(0, 0, 4, 4)
    ret_task(0, 0, 3, 2)
    ret_task(0, 1, 4, 4)
    hand_out_last()
    finish(2, 2)
    hand_out(2, 1)
    ret_task(0, 0, 4, 2)
    ret_task(0, 1, 4, 2)
    finish(0, 4)
    hand_out(0, 0)
    finish(0, 2)
    hand_out(0, 1)

    seven = pl.ds(0, 7)
    wait_for(as_sem.at[0], send.at[seven])
    wait_for(as_sem.at[1], send_x.at[seven])
    weights_wait(ws_sem)
    for w in range(2):
        wait_for(xs_sem.at[w], yx[w])
        wait_for(ys_sem.at[w], yx[w])
        wait_for(gs_sem.at[w], gu_out[w])
        wait_for(hs_sem.at[w], hid[w].at[0])
        for sem in (zs_sem, bs_sem):
            wait_for(sem.at[2 * w], x_a[w].at[seven])
            wait_for(sem.at[2 * w + 1], yx[w].at[seven])
    for sem in (zs_sem, bs_sem):
        wait_for(sem.at[4], xo.at[seven, 0])
    for sem in (xs_sem, ys_sem):
        wait_for(sem.at[2], yxo)
    gate_col = jnp.sum(jnp.where(rows_i == cols_i, gate_ref[...], 0.0), axis=1, keepdims=True)
    halves = ((0, result_a, 0, wa), (1, result_b, wa, wa + wb))
    rows = []
    for kind, result, lo, hi in halves:
        wait_for(dr_sem.at[kind], result.at[seven])
        rows.append(dot(sel[0], result[...].reshape(EXPERTS * MAIN, hi - lo)))
    wait_for(dr_sem.at[2], result_x.at[seven])
    extra = unfold([result_x[...].reshape(EXPERTS * MAIN, 128)], (wa + wb) // 128)
    for kind, _, lo, hi in halves:
        out_ref[:, lo:hi] = (gate_col * (rows[kind] + dot(sel[1][:, :16], extra[:, lo:hi]))).astype(BF16)
    for kind, parcel in enumerate((parcel_a, parcel_b, parcel_x)):
        wait_for(ds_sem.at[kind], parcel.at[seven])


def local(tokens, expert_ids, router_gate, w_gate, w_up, w_down):
    n_tok, dmodel = tokens.shape
    units = w_gate.shape[0]
    wa, wb, wo = widths_of(dmodel)
    share = 2 * wa + wb
    folded = -(-share // 2048) * 128
    vmem, dma = pltpu.VMEM, pltpu.SemaphoreType.DMA
    n_rows = [group_rows(w, len(GROUPS[w]))[0] for w in range(2)]

    def waves(*shape, dtype=BF16):
        return [vmem(shape, dtype)] * 2

    def per_row(*shape, dtype=F32):
        return [vmem((2, n, units), dtype) for n in n_rows]

    return pl.pallas_call(
        kernel,
        out_shape=jax.ShapeDtypeStruct((n_tok, wa + wb), BF16),
        in_specs=[pl.BlockSpec(memory_space=pl.ANY)] + [pl.BlockSpec(memory_space=pltpu.VMEM)] * 2
        + [pl.BlockSpec(memory_space=pl.ANY)] * 3,
        out_specs=pl.BlockSpec(memory_space=pltpu.VMEM),
        scratch_shapes=[
            vmem((n_tok, share), BF16),
            vmem((2, n_tok, EXPERTS * MAIN), BF16),
            vmem((EXPERTS, MAIN, share), BF16),
            vmem((EXPERTS, MAIN, folded), BF16),
            vmem((EXPERTS, MAIN, share), BF16),
            vmem((EXPERTS, MAIN, folded), BF16),
            vmem((2, 2, 2, units, wa), BF16),
            vmem((2, 2, 2, units, wb), BF16),
            vmem((2, 2, units, wa), BF16),
            vmem((2, 2, units, wb), BF16),
            vmem((EXPERTS, MAIN, wa), BF16),
            vmem((EXPERTS, MAIN, wb), BF16),
            vmem((EXPERTS, MAIN, 128), BF16),
            vmem((EXPERTS, MAIN, wa), BF16),
            vmem((EXPERTS, MAIN, wb), BF16),
            vmem((EXPERTS, MAIN, 128), BF16),
            vmem((RING, 2, 16, wa + wo), BF16),
            vmem((RING, 2, 16, wa + wo), BF16),
            vmem((RING, 16, wo), BF16),
            vmem((2, 4, 16, wa + wo), BF16),
            vmem((16, wa + wo), BF16),
            vmem((16, wa), BF16),
            *waves(RING, 2, N, wa),
            *waves(RING, 2, N, wb),
            *per_row(),
            *per_row(),
            *per_row(),
            *per_row(dtype=BF16),
            *waves(RING, 2, N, wa),
            *waves(RING, 2, N, wb),
            *waves(RING, N, wb),
            *waves(2, 4, 2, N, wa),
            *waves(2, 4, N, wb),
            *waves(2, N, wa),
            *waves(N, wb),
            *waves(N, wa),
            dma((3,)),
            dma((2, 2)), dma((2, 2)), dma((2, 2)),
            dma((2,)), dma((3,)),
            dma((5,)), [dma((2, 4, len(unit[3]))) for unit in UNITS],
            dma((3,)), dma((3, 3)),
            dma((2,)), dma((2, 3)),
            dma((2,)), dma((2, 3)),
            dma((3,)), dma((3, 5)),
            dma((5,)), [dma((2, 4, len(unit[3]))) for unit in UNITS],
            dma((4,)), dma((4,)),
            dma((3,)), dma((3,)),
        ],
        compiler_params=pltpu.CompilerParams(
            collective_id=0, has_side_effects=True, vmem_limit_bytes=60 * 2**20
        ),
        cost_estimate=pl.CostEstimate(flops=7 * 10**9, bytes_accessed=10**7, transcendentals=200000),
        name="routed_experts",
    )(tokens, expert_ids.reshape(1, n_tok), router_gate.reshape(1, n_tok), w_gate, w_up, w_down)


def solution(mesh):
    placed = (
        P("fsdp", None),
        P("fsdp", None),
        P("fsdp"),
        P(("fsdp", "ctx"), None),
        P(("fsdp", "ctx"), None),
        P(("fsdp", "ctx"), None),
    )
    return jax.shard_map(
        local, mesh=mesh, in_specs=placed, out_specs=P("fsdp", "ctx"), check_vma=False
    )
```
